32 devices in a mesh: batch: 8 (over z, core), seq: 4 (over y, x).
Axes of the slice: x: 2, y: 2, z: 4, core: 2. Of those that a mesh axis runs over, the one named last changes fastest.
Arguments:
- layer_input: bfloat16 [8, 2048, 2048], P('batch', 'seq'), may hold values from -6 to 6
- cotangent: bfloat16 [8, 2048, 2048], P('batch', 'seq'), may hold values from -6 to 6
- w_qkv: bfloat16 [2048, 6144], P(('batch', 'seq')), may hold values from -0.125 to 0.125
- bias_qkv: bfloat16 [3, 2048], P(None, ('batch', 'seq')), may hold values from -2 to 2
- w_out: bfloat16 [2048, 2048], P(('batch', 'seq')), may hold values from -0.125 to 0.125
- w_up: bfloat16 [2048, 8192], P(('batch', 'seq')), may hold values from -0.125 to 0.125
- w_down: bfloat16 [8192, 2048], P(('batch', 'seq')), may hold values from -0.0625 to 0.0625
- gains_d: bfloat16 [3, 2048], P(None, ('batch', 'seq')), may hold values from 0.25 to 1.75
- biases_d: bfloat16 [5, 2048], P(None, ('batch', 'seq')), may hold values from -2 to 2
- gain_ff: bfloat16 [8192], P(('batch', 'seq')), may hold values from 0.25 to 1.75
- biases_ff: bfloat16 [2, 8192], P(None, ('batch', 'seq')), may hold values from -2 to 2
- data_type: int32 [8], P('batch'), may hold values from 0 to 2
- doc_bounds: int32 [8, 3], P('batch'), may hold values from 1 to 2048, as said below
- span_starts: int32 [8, 4], P('batch'), may hold values from 0 to 1984, as said below
Outputs:
- layer_output: bfloat16 [8, 2048, 2048], P('batch', 'seq')
- grad_input: float32 [8, 2048, 2048], P('batch', 'seq')
- grad_w_qkv: float32 [2048, 6144], P(('batch', 'seq'))
- grad_bias_qkv: float32 [3, 2048], P(None, ('batch', 'seq'))
- grad_w_out: float32 [2048, 2048], P(('batch', 'seq'))
- grad_w_up: float32 [2048, 8192], P(('batch', 'seq'))
- grad_w_down: float32 [8192, 2048], P(('batch', 'seq'))
- grad_gains_d: float32 [3, 2048], P(None, ('batch', 'seq'))
- grad_biases_d: float32 [5, 2048], P(None, ('batch', 'seq'))
- grad_gain_ff: float32 [8192], P(('batch', 'seq'))
- grad_biases_ff: float32 [2, 8192], P(None, ('batch', 'seq'))
The draws below stay inside these ranges and needn't reach their ends.
Inputs may be any that keep to these rules, and one draw needn't show every extreme that they name: `doc_bounds`: in each pair of sequences 2b and 2b + 1 one has all its entries equal to 2048; the other's entries lie in 1 to 2047 in no particular order. `span_starts`: span j starts between j * 512 and (j + 1) * 512 - 64, so spans never intersect; in every draw some sequence's first span starts at 0 and some sequence's last span starts at 1984.
All inputs are finite; a program needn't handle non-finite values.
Results may differ from the reference program's by a relative error of at most 0.017.
Values may be sent and summed in bfloat16 or wider, within the bound.
No kernel may reach another device: no remote copies, remote signals or barrier semaphores. Data moves between devices by JAX's collectives and lax.ppermute only.
A program may use at most 512 MiB of HBM per device.

```python
import jax
import jax.numpy as jnp
from jax import lax

D = 2048
HEADS = 32
HEAD_DIM = 64
FF = 8192
SEQ_LEN = 2048
SPAN = 64
SPANS = 4
DOCS_CUT = 3
SEQS = 8


def draw_doc_bounds(key, part):
    picked = jax.random.randint(jax.random.fold_in(key, 11), (SEQS // 2,), 0, 2)
    raw_bounds = jax.random.randint(jax.random.fold_in(key, 12), (SEQS, DOCS_CUT), 1, SEQ_LEN)
    single = jnp.repeat(picked, 2) == jnp.arange(SEQS) % 2
    return jnp.where(single[:, None], SEQ_LEN, raw_bounds).astype(jnp.int32)


def draw_span_starts(key, part):
    slot_len = SEQ_LEN // SPANS
    offsets = jax.random.randint(jax.random.fold_in(key, 21), (SEQS, SPANS), 0, slot_len - SPAN + 1)
    low_row = jax.random.randint(jax.random.fold_in(key, 22), (), 0, SEQS)
    high_row = jax.random.randint(jax.random.fold_in(key, 23), (), 0, SEQS)
    rows = jnp.arange(SEQS)[:, None]
    cols = jnp.arange(SPANS)[None, :]
    offsets = jnp.where((rows == low_row) & (cols == 0), 0, offsets)
    offsets = jnp.where((rows == high_row) & (cols == SPANS - 1), slot_len - SPAN, offsets)
    return (offsets + cols * slot_len).astype(jnp.int32)


def with_ends(entries, stream_key, low, largest):
    longest = entries.shape.index(max(entries.shape))
    spots = []
    for shift in (0, 1):
        where = [jax.random.randint(jax.random.fold_in(stream_key, axis), (), 0, length) for axis, length in enumerate(entries.shape)]
        where[longest] = (where[longest] + shift) % entries.shape[longest]
        spots.append(tuple(where))
    return entries.at[spots[0]].set(low).at[spots[1]].set(largest)


def levels(stream_key, dims, cuts, least, largest):
    level, own = 1.0, jax.random.fold_in(stream_key, 6)
    for dim, blocks in cuts:
        steps = jnp.exp(jax.random.uniform(jax.random.fold_in(own, dim), (blocks,), jnp.float32, least / len(cuts), largest / len(cuts)))
        level = level * jnp.repeat(steps, dims[dim] // blocks).reshape([-1 if axis == dim else 1 for axis in range(len(dims))])
    return level


def scatter_about(key, dims, scale, most, shards=(), kind=jnp.bfloat16):
    array = scale * jax.random.normal(key, dims, jnp.float32)
    if shards:
        array = array * levels(key, dims, shards, -0.22, 0.18)
    return jnp.clip(array, -most, most).astype(kind)


def setup_inputs(seed: int = 0) -> dict:
    key_list = jax.random.split(jax.random.key(seed), 15)
    return {
        "layer_input": scatter_about(key_list[0], (SEQS, SEQ_LEN, D), 1.0, 6.0, ((0, 8), (1, 4))),
        "cotangent": scatter_about(key_list[1], (SEQS, SEQ_LEN, D), 1.0, 6.0, ((0, 8), (1, 4))),
        "w_qkv": scatter_about(key_list[2], (D, 3 * D), D ** -0.5, 0.125, ((0, 32),)),
        "bias_qkv": scatter_about(key_list[3], (3, D), 0.3, 2.0, ((1, 32),)),
        "w_out": scatter_about(key_list[4], (D, D), D ** -0.5, 0.125, ((0, 32),)),
        "w_up": scatter_about(key_list[5], (D, FF), D ** -0.5, 0.125, ((0, 32),)),
        "w_down": scatter_about(key_list[6], (FF, D), FF ** -0.5, 0.0625, ((0, 32),)),
        "gains_d": jnp.clip(1.0 + 0.15 * jax.random.normal(key_list[7], (3, D), jnp.float32), 0.25, 1.75).astype(jnp.bfloat16),
        "biases_d": scatter_about(key_list[8], (5, D), 0.3, 2.0, ((1, 32),)),
        "gain_ff": jnp.clip(1.0 + 0.15 * jax.random.normal(key_list[9], (FF,), jnp.float32), 0.25, 1.75).astype(jnp.bfloat16),
        "biases_ff": scatter_about(key_list[10], (2, FF), 0.3, 2.0, ((1, 32),)),
        "data_type": with_ends(jax.random.randint(key_list[11], (SEQS,), 0, 3), jax.random.fold_in(key_list[11], 1), 0, 2).astype(jnp.int32),
        "doc_bounds": draw_doc_bounds(jax.random.fold_in(key_list[14], 71), 0),
        "span_starts": draw_span_starts(jax.random.fold_in(key_list[14], 71), 0),
    }


NEG_FILL = -1e+30

@jax.custom_vjp
def low(v):
    return lax.optimization_barrier(v.astype(jnp.bfloat16)).astype(jnp.float32)

@jax.custom_vjp
def low_back(v):
    return v

def low_keep(v):
    return (low(v), None)

def low_pass(kept, grad):
    return (grad,)

def back_keep(v):
    return (v, None)

def back_low(kept, grad):
    return (low(grad),)
low.defvjp(low_keep, low_pass)
low_back.defvjp(back_keep, back_low)

def norm_rows(values, gain, shift):
    center = lax.optimization_barrier(jnp.mean(values, axis=-1, keepdims=True))
    spread = values - center
    inverse = lax.rsqrt(lax.optimization_barrier(jnp.mean(spread * spread, axis=-1, keepdims=True)) + 1e-05)
    return spread * inverse * gain + shift

def partner(values):
    is_even = jnp.arange(values.shape[-1]) % 2 == 0
    return jnp.where(is_even, -jnp.roll(values, -1, axis=-1), jnp.roll(values, 1, axis=-1))

def rot_tables():
    places = jnp.arange(SEQ_LEN).astype(jnp.float32)
    column = jnp.arange(D) % HEAD_DIM
    pair_idx = (column // 2).astype(jnp.float32)
    frequency = jnp.power(10000.0, -2.0 * pair_idx / HEAD_DIM)
    angles = places[:, None] * frequency[None, :]
    zeta_base = (2.0 * pair_idx + 0.4 * HEAD_DIM) / (1.4 * HEAD_DIM)
    exponent = (places - SEQ_LEN // 2) / 512.0
    scales = jnp.power(zeta_base[None, :], exponent[:, None])
    return (jnp.cos(angles), jnp.sin(angles), scales)

def turn(values, cosine, sine_vals, factor):
    return (values * cosine + partner(values) * sine_vals) * factor

def attention(query_rot, key_rot, value_low, seq_kind, bounds_row, spans_row):
    precise = lax.Precision.HIGHEST
    head_scale = HEAD_DIM ** (-0.5)
    places = jnp.arange(SEQ_LEN).astype(jnp.int32)
    doc_ids = lax.optimization_barrier(jnp.sum((bounds_row[None, :] <= places[:, None]).astype(jnp.int32), axis=1))
    in_span = ((spans_row[None, :] <= places[:, None]) & (places[:, None] < spans_row[None, :] + SPAN) & (seq_kind > 0)).astype(jnp.float32)
    keys_h = key_rot.reshape(SEQ_LEN, HEADS, HEAD_DIM)
    values_h = value_low.reshape(SEQ_LEN, HEADS, HEAD_DIM)
    block = min(512, SEQ_LEN)
    blocks = SEQ_LEN // block

    def one_block(element):
        query_blk, first_row = element
        query_pos = first_row + jnp.arange(block).astype(jnp.int32)
        query_doc = lax.dynamic_slice_in_dim(doc_ids, first_row, block, 0)
        query_span = lax.dynamic_slice_in_dim(in_span, first_row, block, 0)
        same_span = jnp.dot(query_span, in_span.T, precision=precise) > 0.5
        allowed = (query_doc[:, None] == doc_ids[None, :]) & ((places[None, :] <= query_pos[:, None]) | same_span)
        scores = low_back(jnp.einsum('qhd,khd->hqk', query_blk, keys_h, precision=precise) * head_scale)
        masked = jnp.where(allowed[None], scores, NEG_FILL)
        peak = lax.optimization_barrier(jnp.max(masked, axis=-1, keepdims=True))
        log_total = peak + jnp.log(lax.optimization_barrier(jnp.sum(jnp.exp(masked - peak), axis=-1, keepdims=True)))
        weights = low(jnp.exp(masked - log_total))
        return jnp.einsum('hqk,khd->qhd', weights, values_h, precision=precise)
    firsts = (jnp.arange(blocks) * block).astype(jnp.int32)
    pieces = lax.map(jax.checkpoint(one_block), (query_rot.reshape(blocks, block, HEADS, HEAD_DIM), firsts))
    return pieces.reshape(SEQ_LEN, D)

def layer(input_float, params, seq_kind, bounds_row, spans_row):
    precise = lax.Precision.HIGHEST
    w_qkv, bias_qkv, w_out, w_up, w_down, gains_d, biases_d, gain_ff, biases_ff = params
    normed_in = low(norm_rows(input_float, gains_d[0], biases_d[0]))
    qkv = low_back(jnp.dot(normed_in, w_qkv, precision=precise) + bias_qkv.reshape(3 * D))
    cosine, sine_vals, scales = rot_tables()
    query_rot = low(turn(qkv[:, :D], cosine, sine_vals, scales))
    key_rot = low(turn(qkv[:, D:2 * D], cosine, sine_vals, 1.0 / scales))
    value_low = low(qkv[:, 2 * D:])
    attn = low_back(attention(query_rot, key_rot, value_low, seq_kind, bounds_row, spans_row))
    branch_low = low(norm_rows(attn, gains_d[1], biases_d[1]))
    resid = input_float + low_back(jnp.dot(branch_low, w_out, precision=precise) + biases_d[3])
    mid_low = low(norm_rows(resid, gains_d[2], biases_d[2]))
    up_proj = low_back(jnp.dot(mid_low, w_up, precision=precise) + biases_ff[1])
    ffn_low = low(norm_rows(jax.nn.gelu(up_proj, approximate=True), gain_ff, biases_ff[0]))
    return resid + low_back(jnp.dot(ffn_low, w_down, precision=precise) + biases_d[4])

def reference(layer_input, cotangent, w_qkv, bias_qkv, w_out, w_up, w_down, gains_d, biases_d, gain_ff, biases_ff, data_type, doc_bounds, span_starts):
    params = tuple((p.astype(jnp.float32) for p in (w_qkv, bias_qkv, w_out, w_up, w_down, gains_d, biases_d, gain_ff, biases_ff)))

    def per_sequence(totals, element):
        input_rows, grad_given, seq_kind, bounds_row, spans_row = element

        def forward(input_value, param_value):
            return layer(input_value, param_value, seq_kind, bounds_row, spans_row)
        result, pullback = jax.vjp(forward, input_rows.astype(jnp.float32), params)
        grad_rows, grad_params = pullback(grad_given.astype(jnp.float32))
        totals = jax.tree.map(lambda first_v, second_v: first_v + second_v, totals, grad_params)
        return (totals, (result.astype(jnp.bfloat16), grad_rows))
    zeros_init = jax.tree.map(jnp.zeros_like, params)
    totals, (results, grad_rows) = lax.scan(per_sequence, zeros_init, (layer_input, cotangent, data_type, doc_bounds, span_starts))
    return (results, grad_rows, totals[0], totals[1], totals[2], totals[3], totals[4], totals[5], totals[6], totals[7], totals[8])
```

```python
import jax
import jax.numpy as jnp
from jax import lax
from jax.experimental import pallas as pl
from jax.experimental.pallas import tpu as pltpu
from jax.sharding import PartitionSpec as P

D = 2048
HEADS = 32
HEAD_DIM = 64
SEQ_LEN = 2048
SPAN = 64
BLK = 256
NEG_FILL = -1e30
NORM_EPS = 1e-05
EVERY = ("batch", "seq")


def nt(a, b):
    return lax.dot_general(a, b, (((1,), (1,)), ((), ())), preferred_element_type=jnp.float32)


def tn(a, b):
    return lax.dot_general(a, b, (((0,), (0,)), ((), ())), preferred_element_type=jnp.float32)


def nn(a, b):
    return jnp.dot(a, b, preferred_element_type=jnp.float32)


def launch(body, grid, ins, outs, scratch=(), prefetch=(), after=(), name=None, flops=0, moved=0):
    n_pre, n_in, n_after = len(prefetch), len(ins), len(after)

    def kernel(*refs):
        body(*refs[: n_pre + n_in], *refs[n_pre + n_in + n_after :])

    return pl.pallas_call(
        kernel,
        out_shape=tuple(jax.ShapeDtypeStruct(s, d) for s, d, _ in outs),
        grid_spec=pltpu.PrefetchScalarGridSpec(
            num_scalar_prefetch=n_pre,
            grid=grid,
            in_specs=[b for _, b in ins] + [pl.BlockSpec(memory_space=pl.ANY)] * n_after,
            out_specs=[b for _, _, b in outs],
            scratch_shapes=list(scratch),
        ),
        compiler_params=pltpu.CompilerParams(vmem_limit_bytes=58 << 20),
        cost_estimate=pl.CostEstimate(flops=flops, bytes_accessed=moved, transcendentals=0),
        name=name,
    )(*prefetch, *(a for a, _ in ins), *after)


def tile(rows, cols):
    return pl.BlockSpec((rows, cols), lambda i, *_: (i, 0))


def fixed(array):
    zeros = (0,) * array.ndim
    return (array, pl.BlockSpec(array.shape, lambda *_: zeros, pipeline_mode=pl.Buffered(1)))


def columns(lines):
    count, width = len(lines), lines[0].shape[1]
    pad = [jnp.zeros((8 - count, width), jnp.float32)] if count < 8 else []
    flat = jnp.concatenate(list(lines) + pad, axis=0).T
    return [flat[:, i : i + 1] for i in range(count)]


def joined(centers, squares, width):
    count = len(centers)
    center = sum(centers) * (1.0 / count)
    total = sum(squares) + width * sum((c - center) ** 2 for c in centers)
    return center, lax.rsqrt(total * (1.0 / (width * count)) + NORM_EPS)


def rotate(value, tables, sign):
    straight, from_right, from_left = tables
    turned = pltpu.roll(value, 127, 1) * from_right + pltpu.roll(value, 1, 1) * from_left
    return value * straight + turned if sign > 0 else value * straight - turned


def qkv_project(low, weight, bias, tables):
    rows, width = low.shape
    cols = weight.shape[1] // 3

    def body(low_ref, w_ref, b_ref, *rest):
        table_refs, outs = rest[:6], rest[6:]
        for part in range(3):
            span = slice(part * cols, (part + 1) * cols)
            value = nn(low_ref[...], w_ref[:, span]) + b_ref[:, span]
            if part == 2:
                outs[2][...] = value.astype(jnp.bfloat16)
                continue
            own = [t[...] for t in table_refs[3 * part : 3 * part + 3]]
            for at in range(0, cols, 128):
                outs[part][:, at : at + 128] = rotate(value[:, at : at + 128], own, 1).astype(jnp.bfloat16)

    return launch(
        body,
        (rows // BLK,),
        [(low, tile(BLK, width)), fixed(weight), fixed(bias)] + [(t, tile(BLK, 128)) for t in tables],
        [((rows, cols), jnp.bfloat16, tile(BLK, cols))] * 3,
        name="qkv_project",
        flops=2 * rows * width * 3 * cols,
        moved=rows * width * 4,
    )


def attention_fwd(q, k, v, lo, hi, slots, first, last):
    rows, width = q.shape
    blocks = rows // BLK
    heads = width // HEAD_DIM
    extra = 16

    def body(slots, first, last, q_ref, k_ref, v_ref, lo_ref, hi_ref, o_ref, lse_ref, stat_ref, vt, acc, qt, kept):
        step = pl.program_id(0)

        @pl.when(step == 0)
        def _():
            for i in range(blocks):
                at = slice(i * BLK, (i + 1) * BLK)
                flat = v_ref[at, :].T
                for h in range(heads):
                    vt[h, :HEAD_DIM, at] = flat[h * HEAD_DIM : (h + 1) * HEAD_DIM]
                    vt[h, HEAD_DIM:, at] = jnp.ones((extra, BLK), jnp.bfloat16)

        flat = (q_ref[...] * jnp.bfloat16(HEAD_DIM**-0.5)).T
        zero = jnp.zeros((HEAD_DIM, BLK), jnp.bfloat16)
        for h in range(heads):
            mine = flat[h * HEAD_DIM : (h + 1) * HEAD_DIM, :]
            qt[h] = jnp.concatenate([mine, zero] if h % 2 == 0 else [zero, mine], axis=0)
        low, high = lo_ref[...], hi_ref[...]
        key_row = lax.broadcasted_iota(jnp.int32, (BLK, BLK), 0)

        def scores(kb, peaks):
            at = pl.ds(pl.multiple_of(slots[kb] * BLK, BLK), BLK)
            spot = key_row + kb * BLK
            seen = (spot >= low) & (spot <= high)
            out = []
            for h in range(heads):
                two = slice(h // 2 * 128, h // 2 * 128 + 128)
                s = jnp.where(seen, nn(k_ref[at, two], qt[h]), NEG_FILL)
                kept[kb, h] = s
                out.append(jnp.maximum(peaks[h], jnp.max(s, axis=0, keepdims=True)))
            return tuple(out)

        start = tuple(jnp.full((1, BLK), NEG_FILL, jnp.float32) for _ in range(heads))
        peaks = lax.fori_loop(first[step], last[step], scores, start)
        acc[...] = jnp.zeros_like(acc)

        def weigh(kb, _):
            at = pl.ds(pl.multiple_of(slots[kb] * BLK, BLK), BLK)
            for h in range(heads):
                p = jnp.exp(kept[kb, h] - peaks[h]).astype(jnp.bfloat16)
                acc[h] += nn(vt[h, :, at], p)
            return 0

        lax.fori_loop(first[step], last[step], weigh, 0)
        parts = []
        for h in range(heads):
            total = acc[h, HEAD_DIM : HEAD_DIM + 1, :]
            lse_ref[h : h + 1, :] = peaks[h] + jnp.log(total)
            parts.append(acc[h, :HEAD_DIM] / total)
        flat = jnp.concatenate(parts, axis=0)
        center = jnp.mean(flat, axis=0, keepdims=True)
        stat_ref[0:1, :] = center
        stat_ref[1:2, :] = jnp.sum((flat - center) ** 2, axis=0, keepdims=True)
        stat_ref[2:8, :] = jnp.zeros((6, BLK), jnp.float32)
        o_ref[...] = flat.T

    by_slot = pl.BlockSpec((BLK, width), lambda i, s, *_: (s[i], 0))
    line = pl.BlockSpec((1, BLK), lambda i, *_: (0, i))
    return launch(
        body,
        (blocks,),
        [(q, by_slot), fixed(k), fixed(v), (lo, line), (hi, line)],
        [
            ((rows, width), jnp.float32, by_slot),
            ((heads, rows), jnp.float32, pl.BlockSpec((heads, BLK), lambda i, s, *_: (0, s[i]))),
            ((8, rows), jnp.float32, pl.BlockSpec((8, BLK), lambda i, s, *_: (0, s[i]))),
        ],
        scratch=[
            pltpu.VMEM((heads, HEAD_DIM + extra, rows), jnp.bfloat16),
            pltpu.VMEM((heads, HEAD_DIM + extra, BLK), jnp.float32),
            pltpu.VMEM((heads, 128, BLK), jnp.bfloat16),
            pltpu.VMEM((blocks, heads, BLK, BLK), jnp.float32),
        ],
        prefetch=(slots, first, last),
        name="attention_forward",
        flops=4 * rows * rows * width,
        moved=rows * width * 12,
    )


def out_project(attn, stats, gain, shift, weight):
    rows, width = attn.shape
    wide = weight.shape[1]

    def body(a_ref, g_ref, s_ref, w_ref, *rest):
        stat_refs, (low_ref, part_ref) = rest[: len(stats)], rest[len(stats) :]
        center, inverse = columns(joined([r[0:1] for r in stat_refs], [r[1:2] for r in stat_refs], width))
        low = ((a_ref[...] - center) * inverse * g_ref[...] + s_ref[...]).astype(jnp.bfloat16)
        low_ref[...] = low
        part_ref[...] = nn(low, w_ref[...]).astype(jnp.bfloat16)

    return launch(
        body,
        (rows // BLK,),
        [(attn, tile(BLK, width)), fixed(gain), fixed(shift), fixed(weight)] + list(stats),
        [((rows, width), jnp.bfloat16, tile(BLK, width)), ((rows, wide), jnp.bfloat16, tile(BLK, wide))],
        name="out_project",
        flops=2 * rows * width * wide,
        moved=rows * (width * 6 + wide * 2),
    )


def own_rows(body, wholes, rows_in, terms, outs, sums=0, after=(), name=None):
    two, half, wide = rows_in[0].shape
    piece = min(128, half)
    count = len(terms[0])

    def kernel(*refs):
        whole_refs, refs = refs[: len(wholes)], refs[len(wholes) :]
        row_refs, refs = refs[: len(rows_in)], refs[len(rows_in) :]
        term_refs, out_refs = refs[: 2 * count], refs[2 * count :]
        vectors = [r[...] for r in whole_refs]
        added = [0.0] * sums
        for side in range(2):
            total = term_refs[side * count][...].astype(jnp.float32)
            for r in term_refs[side * count + 1 : (side + 1) * count]:
                total = total + r[...].astype(jnp.float32)
            values = body(vectors, [r[side] for r in row_refs], total)
            for ref, value in zip(out_refs, values[: len(outs)]):
                ref[side] = value.astype(ref.dtype)
            added = [a + jnp.sum(v, axis=0, keepdims=True) for a, v in zip(added, values[len(outs) :])]
        if sums:
            sum_ref = out_refs[len(outs)]

            @pl.when(pl.program_id(0) == 0)
            def _():
                sum_ref[...] = jnp.zeros_like(sum_ref)

            for i, a in enumerate(added):
                sum_ref[i : i + 1, :] += a

    own = pl.BlockSpec((2, piece, wide), lambda i: (0, i, 0))
    pieces = []
    for side in range(2):
        for array, start in terms[side]:
            pieces.append((array, pl.BlockSpec((piece, wide), lambda i, at=start // piece: (at + i, 0))))
    results = [((2, half, wide), d, own) for d in outs]
    if sums:
        results.append(((8, wide), jnp.float32, pl.BlockSpec((8, wide), lambda i: (0, 0))))
    return launch(
        kernel,
        (half // piece,),
        [fixed(w) for w in wholes] + [(r, own) for r in rows_in] + pieces,
        results,
        after=after,
        name=name,
        flops=40 * half * wide,
        moved=half * wide * 16,
    )


def norm_parts(values):
    center = jnp.mean(values, axis=-1, keepdims=True)
    spread = values - center
    inverse = lax.rsqrt(jnp.mean(spread * spread, axis=-1, keepdims=True) + NORM_EPS)
    return spread * inverse, inverse


def norm_lower(normed, inverse, gain, upper):
    scaled = upper * gain
    first_mean = jnp.mean(scaled, axis=-1, keepdims=True)
    second_mean = jnp.mean(scaled * normed, axis=-1, keepdims=True)
    return inverse * (scaled - first_mean - normed * second_mean)


GELU_A = 0.044715
GELU_C = 0.7978845608028654


def ffn_up(mid, cot, w_up, w_down, bias, gain, after=()):
    rows, wide = mid.shape
    units = w_up.shape[1]
    chunk = min(512, units)

    def body(m_ref, c_ref, u_w, d_w, b_ref, g_ref, up_ref, grad_ref, stat_ref, gel_ref):
        total = scaled_total = 0.0
        for at in range(0, units, chunk):
            span = slice(at, at + chunk)
            up = nn(m_ref[...], u_w[:, span]) + b_ref[:, span]
            grad = nt(c_ref[...], d_w[span, :])
            up_ref[:, span] = up
            grad_ref[:, span] = grad
            gel = 0.5 * up * (1.0 + jnp.tanh(GELU_C * (up + GELU_A * up * up * up)))
            gel_ref[:, span] = gel
            total = total + jnp.sum(gel, axis=1, keepdims=True)
            scaled_total = scaled_total + jnp.sum(grad * g_ref[:, span], axis=1, keepdims=True)
        center = total * (1.0 / units)
        square = product = 0.0
        for at in range(0, units, chunk):
            span = slice(at, at + chunk)
            spread = gel_ref[:, span] - center
            square = square + jnp.sum(spread * spread, axis=1, keepdims=True)
            product = product + jnp.sum(grad_ref[:, span] * g_ref[:, span] * spread, axis=1, keepdims=True)
        lane = lax.broadcasted_iota(jnp.int32, (BLK, 128), 1)
        flat = jnp.zeros((BLK, 128), jnp.float32)
        for i, value in enumerate((center, square, scaled_total, product)):
            flat = jnp.where(lane == i, value, flat)
        stat_ref[...] = flat.T[0:8, :]

    return launch(
        body,
        (rows // BLK,),
        [(mid, tile(BLK, wide)), (cot, tile(BLK, wide)), fixed(w_up), fixed(w_down), fixed(bias), fixed(gain)],
        [
            ((rows, units), jnp.float32, tile(BLK, units)),
            ((rows, units), jnp.float32, tile(BLK, units)),
            ((8, rows), jnp.float32, pl.BlockSpec((8, BLK), lambda i, *_: (0, i))),
        ],
        scratch=[pltpu.VMEM((BLK, units), jnp.float32)],
        after=after,
        name="ffn_up",
        flops=4 * rows * wide * units,
        moved=rows * (wide * 4 + units * 8),
    )


def ffn_mid(up, grad, stats, gain, shift, w_up):
    rows, units = up.shape
    wide = w_up.shape[0]
    chunk = min(512, units)
    ranks = len(stats)

    def body(u_ref, f_ref, g_ref, s_ref, w_ref, *rest):
        stat_refs, (low_ref, gup_ref, part_ref, sum_ref) = rest[:ranks], rest[ranks:]
        centers = [r[0:1] for r in stat_refs]
        center, inverse = joined(centers, [r[1:2] for r in stat_refs], units)
        share = 1.0 / (units * ranks)
        first = sum(r[2:3] for r in stat_refs) * share
        second = inverse * share * sum(r[3:4] + (c - center) * r[2:3] for r, c in zip(stat_refs, centers))
        center, inverse, first, second = columns([center, inverse, first, second])

        @pl.when(pl.program_id(0) == 0)
        def _():
            sum_ref[...] = jnp.zeros_like(sum_ref)

        for at in range(0, units, chunk):
            span = slice(at, at + chunk)
            u, f = u_ref[:, span], f_ref[:, span]
            squared = u * u
            t = jnp.tanh(GELU_C * u * (1.0 + GELU_A * squared))
            one = 0.5 * (1.0 + t)
            slope = one + 0.5 * u * (1.0 - t * t) * (GELU_C * (1.0 + 3.0 * GELU_A * squared))
            normed = (u * one - center) * inverse
            low_ref[:, span] = (normed * g_ref[:, span] + s_ref[:, span]).astype(jnp.bfloat16)
            lower = inverse * (f * g_ref[:, span] - first - normed * second)
            gup = (lower * slope).astype(jnp.bfloat16)
            gup_ref[:, span] = gup
            sum_ref[0:1, span] += jnp.sum(f * normed, axis=0, keepdims=True)
            sum_ref[1:2, span] += jnp.sum(f, axis=0, keepdims=True)
            sum_ref[2:3, span] += jnp.sum(gup.astype(jnp.float32), axis=0, keepdims=True)
        part_ref[...] = nt(gup_ref[...], w_ref[...]).astype(jnp.bfloat16)

    return launch(
        body,
        (rows // BLK,),
        [(up, tile(BLK, units)), (grad, tile(BLK, units)), fixed(gain), fixed(shift), fixed(w_up)] + list(stats),
        [
            ((rows, units), jnp.bfloat16, tile(BLK, units)),
            ((rows, units), jnp.bfloat16, tile(BLK, units)),
            ((rows, wide), jnp.bfloat16, tile(BLK, wide)),
            ((8, units), jnp.float32, pl.BlockSpec((8, units), lambda i, *_: (0, 0))),
        ],
        name="ffn_mid",
        flops=2 * rows * wide * units,
        moved=rows * (wide * 2 + units * 12),
    )


def branch_back(resid, w_out, attn, stats, gain, after=()):
    rows, wide = resid.shape
    width = attn.shape[1]
    ranks = len(stats)

    def body(r_ref, w_ref, a_ref, g_ref, *rest):
        stat_refs, (grad_ref, stat_ref, sum_ref) = rest[:ranks], rest[ranks:]
        center, inverse = columns(joined([r[0:1] for r in stat_refs], [r[1:2] for r in stat_refs], width))

        @pl.when(pl.program_id(0) == 0)
        def _():
            sum_ref[...] = jnp.zeros_like(sum_ref)

        grad = nt(r_ref[...], w_ref[...])
        grad_ref[...] = grad
        normed = (a_ref[...] - center) * inverse
        scaled = grad * g_ref[...]
        sum_ref[0:1, :] += jnp.sum(grad * normed, axis=0, keepdims=True)
        sum_ref[1:2, :] += jnp.sum(grad, axis=0, keepdims=True)
        lane = lax.broadcasted_iota(jnp.int32, (BLK, 128), 1)
        flat = jnp.where(lane == 0, jnp.sum(scaled, axis=1, keepdims=True), 0.0)
        flat = jnp.where(lane == 1, jnp.sum(scaled * normed, axis=1, keepdims=True), flat)
        stat_ref[...] = flat.T[0:8, :]

    return launch(
        body,
        (rows // BLK,),
        [(resid, tile(BLK, wide)), fixed(w_out), (attn, tile(BLK, width)), fixed(gain)] + list(stats),
        [
            ((rows, width), jnp.float32, tile(BLK, width)),
            ((8, rows), jnp.float32, pl.BlockSpec((8, BLK), lambda i, *_: (0, i))),
            ((8, width), jnp.float32, pl.BlockSpec((8, width), lambda i, *_: (0, 0))),
        ],
        after=after,
        name="branch_back",
        flops=2 * rows * wide * width,
        moved=rows * (wide * 2 + width * 8),
    )


def attn_grad(grad, attn, stats, sums, gain, after=()):
    rows, width = attn.shape
    ranks = len(stats)
    heads = width // HEAD_DIM

    def body(f_ref, a_ref, g_ref, *rest):
        stat_refs, sum_refs = rest[:ranks], rest[ranks : 2 * ranks]
        out_ref, dot_ref = rest[2 * ranks :]
        center, inverse = joined([r[0:1] for r in stat_refs], [r[1:2] for r in stat_refs], width)
        share = 1.0 / (width * ranks)
        first = sum(r[0:1] for r in sum_refs) * share
        second = sum(r[1:2] for r in sum_refs) * share
        center, inverse, first, second = columns([center, inverse, first, second])
        attn_here = a_ref[...]
        normed = (attn_here - center) * inverse
        out = (inverse * (f_ref[...] * g_ref[...] - first - normed * second)).astype(jnp.bfloat16)
        out_ref[...] = out
        product = (out.astype(jnp.float32) * attn_here).T
        for h in range(heads):
            dot_ref[h : h + 1, :] = jnp.sum(product[h * HEAD_DIM : (h + 1) * HEAD_DIM], axis=0, keepdims=True)

    return launch(
        body,
        (rows // BLK,),
        [(grad, tile(BLK, width)), (attn, tile(BLK, width)), fixed(gain)] + list(stats) + list(sums),
        [
            ((rows, width), jnp.bfloat16, tile(BLK, width)),
            ((heads, rows), jnp.float32, pl.BlockSpec((heads, BLK), lambda i, *_: (0, i))),
        ],
        after=after,
        name="attn_grad",
        flops=20 * rows * width,
        moved=rows * width * 10,
    )


def attention_bwd(q, k, v, g, lse, dot, lo, hi, tables, slots, first, last, after=()):
    rows, width = q.shape
    blocks = rows // BLK
    heads = width // HEAD_DIM
    scale = HEAD_DIM**-0.5

    def body(slots, first, last, q_ref, k_ref, v_ref, g_ref, lse_ref, dot_ref, lo_ref, hi_ref, *rest):
        table_refs, (out_ref, dqt, qt, gt, accs) = rest[:6], rest[6:]
        key_row = lax.broadcasted_iota(jnp.int32, (BLK, BLK), 0)
        lane = lax.broadcasted_iota(jnp.int32, (BLK, 128), 1)
        zero = jnp.zeros((), jnp.bfloat16)
        dqt[...] = jnp.zeros_like(dqt)
        for i in range(blocks):
            at = slice(i * BLK, (i + 1) * BLK)
            qt[:, at] = q_ref[at, :].T
            gt[:, at] = g_ref[at, :].T

        def outer(kb, _):
            rows_k = pl.ds(pl.multiple_of(slots[kb] * BLK, BLK), BLK)
            k, v = k_ref[rows_k, :] * jnp.bfloat16(scale), v_ref[rows_k, :]
            kts = k.T
            spot = key_row + kb * BLK

            def halves(x, h):
                x = x[:, h // 2 * 128 : h // 2 * 128 + 128]
                return jnp.where((lane < HEAD_DIM) == (h % 2 == 0), x, zero)

            ks = [halves(k, h) for h in range(heads)]
            vs = [halves(v, h) for h in range(heads)]
            accs[...] = jnp.zeros_like(accs)

            def inner(qb, _):
                at = pl.ds(pl.multiple_of(slots[qb] * BLK, BLK), BLK)
                here = pl.ds(pl.multiple_of(qb * BLK, BLK), BLK)
                seen = (spot >= lo_ref[0:1, here]) & (spot <= hi_ref[0:1, here])
                for h in range(heads):
                    two = slice(h // 2 * 128, h // 2 * 128 + 128)
                    span = slice(h * HEAD_DIM, (h + 1) * HEAD_DIM)
                    s = nn(ks[h], qt[two, at])
                    p = jnp.where(seen, jnp.exp(s - lse_ref[h : h + 1, at]), 0.0)
                    dp = nn(vs[h], gt[two, at])
                    ds = (p * (dp - dot_ref[h : h + 1, at])).astype(jnp.bfloat16)
                    accs[1, h] += nn(p.astype(jnp.bfloat16), g_ref[at, two])
                    accs[0, h] += nn(ds, q_ref[at, two])
                    dqt[span, at] += nn(kts[span, :], ds)
                return 0

            lax.fori_loop(first[kb], last[kb], inner, 0)
            own = [t[rows_k, :] for t in table_refs[3:]]
            for h in range(0, heads, 2):
                at = h * HEAD_DIM
                grad_k = jnp.where(lane < HEAD_DIM, accs[0, h], accs[0, h + 1]) * scale
                grad_v = jnp.where(lane < HEAD_DIM, accs[1, h], accs[1, h + 1])
                out_ref[rows_k, width + at : width + at + 128] = rotate(grad_k, own, -1).astype(jnp.bfloat16)
                out_ref[rows_k, 2 * width + at : 2 * width + at + 128] = grad_v.astype(jnp.bfloat16)
            return 0

        lax.fori_loop(0, blocks, outer, 0)
        for i in range(blocks):
            at = slice(i * BLK, (i + 1) * BLK)
            grad_q = dqt[:, at].T
            own = [t[at, :] for t in table_refs[:3]]
            for col in range(0, width, 128):
                out_ref[at, col : col + 128] = rotate(grad_q[:, col : col + 128], own, -1).astype(jnp.bfloat16)

    return launch(
        body,
        (1,),
        [fixed(a) for a in (q, k, v, g, lse, dot, lo, hi, *tables)],
        [((rows, 3 * width), jnp.bfloat16, pl.BlockSpec((rows, 3 * width), lambda *_: (0, 0), pipeline_mode=pl.Buffered(1)))],
        scratch=[
            pltpu.VMEM((width, rows), jnp.float32),
            pltpu.VMEM((width, rows), jnp.bfloat16),
            pltpu.VMEM((width, rows), jnp.bfloat16),
            pltpu.VMEM((2, heads, BLK, 128), jnp.float32),
        ],
        prefetch=(slots, first, last),
        after=after,
        name="attention_backward",
        flops=10 * rows * rows * width,
        moved=rows * width * 14,
    )[0]


def input_back(grad, weight, x, after=()):
    rows, cols = grad.shape
    wide = weight.shape[0]

    def body(g_ref, w_ref, x_ref, part_ref, bias_ref, sum_ref):
        @pl.when(pl.program_id(0) == 0)
        def _():
            sum_ref[...] = jnp.zeros_like(sum_ref)
            bias_ref[...] = jnp.zeros_like(bias_ref)

        part = nt(g_ref[...], w_ref[...])
        part_ref[...] = part.astype(jnp.bfloat16)
        bias_ref[0:1, :] += jnp.sum(g_ref[...].astype(jnp.float32), axis=0, keepdims=True)
        normed, _ = norm_parts(x_ref[...].astype(jnp.float32))
        sum_ref[0:1, :] += jnp.sum(part * normed, axis=0, keepdims=True)
        sum_ref[1:2, :] += jnp.sum(part, axis=0, keepdims=True)

    return launch(
        body,
        (rows // BLK,),
        [(grad, tile(BLK, cols)), fixed(weight), (x, tile(BLK, wide))],
        [
            ((rows, wide), jnp.bfloat16, tile(BLK, wide)),
            ((8, cols), jnp.float32, pl.BlockSpec((8, cols), lambda i, *_: (0, 0))),
            ((8, wide), jnp.float32, pl.BlockSpec((8, wide), lambda i, *_: (0, 0))),
        ],
        after=after,
        name="input_back",
        flops=2 * rows * cols * wide,
        moved=rows * (wide * 4 + cols * 2),
    )


def key_limits(bounds, spans, kind, total):
    places = jnp.arange(total, dtype=jnp.int32)
    below = bounds[:, None] <= places[None, :]
    doc_first = jnp.max(jnp.where(below, bounds[:, None], 0), axis=0)
    doc_last = jnp.min(jnp.where(below, total, bounds[:, None]), axis=0) - 1
    doc_last = jnp.minimum(doc_last, total - 1)
    inside = (spans[:, None] <= places[None, :]) & (places[None, :] < spans[:, None] + SPAN) & (kind > 0)
    span_last = jnp.max(jnp.where(inside, spans[:, None] + SPAN - 1, 0), axis=0)
    span_first = jnp.min(jnp.where(inside, spans[:, None], total), axis=0)
    hi = jnp.minimum(jnp.maximum(places, span_last), doc_last)
    q_first = jnp.maximum(jnp.minimum(places, span_first), doc_first)
    return doc_first, hi, q_first, doc_last


def block_limits(lo, hi, qf, ql):
    low = lo.reshape(-1, BLK)[:, 0] // BLK
    high = hi.reshape(-1, BLK)[:, -1] // BLK + 1
    qlow = qf.reshape(-1, BLK)[:, 0] // BLK
    qhigh = ql.reshape(-1, BLK)[:, -1] // BLK + 1
    return low, high, qlow, qhigh


class Exchange:
    def __init__(self, ranks, batches, rows, me):
        self.ranks, self.batches, self.rows, self.me = ranks, batches, rows, me
        self.square = ranks == 4 and rows == 2 * BLK
        self.half = rows // 2
        self.order = ((0, 1, 2, 3), (0, 2, 1, 3))
        total = ranks * rows
        block = jnp.arange(total // BLK, dtype=jnp.int32)
        if self.square:
            owner, part = block // 2, block % 2
            near = owner ^ me
            swapped = (near >> 1) | ((near & 1) << 1)
            self.slots = (part * 4 + jnp.where(part == 0, near, swapped)).astype(jnp.int32)
            owners = jnp.stack([me ^ r for half in self.order for r in half])
            firsts = owners * rows + jnp.repeat(jnp.arange(2), 4) * self.half
            self.places = (firsts[:, None] + jnp.arange(self.half)[None, :]).reshape(total).astype(jnp.int32)
        else:
            self.slots = block
            self.places = jnp.arange(total, dtype=jnp.int32)

    def swap(self, value, bit):
        return lax.ppermute(value, "seq", [(r, r ^ bit) for r in range(self.ranks)])

    def gather(self, upper, lower):
        if not self.square:
            return lax.all_gather(jnp.concatenate([upper, lower], axis=0), "seq", axis=0, tiled=True)
        upper = jnp.concatenate([upper, self.swap(upper, 1)], axis=0)
        lower = jnp.concatenate([lower, self.swap(lower, 2)], axis=0)
        return jnp.concatenate([upper, self.swap(upper, 2), lower, self.swap(lower, 1)], axis=0)

    def scatter(self, low):
        n = self.half
        if not self.square:
            own = lax.psum_scatter(low, "seq", scatter_dimension=0, tiled=True)
            return [[(own, 0)], [(own, n)]]
        out = []
        for at, bits in ((0, (2, 1)), (4 * n, (1, 2))):
            near = self.swap(low[at + 2 * n : at + 4 * n], bits[0])
            far = low[at + n : at + 2 * n].astype(jnp.float32) + near[n:].astype(jnp.float32)
            far = self.swap(far.astype(jnp.bfloat16), bits[1])
            out.append([(low, at), (near, 0), (far, 0)])
        return out

    def spread(self, value):
        lines = value.shape[0]
        if not self.square:
            every = lax.all_gather(value, "seq", axis=0)
            return [(every[r], pl.BlockSpec((lines, BLK), lambda i, *_: (0, i))) for r in range(self.ranks)]
        out = [(value, pl.BlockSpec((lines, BLK), lambda i, *_: (0, i)))]
        for bit, other in ((1, 2), (2, 1), (3, 3)):
            spec = pl.BlockSpec(
                (lines, BLK), lambda i, *_, a=bit, b=other: (0, (i // 4) * 4 + ((i % 4) ^ (a + (i // 4) * (b - a))))
            )
            out.append((self.swap(value, bit), spec))
        return out


def flipped(value, batch, me, bits):
    device = batch * 4 + me
    shape = value.shape
    for bit in range(bits):
        two = value.reshape((-1, 2, 1 << bit) + shape[1:])
        value = jnp.where((device >> bit) & 1, two[:, ::-1], two).reshape(shape)
    return value


def share_small(value, batches, ranks):
    if (batches, ranks) != (8, 4):
        return lax.all_gather(value, EVERY, axis=0)
    batch, me = lax.axis_index("batch"), lax.axis_index("seq")
    parts = value[None]
    for axis, count, steps in (("seq", ranks, (1, 2, 3)), ("batch", batches, (1,)), ("batch", batches, (2, 4, 6))):
        parts = jnp.concatenate(
            [parts] + [lax.ppermute(parts, axis, [(r, r ^ s) for r in range(count)]) for s in steps], axis=0
        )
    return flipped(parts, batch, me, 5)


def sum_small(value, batches, ranks):
    if (batches, ranks) != (8, 4):
        return lax.psum_scatter(value, EVERY, scatter_dimension=0, tiled=True)[0]
    batch, me = lax.axis_index("batch"), lax.axis_index("seq")
    value = flipped(value, batch, me, 5)
    for axis, count, steps, left in (("batch", batches, (2, 4, 6), 8), ("batch", batches, (1,), 4), ("seq", ranks, (1, 2, 3), 1)):
        total = value[:left]
        for i, s in enumerate(steps):
            at = (i + 1) * left
            total = total + lax.ppermute(value[at : at + left], axis, [(r, r ^ s) for r in range(count)])
        value = total
    return value[0]


def rot_tables(places):
    column = jnp.arange(128) % HEAD_DIM
    pair_idx = (column // 2).astype(jnp.float32)
    frequency = jnp.power(10000.0, -2.0 * pair_idx / HEAD_DIM)
    place_float = places.astype(jnp.float32)
    angles = place_float[:, None] * frequency[None, :]
    zeta_base = (2.0 * pair_idx + 0.4 * HEAD_DIM) / (1.4 * HEAD_DIM)
    exponent = (place_float - SEQ_LEN // 2) / 512.0
    scales = jnp.power(zeta_base[None, :], exponent[:, None])
    cosine, sine = jnp.cos(angles), jnp.sin(angles)
    even = (column % 2 == 0)[None, :]
    right, left = jnp.where(even, -sine, 0.0), jnp.where(even, 0.0, sine)
    return tuple(t * s for s in (scales, 1.0 / scales) for t in (cosine, right, left))


def local(
    layer_input,
    cotangent,
    w_qkv,
    bias_qkv,
    w_out,
    w_up,
    w_down,
    gains_d,
    biases_d,
    gain_ff,
    biases_ff,
    data_type,
    doc_bounds,
    span_starts,
    *,
    batches,
    ranks,
):
    me = lax.axis_index("seq")
    rows = layer_input.shape[1]
    half = rows // 2
    move = Exchange(ranks, batches, rows, me)
    tokens = rows * ranks
    cols = D // ranks
    strip, d_rows = w_down.shape[0], w_up.shape[0]
    units = strip * batches
    f32, bf16 = jnp.float32, jnp.bfloat16
    x_own, cot_own = layer_input.reshape(2, half, D), cotangent.reshape(2, half, D)

    part_qkv = lax.all_to_all(w_qkv.reshape(d_rows, 3, ranks, cols), "seq", 2, 0).reshape(d_rows * ranks, 3 * cols)
    full_qkv = lax.all_gather(part_qkv, "batch", axis=0, tiled=True)
    x_full = move.gather(x_own[0], x_own[1])
    small = jnp.concatenate(
        [bias_qkv.reshape(-1), gains_d.reshape(-1), biases_d.reshape(-1), gain_ff, biases_ff.reshape(-1)]
    )
    small = share_small(small, batches, ranks)
    cut = 11 * d_rows
    rows_d = small[:, :cut].reshape(-1, 11, d_rows).swapaxes(0, 1).reshape(11, D).astype(f32)
    rows_f = small[:, cut:].reshape(batches, ranks, 3, strip)
    rows_f = lax.dynamic_index_in_dim(rows_f, me, 1, False).swapaxes(0, 1).reshape(3, units).astype(f32)
    qkv_shift = lax.dynamic_slice_in_dim(rows_d[:3], me * cols, cols, 1).reshape(1, 3 * cols)
    branch = lax.dynamic_slice_in_dim(rows_d[3:], me * cols, cols, 1)
    gain_in, gain_mid = rows_d[3:4], rows_d[5:6]
    shift_in, shift_mid, shift_out, shift_down = rows_d[6:7], rows_d[8:9], rows_d[9:10], rows_d[10:11]
    gain_branch, shift_branch = branch[1:2], branch[4:5]
    gain_ffn, shift_ffn, shift_up = rows_f[0:1], rows_f[1:2], rows_f[2:3]

    order = [(i, (i % batches) * ranks + i // batches) for i in range(batches * ranks)]
    part_out = lax.ppermute(w_out, EVERY, order)
    full_out = lax.all_gather(part_out, "batch", axis=0, tiled=True)
    part_up = lax.all_to_all(w_up.reshape(d_rows, batches, ranks, strip), "seq", 2, 0).reshape(d_rows * ranks, units)
    full_down = lax.all_gather(w_down, "batch", axis=0, tiled=True)
    full_up = lax.all_gather(part_up, "batch", axis=0, tiled=True)
    cot_full = move.gather(cot_own[0], cot_own[1])

    normed_all, _ = norm_parts(x_full.astype(f32))
    input_low = (normed_all * gain_in + shift_in).astype(bf16)
    tables = rot_tables(move.places)
    query_rot, key_rot, value_low = qkv_project(input_low, full_qkv, qkv_shift, tables)
    lo, hi, q_lo, q_hi = key_limits(doc_bounds[0], span_starts[0], data_type[0], tokens)
    k_first, k_last, q_first, q_last = block_limits(lo, hi, q_lo, q_hi)
    lo, hi = lo[None], hi[None]
    attn, lse, stat = attention_fwd(query_rot, key_rot, value_low, lo, hi, move.slots, k_first, k_last)
    stats2 = move.spread(stat)
    branch_low, part = out_project(attn, stats2, gain_branch, shift_branch, full_out)

    def enter(vectors, values, arrived):
        resid = values[0].astype(f32) + (arrived + vectors[0])
        normed, _ = norm_parts(resid)
        return resid, normed * vectors[1] + vectors[2]

    resid, mid_own = own_rows(
        enter, [shift_out, gain_mid, shift_mid], [x_own], move.scatter(part), [f32, bf16], name="enter_ffn"
    )
    mid_low = move.gather(mid_own[0], mid_own[1])
    up_proj, grad_ffn, stat = ffn_up(mid_low, cot_full, full_up, full_down, shift_up, gain_ffn)
    stats4 = move.spread(stat)
    ffn_low, grad_up, part, sums_ff = ffn_mid(up_proj, grad_ffn, stats4, gain_ffn, shift_ffn, full_up)
    arriving = move.scatter(part)
    g_up = tn(mid_low, grad_up).astype(bf16)
    g_down = tn(ffn_low, cot_full).astype(bf16)
    sum_up = lax.psum_scatter(g_up, "batch", scatter_dimension=0, tiled=True)
    sum_down = lax.psum_scatter(g_down, "batch", scatter_dimension=0, tiled=True)

    def leave(vectors, values, arrived):
        normed, inverse = norm_parts(values[0])
        cot = values[1].astype(f32)
        grad = cot + norm_lower(normed, inverse, vectors[0], arrived)
        low = grad.astype(bf16)
        return grad, low, arrived * normed, arrived, low.astype(f32), cot

    grad_resid, resid_own, sums_mid = own_rows(
        leave, [gain_mid], [resid, cot_own], arriving, [f32, bf16], sums=4, after=(g_up, g_down), name="leave_ffn"
    )
    resid_low = move.gather(resid_own[0], resid_own[1])
    down = nn(ffn_low, full_down).astype(bf16)

    grad_branch, stat, sums_branch = branch_back(resid_low, full_out, attn, stats2, gain_branch, after=(down,))
    down, _ = lax.optimization_barrier((down, stat))
    arriving = move.scatter(down)
    stats3 = move.spread(stat)
    g_out = tn(branch_low, resid_low).astype(bf16)
    attn_low, dots = attn_grad(grad_branch, attn, stats2, stats3, gain_branch, after=(g_out,))
    sum_out = lax.psum_scatter(g_out, "batch", scatter_dimension=0, tiled=True)
    grad_qkv = attention_bwd(
        query_rot, key_rot, value_low, attn_low, lse, dots, lo, hi, tables, move.slots, q_first, q_last
    )

    def finish(vectors, values, arrived):
        return (values[0] + (arrived + vectors[0]),)

    result = own_rows(finish, [shift_down], [resid], arriving, [bf16], after=(grad_qkv,), name="finish")[0]
    g_qkv = tn(input_low, grad_qkv).astype(bf16)
    sum_qkv = lax.psum_scatter(g_qkv, "batch", scatter_dimension=0, tiled=True)
    part, sums_qkv, sums_in = input_back(grad_qkv, full_qkv, x_full, after=(g_qkv,))
    arriving = move.scatter(part)

    def end(vectors, values, arrived):
        normed, inverse = norm_parts(values[0].astype(f32))
        return (values[1] + norm_lower(normed, inverse, vectors[0], arrived),)

    def placed(value):
        return lax.dynamic_update_slice(jnp.zeros((value.shape[0], D), f32), value, (0, me * cols))

    branch_rows = placed(sums_branch[:2])
    vector_d = jnp.concatenate(
        [
            placed(sums_qkv[0].reshape(3, cols)),
            sums_in[:1],
            branch_rows[:1],
            sums_mid[:1],
            sums_in[1:2],
            branch_rows[1:],
            sums_mid[1:4],
        ]
    )
    vector_f = sums_ff[:3].reshape(3, batches, 1, strip)
    vector_f = lax.dynamic_update_slice(jnp.zeros((3, batches, ranks, strip), f32), vector_f, (0, 0, me, 0))
    vector = jnp.concatenate(
        [
            vector_d.reshape(11, batches * ranks, d_rows).swapaxes(0, 1).reshape(batches * ranks, -1),
            vector_f.reshape(3, batches * ranks, strip).swapaxes(0, 1).reshape(batches * ranks, -1),
        ],
        axis=1,
    )
    vector = sum_small(vector, batches, ranks)
    grad_total = own_rows(end, [gain_in], [x_own, grad_resid], arriving, [f32], name="end")[0]

    def to_rows(value, groups, wide):
        value = lax.all_to_all(value.reshape(ranks, d_rows, groups, wide), "seq", 0, 2)
        return value.reshape(d_rows, groups * ranks * wide).astype(f32)

    out_qkv = to_rows(sum_qkv, 3, cols)
    out_up = to_rows(sum_up, batches, strip)
    out_out = lax.ppermute(sum_out, EVERY, [(b, a) for a, b in order]).astype(f32)
    out_down = sum_down.astype(f32)
    own_d = vector[:cut].reshape(11, d_rows)
    own_f = vector[cut:].reshape(3, strip)
    return (
        result.reshape(1, rows, D),
        grad_total.reshape(1, rows, D),
        out_qkv,
        own_d[:3],
        out_out,
        out_up,
        out_down,
        own_d[3:6],
        own_d[6:],
        own_f[0],
        own_f[1:],
    )


def solution(mesh):
    sizes = dict(mesh.shape)

    def run(*args):
        return local(*args, batches=sizes["batch"], ranks=sizes["seq"])

    return jax.shard_map(
        run,
        mesh=mesh,
        in_specs=(
            P("batch", "seq", None),
            P("batch", "seq", None),
            P(("batch", "seq"), None),
            P(None, ("batch", "seq")),
            P(("batch", "seq"), None),
            P(("batch", "seq"), None),
            P(("batch", "seq"), None),
            P(None, ("batch", "seq")),
            P(None, ("batch", "seq")),
            P(("batch", "seq")),
            P(None, ("batch", "seq")),
            P("batch"),
            P("batch", None),
            P("batch", None),
        ),
        out_specs=(
            P("batch", "seq", None),
            P("batch", "seq", None),
            P(("batch", "seq"), None),
            P(None, ("batch", "seq")),
            P(("batch", "seq"), None),
            P(("batch", "seq"), None),
            P(("batch", "seq"), None),
            P(None, ("batch", "seq")),
            P(None, ("batch", "seq")),
            P(("batch", "seq")),
            P(None, ("batch", "seq")),
        ),
        check_vma=False,
    )
```

```python
import jax
import jax.numpy as jnp
from jax import lax
from jax.experimental import pallas as pl
from jax.experimental.pallas import tpu as pltpu
from jax.sharding import PartitionSpec as P

D = 2048
HEADS = 32
HEAD_DIM = 64
SEQ_LEN = 2048
SPAN = 64
BLK = 256
NEG_FILL = -1e30
NORM_EPS = 1e-05
EVERY = ("batch", "seq")


def nt(a, b):
    return lax.dot_general(a, b, (((1,), (1,)), ((), ())), preferred_element_type=jnp.float32)


def tn(a, b):
    return lax.dot_general(a, b, (((0,), (0,)), ((), ())), preferred_element_type=jnp.float32)


def nn(a, b):
    return jnp.dot(a, b, preferred_element_type=jnp.float32)


TAKES = {
    "enter_attention": 12,
    "qkv_project": 19,
    "attention_forward": 41,
    "out_project": 14,
    "down_project": 200,
    "add_rows": 30,
    "ffn_up": 54,
    "ffn_mid": 47,
    "branch_back": 150,
    "attn_grad": 38.0,
    "attention_backward": 200.0,
    "input_back": 112.0,
    "enter_ffn": 7,
    "leave_ffn": 100,
    "finish": 6,
    "end": 8,
}


def launch(body, grid, ins, outs, scratch=(), prefetch=(), after=(), name=None):
    n_pre, n_in, n_after = len(prefetch), len(ins), len(after)

    def kernel(*refs):
        body(*refs[: n_pre + n_in], *refs[n_pre + n_in + n_after :])

    return pl.pallas_call(
        kernel,
        out_shape=tuple(jax.ShapeDtypeStruct(s, d) for s, d, _ in outs),
        grid_spec=pltpu.PrefetchScalarGridSpec(
            num_scalar_prefetch=n_pre,
            grid=grid,
            in_specs=[b for _, b in ins] + [pl.BlockSpec(memory_space=pl.ANY)] * n_after,
            out_specs=[b for _, _, b in outs],
            scratch_shapes=list(scratch),
        ),
        compiler_params=pltpu.CompilerParams(vmem_limit_bytes=58 << 20),
        cost_estimate=pl.CostEstimate(flops=int(TAKES[name] * 1e9), bytes_accessed=int(TAKES[name] * 2e6), transcendentals=0),
        name=name,
    )(*prefetch, *(a for a, _ in ins), *after)


def tile(rows, cols):
    return pl.BlockSpec((rows, cols), lambda i, *_: (i, 0))


def fixed(array):
    zeros = (0,) * array.ndim
    return (array, pl.BlockSpec(array.shape, lambda *_: zeros, pipeline_mode=pl.Buffered(1)))


def arrivals(pieces, width):
    counts = [p.shape[0] // BLK for p in pieces]
    starts = [sum(counts[:a]) for a in range(len(counts))]
    inputs = []
    for piece, start, count in zip(pieces, starts, counts):
        if count == 1:
            inputs.append(fixed(piece))
        else:
            spec = pl.BlockSpec((BLK, width), lambda i, *_, s=start, c=count: (jnp.clip(i - s, 0, c - 1), 0))
            inputs.append((piece, spec))

    def read(refs, buffer):
        step = pl.program_id(0)
        for ref, start, count in zip(refs, starts, counts):

            @pl.when((step >= start) & (step < start + count))
            def _():
                buffer[...] = ref[...]

    return inputs, read


def departures(rows, width, groups):
    count = rows // BLK // groups
    outs = []
    for a in range(groups):
        spec = pl.BlockSpec((BLK, width), lambda i, *_, s=a * count: (jnp.clip(i - s, 0, count - 1), 0))
        outs.append(((rows // groups, width), jnp.bfloat16, spec))

    def write(refs, value):
        step = pl.program_id(0)
        for a, ref in enumerate(refs):

            @pl.when(step // count == a)
            def _():
                ref[...] = value

    return outs, write


def columns(lines):
    count, width = len(lines), lines[0].shape[1]
    pad = [jnp.zeros((8 - count, width), jnp.float32)] if count < 8 else []
    flat = jnp.concatenate(list(lines) + pad, axis=0).T
    return [flat[:, i : i + 1] for i in range(count)]


def joined(centers, squares, width):
    count = len(centers)
    center = sum(centers) * (1.0 / count)
    total = sum(squares) + width * sum((c - center) ** 2 for c in centers)
    return center, lax.rsqrt(total * (1.0 / (width * count)) + NORM_EPS)


def rotate(value, tables, sign):
    straight, from_right, from_left = tables
    turned = pltpu.roll(value, 127, 1) * from_right + pltpu.roll(value, 1, 1) * from_left
    return value * straight + turned if sign > 0 else value * straight - turned


def enter_attention(pieces, gain, shift):
    rows, wide = sum(p.shape[0] for p in pieces), pieces[0].shape[1]
    inputs, read = arrivals(pieces, wide)

    def body(g_ref, s_ref, *rest):
        piece_refs, (x_ref, low_ref, stat_ref) = rest[: len(pieces)], rest[len(pieces) :]
        read(piece_refs, x_ref)
        spread = x_ref[...].astype(jnp.float32)
        center = jnp.mean(spread, axis=-1, keepdims=True)
        spread = spread - center
        inverse = lax.rsqrt(jnp.mean(spread * spread, axis=-1, keepdims=True) + NORM_EPS)
        low_ref[...] = (spread * inverse * g_ref[...] + s_ref[...]).astype(jnp.bfloat16)
        lane = lax.broadcasted_iota(jnp.int32, (BLK, 128), 1)
        stat_ref[...] = jnp.where(lane == 0, center, inverse)

    return launch(
        body,
        (rows // BLK,),
        [fixed(gain), fixed(shift)] + inputs,
        [((rows, wide), jnp.bfloat16, tile(BLK, wide))] * 2 + [((rows, 128), jnp.float32, tile(BLK, 128))],
        name="enter_attention",
    )


def qkv_project(low, weight, bias, tables, after=()):
    rows, width = low.shape
    cols = weight.shape[1] // 3

    def body(low_ref, w_ref, b_ref, *rest):
        table_refs, outs = rest[:6], rest[6:]
        for part in range(3):
            span = slice(part * cols, (part + 1) * cols)
            value = nn(low_ref[...], w_ref[:, span]) + b_ref[:, span]
            if part == 2:
                outs[2][...] = value.astype(jnp.bfloat16)
                continue
            own = [t[...] for t in table_refs[3 * part : 3 * part + 3]]
            for at in range(0, cols, 128):
                outs[part][:, at : at + 128] = rotate(value[:, at : at + 128], own, 1).astype(jnp.bfloat16)

    return launch(
        body,
        (rows // BLK,),
        [(low, tile(BLK, width)), fixed(weight), fixed(bias)] + [(t, tile(BLK, 128)) for t in tables],
        [((rows, cols), jnp.bfloat16, tile(BLK, cols))] * 3,
        after=after,
        name="qkv_project",
    )


def attention_fwd(q, k, v, lo, hi, slots, first, last, after=()):
    rows, width = q.shape
    blocks = rows // BLK
    heads = width // HEAD_DIM
    extra = 16

    def body(slots, first, last, q_ref, k_ref, v_ref, lo_ref, hi_ref, o_ref, lse_ref, stat_ref, vt, acc, qt, kept):
        step = pl.program_id(0)

        @pl.when(step == 0)
        def _():
            for i in range(blocks):
                at = slice(i * BLK, (i + 1) * BLK)
                flat = v_ref[at, :].T
                for h in range(heads):
                    vt[h, :HEAD_DIM, at] = flat[h * HEAD_DIM : (h + 1) * HEAD_DIM]
                    vt[h, HEAD_DIM:, at] = jnp.ones((extra, BLK), jnp.bfloat16)

        flat = (q_ref[...] * jnp.bfloat16(HEAD_DIM**-0.5)).T
        zero = jnp.zeros((HEAD_DIM, BLK), jnp.bfloat16)
        for h in range(heads):
            mine = flat[h * HEAD_DIM : (h + 1) * HEAD_DIM, :]
            qt[h] = jnp.concatenate([mine, zero] if h % 2 == 0 else [zero, mine], axis=0)
        low, high = lo_ref[...], hi_ref[...]
        key_row = lax.broadcasted_iota(jnp.int32, (BLK, BLK), 0)

        def scores(kb, peaks):
            at = pl.ds(pl.multiple_of(slots[kb] * BLK, BLK), BLK)
            spot = key_row + kb * BLK
            seen = (spot >= low) & (spot <= high)
            out = []
            for h in range(heads):
                two = slice(h // 2 * 128, h // 2 * 128 + 128)
                s = jnp.where(seen, nn(k_ref[at, two], qt[h]), NEG_FILL)
                kept[kb, h] = s
                out.append(jnp.maximum(peaks[h], jnp.max(s, axis=0, keepdims=True)))
            return tuple(out)

        start = tuple(jnp.full((1, BLK), NEG_FILL, jnp.float32) for _ in range(heads))
        peaks = lax.fori_loop(first[step], last[step], scores, start)
        acc[...] = jnp.zeros_like(acc)

        def weigh(kb, _):
            at = pl.ds(pl.multiple_of(slots[kb] * BLK, BLK), BLK)
            for h in range(heads):
                p = jnp.exp(kept[kb, h] - peaks[h]).astype(jnp.bfloat16)
                acc[h] += nn(vt[h, :, at], p)
            return 0

        lax.fori_loop(first[step], last[step], weigh, 0)
        parts = []
        for h in range(heads):
            total = acc[h, HEAD_DIM : HEAD_DIM + 1, :]
            lse_ref[h : h + 1, :] = peaks[h] + jnp.log(total)
            parts.append(acc[h, :HEAD_DIM] / total)
        flat = jnp.concatenate(parts, axis=0)
        center = jnp.mean(flat, axis=0, keepdims=True)
        stat_ref[0:1, :] = center
        stat_ref[1:2, :] = jnp.sum((flat - center) ** 2, axis=0, keepdims=True)
        stat_ref[2:8, :] = jnp.zeros((6, BLK), jnp.float32)
        o_ref[...] = flat.T

    by_slot = pl.BlockSpec((BLK, width), lambda i, s, *_: (s[i], 0))
    line = pl.BlockSpec((1, BLK), lambda i, *_: (0, i))
    return launch(
        body,
        (blocks,),
        [(q, by_slot), fixed(k), fixed(v), (lo, line), (hi, line)],
        [
            ((rows, width), jnp.float32, by_slot),
            ((heads, rows), jnp.float32, pl.BlockSpec((heads, BLK), lambda i, s, *_: (0, s[i]))),
            ((8, rows), jnp.float32, pl.BlockSpec((8, BLK), lambda i, s, *_: (0, s[i]))),
        ],
        scratch=[
            pltpu.VMEM((heads, HEAD_DIM + extra, rows), jnp.bfloat16),
            pltpu.VMEM((heads, HEAD_DIM + extra, BLK), jnp.float32),
            pltpu.VMEM((heads, 128, BLK), jnp.bfloat16),
            pltpu.VMEM((blocks, heads, BLK, BLK), jnp.float32),
        ],
        prefetch=(slots, first, last),
        after=after,
        name="attention_forward",
    )


def out_project(attn, stats, gain, shift, weight, groups, after=()):
    rows, width = attn.shape
    wide = weight.shape[1]
    outs, write = departures(rows, wide, groups)

    def body(a_ref, g_ref, s_ref, w_ref, *rest):
        stat_refs, (low_ref, *part_refs) = rest[: len(stats)], rest[len(stats) :]
        center, inverse = columns(joined([r[0:1] for r in stat_refs], [r[1:2] for r in stat_refs], width))
        low = ((a_ref[...] - center) * inverse * g_ref[...] + s_ref[...]).astype(jnp.bfloat16)
        low_ref[...] = low
        write(part_refs, nn(low, w_ref[...]).astype(jnp.bfloat16))

    low, *parts = launch(
        body,
        (rows // BLK,),
        [(attn, tile(BLK, width)), fixed(gain), fixed(shift), fixed(weight)] + list(stats),
        [((rows, width), jnp.bfloat16, tile(BLK, width))] + outs,
        after=after,
        name="out_project",
    )
    return low, parts


def down_project(low, weight, groups, after=()):
    rows, width = low.shape
    wide = weight.shape[1]
    outs, write = departures(rows, wide, groups)

    def body(l_ref, w_ref, *part_refs):
        write(part_refs, nn(l_ref[...], w_ref[...]).astype(jnp.bfloat16))

    return launch(
        body,
        (rows // BLK,),
        [(low, tile(BLK, width)), fixed(weight)],
        outs,
        after=after,
        name="down_project",
    )


def add_rows(pairs, after=()):
    wide = pairs[0][0].shape[1]
    half = pairs[0][0].shape[0] // 2
    piece = min(128, half)

    def body(*refs):
        ins, outs = refs[: 2 * len(pairs)], refs[2 * len(pairs) :]
        for i, ref in enumerate(outs):
            ref[...] = (ins[2 * i][...].astype(jnp.float32) + ins[2 * i + 1][...].astype(jnp.float32)).astype(jnp.bfloat16)

    spec = pl.BlockSpec((piece, wide), lambda i: (half // piece + i, 0))
    return launch(
        body,
        (half // piece,),
        [(x, spec) for pair in pairs for x in pair],
        [((half, wide), jnp.bfloat16, tile(piece, wide))] * len(pairs),
        after=after,
        name="add_rows",
    )


def own_rows(body, wholes, rows_in, terms, outs, sums=0, after=(), name=None):
    half, wide = rows_in[0][0].shape
    piece = min(128, half)
    count = len(terms[0])

    def kernel(*refs):
        whole_refs, refs = refs[: len(wholes)], refs[len(wholes) :]
        row_refs, refs = refs[: 2 * len(rows_in)], refs[2 * len(rows_in) :]
        term_refs, out_refs = refs[: 2 * count], list(refs[2 * count :])
        targets = []
        for _, stacked in outs:
            if stacked:
                ref = out_refs.pop(0)
                targets.append((ref.at[0], ref.at[1]))
            else:
                targets.append((out_refs.pop(0), out_refs.pop(0)))
        vectors = [r[...] for r in whole_refs]
        added = [0.0] * sums
        for side in range(2):
            total = term_refs[side * count][...].astype(jnp.float32)
            for r in term_refs[side * count + 1 : (side + 1) * count]:
                total = total + r[...].astype(jnp.float32)
            values = body(vectors, [r[...] for r in row_refs[side::2]], total)
            for target, value in zip(targets, values[: len(outs)]):
                target[side][...] = value.astype(target[side].dtype)
            added = [a + jnp.sum(v, axis=0, keepdims=True) for a, v in zip(added, values[len(outs) :])]
        if sums:
            sum_ref = out_refs[0]

            @pl.when(pl.program_id(0) == 0)
            def _():
                sum_ref[...] = jnp.zeros_like(sum_ref)

            for i, a in enumerate(added):
                sum_ref[i : i + 1, :] += a

    pieces = []
    for side in range(2):
        for array, start in terms[side]:
            pieces.append((array, pl.BlockSpec((piece, wide), lambda i, at=start // piece: (at + i, 0))))
    results = []
    for d, stacked in outs:
        if stacked:
            results.append(((2, half, wide), d, pl.BlockSpec((2, piece, wide), lambda i: (0, i, 0))))
        else:
            results += [((half, wide), d, tile(piece, wide))] * 2
    if sums:
        results.append(((8, wide), jnp.float32, pl.BlockSpec((8, wide), lambda i: (0, 0))))
    return launch(
        kernel,
        (half // piece,),
        [fixed(w) for w in wholes] + [(r, tile(piece, wide)) for pair in rows_in for r in pair] + pieces,
        results,
        after=after,
        name=name,
    )


def norm_parts(values):
    center = jnp.mean(values, axis=-1, keepdims=True)
    spread = values - center
    inverse = lax.rsqrt(jnp.mean(spread * spread, axis=-1, keepdims=True) + NORM_EPS)
    return spread * inverse, inverse


def norm_lower(normed, inverse, gain, upper):
    scaled = upper * gain
    first_mean = jnp.mean(scaled, axis=-1, keepdims=True)
    second_mean = jnp.mean(scaled * normed, axis=-1, keepdims=True)
    return inverse * (scaled - first_mean - normed * second_mean)


GELU_A = 0.044715
GELU_C = 0.7978845608028654


def ffn_up(pieces, cot, w_up, w_down, bias, gain, after=()):
    rows, wide = cot.shape
    inputs, read = arrivals(pieces, wide)
    units = w_up.shape[1]
    chunk = min(512, units)

    def body(c_ref, u_w, d_w, b_ref, g_ref, *rest):
        m_ref, up_ref, grad_ref, stat_ref, gel_ref = rest[len(pieces) :]
        read(rest[: len(pieces)], m_ref)
        total = scaled_total = 0.0
        for at in range(0, units, chunk):
            span = slice(at, at + chunk)
            up = nn(m_ref[...], u_w[:, span]) + b_ref[:, span]
            grad = nt(c_ref[...], d_w[span, :])
            up_ref[:, span] = up
            grad_ref[:, span] = grad
            gel = 0.5 * up * (1.0 + jnp.tanh(GELU_C * (up + GELU_A * up * up * up)))
            gel_ref[:, span] = gel
            total = total + jnp.sum(gel, axis=1, keepdims=True)
            scaled_total = scaled_total + jnp.sum(grad * g_ref[:, span], axis=1, keepdims=True)
        center = total * (1.0 / units)
        square = product = 0.0
        for at in range(0, units, chunk):
            span = slice(at, at + chunk)
            spread = gel_ref[:, span] - center
            square = square + jnp.sum(spread * spread, axis=1, keepdims=True)
            product = product + jnp.sum(grad_ref[:, span] * g_ref[:, span] * spread, axis=1, keepdims=True)
        lane = lax.broadcasted_iota(jnp.int32, (BLK, 128), 1)
        flat = jnp.zeros((BLK, 128), jnp.float32)
        for i, value in enumerate((center, square, scaled_total, product)):
            flat = jnp.where(lane == i, value, flat)
        stat_ref[...] = flat.T[0:8, :]

    return launch(
        body,
        (rows // BLK,),
        [(cot, tile(BLK, wide)), fixed(w_up), fixed(w_down), fixed(bias), fixed(gain)] + inputs,
        [
            ((rows, wide), jnp.bfloat16, tile(BLK, wide)),
            ((rows, units), jnp.float32, tile(BLK, units)),
            ((rows, units), jnp.float32, tile(BLK, units)),
            ((8, rows), jnp.float32, pl.BlockSpec((8, BLK), lambda i, *_: (0, i))),
        ],
        scratch=[pltpu.VMEM((BLK, units), jnp.float32)],
        after=after,
        name="ffn_up",
    )


def ffn_mid(up, grad, stats, gain, shift, w_up, groups):
    rows, units = up.shape
    wide = w_up.shape[0]
    chunk = min(512, units)
    ranks = len(stats)
    outs, write = departures(rows, wide, groups)

    def body(u_ref, f_ref, g_ref, s_ref, w_ref, *rest):
        stat_refs, (low_ref, gup_ref, sum_ref, *part_refs) = rest[:ranks], rest[ranks:]
        centers = [r[0:1] for r in stat_refs]
        center, inverse = joined(centers, [r[1:2] for r in stat_refs], units)
        share = 1.0 / (units * ranks)
        first = sum(r[2:3] for r in stat_refs) * share
        second = inverse * share * sum(r[3:4] + (c - center) * r[2:3] for r, c in zip(stat_refs, centers))
        center, inverse, first, second = columns([center, inverse, first, second])

        @pl.when(pl.program_id(0) == 0)
        def _():
            sum_ref[...] = jnp.zeros_like(sum_ref)

        for at in range(0, units, chunk):
            span = slice(at, at + chunk)
            u, f = u_ref[:, span], f_ref[:, span]
            squared = u * u
            t = jnp.tanh(GELU_C * u * (1.0 + GELU_A * squared))
            one = 0.5 * (1.0 + t)
            slope = one + 0.5 * u * (1.0 - t * t) * (GELU_C * (1.0 + 3.0 * GELU_A * squared))
            normed = (u * one - center) * inverse
            low_ref[:, span] = (normed * g_ref[:, span] + s_ref[:, span]).astype(jnp.bfloat16)
            lower = inverse * (f * g_ref[:, span] - first - normed * second)
            gup = (lower * slope).astype(jnp.bfloat16)
            gup_ref[:, span] = gup
            sum_ref[0:1, span] += jnp.sum(f * normed, axis=0, keepdims=True)
            sum_ref[1:2, span] += jnp.sum(f, axis=0, keepdims=True)
            sum_ref[2:3, span] += jnp.sum(gup.astype(jnp.float32), axis=0, keepdims=True)
        write(part_refs, nt(gup_ref[...], w_ref[...]).astype(jnp.bfloat16))

    low, gup, sums, *parts = launch(
        body,
        (rows // BLK,),
        [(up, tile(BLK, units)), (grad, tile(BLK, units)), fixed(gain), fixed(shift), fixed(w_up)] + list(stats),
        [
            ((rows, units), jnp.bfloat16, tile(BLK, units)),
            ((rows, units), jnp.bfloat16, tile(BLK, units)),
            ((8, units), jnp.float32, pl.BlockSpec((8, units), lambda i, *_: (0, 0))),
        ]
        + outs,
        name="ffn_mid",
    )
    return low, gup, sums, parts


def branch_back(pieces, w_out, attn, stats, gain, after=()):
    rows, width = attn.shape
    wide = w_out.shape[1]
    ranks = len(stats)
    inputs, read = arrivals(pieces, wide)

    def body(w_ref, a_ref, g_ref, *rest):
        stat_refs, rest = rest[:ranks], rest[ranks:]
        r_ref, grad_ref, stat_ref, sum_ref = rest[len(pieces) :]
        read(rest[: len(pieces)], r_ref)
        center, inverse = columns(joined([r[0:1] for r in stat_refs], [r[1:2] for r in stat_refs], width))

        @pl.when(pl.program_id(0) == 0)
        def _():
            sum_ref[...] = jnp.zeros_like(sum_ref)

        grad = nt(r_ref[...], w_ref[...])
        grad_ref[...] = grad
        normed = (a_ref[...] - center) * inverse
        scaled = grad * g_ref[...]
        sum_ref[0:1, :] += jnp.sum(grad * normed, axis=0, keepdims=True)
        sum_ref[1:2, :] += jnp.sum(grad, axis=0, keepdims=True)
        lane = lax.broadcasted_iota(jnp.int32, (BLK, 128), 1)
        flat = jnp.where(lane == 0, jnp.sum(scaled, axis=1, keepdims=True), 0.0)
        flat = jnp.where(lane == 1, jnp.sum(scaled * normed, axis=1, keepdims=True), flat)
        stat_ref[...] = flat.T[0:8, :]

    return launch(
        body,
        (rows // BLK,),
        [fixed(w_out), (attn, tile(BLK, width)), fixed(gain)] + list(stats) + inputs,
        [
            ((rows, wide), jnp.bfloat16, tile(BLK, wide)),
            ((rows, width), jnp.float32, tile(BLK, width)),
            ((8, rows), jnp.float32, pl.BlockSpec((8, BLK), lambda i, *_: (0, i))),
            ((8, width), jnp.float32, pl.BlockSpec((8, width), lambda i, *_: (0, 0))),
        ],
        after=after,
        name="branch_back",
    )


def attn_grad(grad, attn, stats, sums, gain, after=()):
    rows, width = attn.shape
    ranks = len(stats)
    heads = width // HEAD_DIM

    def body(f_ref, a_ref, g_ref, *rest):
        stat_refs, sum_refs = rest[:ranks], rest[ranks : 2 * ranks]
        out_ref, dot_ref = rest[2 * ranks :]
        center, inverse = joined([r[0:1] for r in stat_refs], [r[1:2] for r in stat_refs], width)
        share = 1.0 / (width * ranks)
        first = sum(r[0:1] for r in sum_refs) * share
        second = sum(r[1:2] for r in sum_refs) * share
        center, inverse, first, second = columns([center, inverse, first, second])
        attn_here = a_ref[...]
        normed = (attn_here - center) * inverse
        out = (inverse * (f_ref[...] * g_ref[...] - first - normed * second)).astype(jnp.bfloat16)
        out_ref[...] = out
        product = (out.astype(jnp.float32) * attn_here).T
        for h in range(heads):
            dot_ref[h : h + 1, :] = jnp.sum(product[h * HEAD_DIM : (h + 1) * HEAD_DIM], axis=0, keepdims=True)

    return launch(
        body,
        (rows // BLK,),
        [(grad, tile(BLK, width)), (attn, tile(BLK, width)), fixed(gain)] + list(stats) + list(sums),
        [
            ((rows, width), jnp.bfloat16, tile(BLK, width)),
            ((heads, rows), jnp.float32, pl.BlockSpec((heads, BLK), lambda i, *_: (0, i))),
        ],
        after=after,
        name="attn_grad",
    )


def attention_bwd(part, parts, q, k, v, g, lse, dot, lo, hi, tables, slots, first, last, after=()):
    rows, width = q.shape
    width //= parts
    blocks = rows // BLK
    heads = width // HEAD_DIM
    base = part * heads
    scale = HEAD_DIM**-0.5
    own_columns = pl.BlockSpec((rows, width), lambda *_: (0, part), pipeline_mode=pl.Buffered(1))

    def body(slots, first, last, q_ref, k_ref, v_ref, g_ref, lse_ref, dot_ref, lo_ref, hi_ref, *rest):
        table_refs, (out_ref, dqt, qt, gt, accs) = rest[:6], rest[6:]
        key_row = lax.broadcasted_iota(jnp.int32, (BLK, BLK), 0)
        lane = lax.broadcasted_iota(jnp.int32, (BLK, 128), 1)
        zero = jnp.zeros((), jnp.bfloat16)
        dqt[...] = jnp.zeros_like(dqt)
        for i in range(blocks):
            at = slice(i * BLK, (i + 1) * BLK)
            qt[:, at] = q_ref[at, :].T
            gt[:, at] = g_ref[at, :].T

        def outer(kb, _):
            rows_k = pl.ds(pl.multiple_of(slots[kb] * BLK, BLK), BLK)
            k, v = k_ref[rows_k, :] * jnp.bfloat16(scale), v_ref[rows_k, :]
            kts = k.T
            spot = key_row + kb * BLK

            def halves(x, h):
                x = x[:, h // 2 * 128 : h // 2 * 128 + 128]
                return jnp.where((lane < HEAD_DIM) == (h % 2 == 0), x, zero)

            ks = [halves(k, h) for h in range(heads)]
            vs = [halves(v, h) for h in range(heads)]
            accs[...] = jnp.zeros_like(accs)

            def inner(qb, _):
                at = pl.ds(pl.multiple_of(slots[qb] * BLK, BLK), BLK)
                here = pl.ds(pl.multiple_of(qb * BLK, BLK), BLK)
                seen = (spot >= lo_ref[0:1, here]) & (spot <= hi_ref[0:1, here])
                for h in range(heads):
                    two = slice(h // 2 * 128, h // 2 * 128 + 128)
                    span = slice(h * HEAD_DIM, (h + 1) * HEAD_DIM)
                    s = nn(ks[h], qt[two, at])
                    p = jnp.where(seen, jnp.exp(s - lse_ref[base + h : base + h + 1, at]), 0.0)
                    dp = nn(vs[h], gt[two, at])
                    ds = (p * (dp - dot_ref[base + h : base + h + 1, at])).astype(jnp.bfloat16)
                    accs[1, h] += nn(p.astype(jnp.bfloat16), g_ref[at, two])
                    accs[0, h] += nn(ds, q_ref[at, two])
                    dqt[span, at] += nn(kts[span, :], ds)
                return 0

            lax.fori_loop(first[kb], last[kb], inner, 0)
            own = [t[rows_k, :] for t in table_refs[3:]]
            for h in range(0, heads, 2):
                at = h * HEAD_DIM
                grad_k = jnp.where(lane < HEAD_DIM, accs[0, h], accs[0, h + 1]) * scale
                grad_v = jnp.where(lane < HEAD_DIM, accs[1, h], accs[1, h + 1])
                out_ref[rows_k, width + at : width + at + 128] = rotate(grad_k, own, -1).astype(jnp.bfloat16)
                out_ref[rows_k, 2 * width + at : 2 * width + at + 128] = grad_v.astype(jnp.bfloat16)
            return 0

        lax.fori_loop(0, blocks, outer, 0)
        for i in range(blocks):
            at = slice(i * BLK, (i + 1) * BLK)
            grad_q = dqt[:, at].T
            own = [t[at, :] for t in table_refs[:3]]
            for col in range(0, width, 128):
                out_ref[at, col : col + 128] = rotate(grad_q[:, col : col + 128], own, -1).astype(jnp.bfloat16)

    return launch(
        body,
        (1,),
        [(a, own_columns) for a in (q, k, v, g)] + [fixed(a) for a in (lse, dot, lo, hi, *tables)],
        [((rows, 3 * width), jnp.bfloat16, pl.BlockSpec((rows, 3 * width), lambda *_: (0, 0), pipeline_mode=pl.Buffered(1)))],
        scratch=[
            pltpu.VMEM((width, rows), jnp.float32),
            pltpu.VMEM((width, rows), jnp.bfloat16),
            pltpu.VMEM((width, rows), jnp.bfloat16),
            pltpu.VMEM((2, heads, BLK, 128), jnp.float32),
        ],
        prefetch=(slots, first, last),
        after=after,
        name="attention_backward",
    )[0]


def input_back(grads, weight, x, row_stats, groups, after=()):
    rows, wide = x.shape
    cols = weight.shape[1]
    parts = len(grads)
    small = cols // parts // 3
    outs, write = departures(rows, wide, groups)

    def body(w_ref, x_ref, stat_ref, *rest):
        grad_refs, (bias_ref, sum_ref, *part_refs), g_ref = rest[:parts], rest[parts:-1], rest[-1]

        @pl.when(pl.program_id(0) == 0)
        def _():
            sum_ref[...] = jnp.zeros_like(sum_ref)
            bias_ref[...] = jnp.zeros_like(bias_ref)

        for p, ref in enumerate(grad_refs):
            for j in range(3):
                at = (j * parts + p) * small
                g_ref[:, at : at + small] = ref[:, j * small : (j + 1) * small]
        value = nt(g_ref[...], w_ref[...])
        write(part_refs, value.astype(jnp.bfloat16))
        bias_ref[0:1, :] += jnp.sum(g_ref[...].astype(jnp.float32), axis=0, keepdims=True)
        normed = (x_ref[...].astype(jnp.float32) - stat_ref[:, 0:1]) * stat_ref[:, 1:2]
        sum_ref[0:1, :] += jnp.sum(value * normed, axis=0, keepdims=True)
        sum_ref[1:2, :] += jnp.sum(value, axis=0, keepdims=True)

    bias_sums, sums, *parts_out = launch(
        body,
        (rows // BLK,),
        [fixed(weight), (x, tile(BLK, wide)), (row_stats, tile(BLK, 128))]
        + [(g, tile(BLK, cols // parts)) for g in grads],
        [
            ((8, cols), jnp.float32, pl.BlockSpec((8, cols), lambda i, *_: (0, 0))),
            ((8, wide), jnp.float32, pl.BlockSpec((8, wide), lambda i, *_: (0, 0))),
        ]
        + outs,
        scratch=[pltpu.VMEM((BLK, cols), jnp.bfloat16)],
        after=after,
        name="input_back",
    )
    return bias_sums, sums, parts_out


def key_limits(bounds, spans, kind, total):
    places = jnp.arange(total, dtype=jnp.int32)
    below = bounds[:, None] <= places[None, :]
    doc_first = jnp.max(jnp.where(below, bounds[:, None], 0), axis=0)
    doc_last = jnp.min(jnp.where(below, total, bounds[:, None]), axis=0) - 1
    doc_last = jnp.minimum(doc_last, total - 1)
    inside = (spans[:, None] <= places[None, :]) & (places[None, :] < spans[:, None] + SPAN) & (kind > 0)
    span_last = jnp.max(jnp.where(inside, spans[:, None] + SPAN - 1, 0), axis=0)
    span_first = jnp.min(jnp.where(inside, spans[:, None], total), axis=0)
    hi = jnp.minimum(jnp.maximum(places, span_last), doc_last)
    q_first = jnp.maximum(jnp.minimum(places, span_first), doc_first)
    return doc_first, hi, q_first, doc_last


def block_limits(lo, hi, qf, ql):
    low = lo.reshape(-1, BLK)[:, 0] // BLK
    high = hi.reshape(-1, BLK)[:, -1] // BLK + 1
    qlow = qf.reshape(-1, BLK)[:, 0] // BLK
    qhigh = ql.reshape(-1, BLK)[:, -1] // BLK + 1
    return low, high, qlow, qhigh


class Exchange:
    def __init__(self, ranks, batches, rows, me):
        self.ranks, self.batches, self.rows, self.me = ranks, batches, rows, me
        self.square = ranks == 4 and rows == 2 * BLK
        self.half = rows // 2
        self.groups = 4 if self.square else 1
        self.forwarded = ()
        self.order = ((0, 1, 2, 3), (0, 2, 1, 3))
        total = ranks * rows
        block = jnp.arange(total // BLK, dtype=jnp.int32)
        if self.square:
            owner, part = block // 2, block % 2
            near = owner ^ me
            swapped = (near >> 1) | ((near & 1) << 1)
            self.slots = (part * 4 + jnp.where(part == 0, near, swapped)).astype(jnp.int32)
            owners = jnp.stack([me ^ r for half in self.order for r in half])
            firsts = owners * rows + jnp.repeat(jnp.arange(2), 4) * self.half
            self.places = (firsts[:, None] + jnp.arange(self.half)[None, :]).reshape(total).astype(jnp.int32)
        else:
            self.slots = block
            self.places = jnp.arange(total, dtype=jnp.int32)

    def swap(self, value, bit):
        return lax.ppermute(value, "seq", [(r, r ^ bit) for r in range(self.ranks)])

    def gather(self, upper, lower, late=None):
        if not self.square:
            return [lax.all_gather(jnp.concatenate([upper, lower], axis=0), "seq", axis=0, tiled=True)]
        near_upper, near_lower = self.swap(upper, 1), self.swap(lower, 2)
        again = (upper, lower, near_upper, near_lower)
        if late is not None:
            again, _ = lax.optimization_barrier((again, late))
        return [upper, near_upper, self.swap(again[0], 2), self.swap(again[2], 2)] + [
            lower,
            near_lower,
            self.swap(again[1], 1),
            self.swap(again[3], 1),
        ]

    def scatter(self, parts, after=()):
        if not self.square:
            own = lax.psum_scatter(parts[0], "seq", scatter_dimension=0, tiled=True)
            return [[(own, 0)], [(own, self.half)]]
        keep_upper, send_upper, keep_lower, send_lower = parts
        near_upper, near_lower = self.swap(send_upper, 2), self.swap(send_lower, 1)
        far_upper, far_lower = add_rows([(keep_upper, near_upper), (keep_lower, near_lower)], after)
        sums = (far_upper, far_lower)
        far_upper, far_lower = self.swap(far_upper, 1), self.swap(far_lower, 2)
        self.forwarded = sums
        return [[(keep_upper, 0), (near_upper, 0), (far_upper, 0)], [(keep_lower, 0), (near_lower, 0), (far_lower, 0)]]

    def picked(self, value, axis):
        if not self.square:
            return [jnp.moveaxis(value, axis, 0)]
        return [lax.dynamic_index_in_dim(value, self.me ^ r, axis, False) for r in range(self.ranks)]

    def sent(self, pieces):
        if not self.square:
            return [lax.all_to_all(pieces[0], "seq", 0, 0)]
        return [pieces[0]] + [self.swap(pieces[r], r) for r in range(1, self.ranks)]

    def ordered(self, pieces):
        return flipped(jnp.stack(pieces), self.me, 2) if self.square else pieces[0]

    def spread(self, value):
        lines = value.shape[0]
        if not self.square:
            every = lax.all_gather(value, "seq", axis=0)
            return [(every[r], pl.BlockSpec((lines, BLK), lambda i, *_: (0, i))) for r in range(self.ranks)]
        out = [(value, pl.BlockSpec((lines, BLK), lambda i, *_: (0, i)))]
        for bit, other in ((1, 2), (2, 1), (3, 3)):
            spec = pl.BlockSpec(
                (lines, BLK), lambda i, *_, a=bit, b=other: (0, (i // 4) * 4 + ((i % 4) ^ (a + (i // 4) * (b - a))))
            )
            out.append((self.swap(value, bit), spec))
        return out


def flipped(value, device, bits):
    shape = value.shape
    for bit in range(bits):
        two = value.reshape((-1, 2, 1 << bit) + shape[1:])
        value = jnp.where((device >> bit) & 1, two[:, ::-1], two).reshape(shape)
    return value


def share_small(value, batches, ranks):
    if (batches, ranks) != (8, 4):
        return lax.all_gather(value, EVERY, axis=0)
    batch, me = lax.axis_index("batch"), lax.axis_index("seq")
    parts = value[None]
    for axis, count, steps in (("seq", ranks, (1, 2, 3)), ("batch", batches, (1,)), ("batch", batches, (2, 4, 6))):
        parts = jnp.concatenate(
            [parts] + [lax.ppermute(parts, axis, [(r, r ^ s) for r in range(count)]) for s in steps], axis=0
        )
    return flipped(parts, batch * ranks + me, 5)


def sum_small(value, batches, ranks, late):
    if (batches, ranks) != (8, 4):
        return lax.psum_scatter(value, EVERY, scatter_dimension=0, tiled=True)[0]
    batch, me = lax.axis_index("batch"), lax.axis_index("seq")
    value = flipped(value, batch * ranks + me, 5)
    for axis, count, steps, left in (("batch", batches, (2, 4, 6), 8), ("batch", batches, (1,), 4), ("seq", ranks, (1, 2, 3), 1)):
        if axis == "seq":
            value, _ = lax.optimization_barrier((value, late))
        total = value[:left]
        for i, s in enumerate(steps):
            at = (i + 1) * left
            total = total + lax.ppermute(value[at : at + left], axis, [(r, r ^ s) for r in range(count)])
        value = total
    return value[0]


def rot_tables(places):
    column = jnp.arange(128) % HEAD_DIM
    pair_idx = (column // 2).astype(jnp.float32)
    frequency = jnp.power(10000.0, -2.0 * pair_idx / HEAD_DIM)
    place_float = places.astype(jnp.float32)
    angles = place_float[:, None] * frequency[None, :]
    zeta_base = (2.0 * pair_idx + 0.4 * HEAD_DIM) / (1.4 * HEAD_DIM)
    exponent = (place_float - SEQ_LEN // 2) / 512.0
    scales = jnp.power(zeta_base[None, :], exponent[:, None])
    cosine, sine = jnp.cos(angles), jnp.sin(angles)
    even = (column % 2 == 0)[None, :]
    right, left = jnp.where(even, -sine, 0.0), jnp.where(even, 0.0, sine)
    return tuple(t * s for s in (scales, 1.0 / scales) for t in (cosine, right, left))


def local(
    layer_input,
    cotangent,
    w_qkv,
    bias_qkv,
    w_out,
    w_up,
    w_down,
    gains_d,
    biases_d,
    gain_ff,
    biases_ff,
    data_type,
    doc_bounds,
    span_starts,
    *,
    batches,
    ranks,
):
    me = lax.axis_index("seq")
    rows = layer_input.shape[1]
    half = rows // 2
    move = Exchange(ranks, batches, rows, me)
    tokens = rows * ranks
    cols = D // ranks
    strip, d_rows = w_down.shape[0], w_up.shape[0]
    units = strip * batches
    f32, bf16 = jnp.float32, jnp.bfloat16
    x_own = [layer_input.reshape(2, half, D)[i] for i in range(2)]
    cot_own = [cotangent.reshape(2, half, D)[i] for i in range(2)]

    x_pieces = move.gather(*x_own, late=())
    small = jnp.concatenate(
        [bias_qkv.reshape(-1), gains_d.reshape(-1), biases_d.reshape(-1), gain_ff, biases_ff.reshape(-1)]
    )
    small = share_small(small, batches, ranks)

    w_qkv, _ = lax.optimization_barrier((w_qkv, x_own))
    part_qkv = move.ordered(move.sent(move.picked(w_qkv.reshape(d_rows, 3, ranks, cols), 2)))
    up_pieces = move.picked(w_up.reshape(d_rows, batches, ranks, strip), 2)
    order = [(i, (i % batches) * ranks + i // batches) for i in range(batches * ranks)]
    part_out = lax.ppermute(w_out, EVERY, order)
    tables = rot_tables(move.places)
    early = (small, part_out, up_pieces, tables, x_pieces[1:2] + x_pieces[5:6])
    part_qkv, (small, part_out, up_pieces, tables, _) = lax.optimization_barrier((part_qkv, early))
    full_qkv = lax.all_gather(part_qkv.reshape(d_rows * ranks, 3 * cols), "batch", axis=0, tiled=True)
    cut = 11 * d_rows
    rows_d = small[:, :cut].reshape(-1, 11, d_rows).swapaxes(0, 1).reshape(11, D).astype(f32)
    rows_f = small[:, cut:].reshape(batches, ranks, 3, strip)
    rows_f = lax.dynamic_index_in_dim(rows_f, me, 1, False).swapaxes(0, 1).reshape(3, units).astype(f32)
    qkv_shift = lax.dynamic_slice_in_dim(rows_d[:3], me * cols, cols, 1).reshape(1, 3 * cols)
    branch = lax.dynamic_slice_in_dim(rows_d[3:], me * cols, cols, 1)
    gain_in, gain_mid = rows_d[3:4], rows_d[5:6]
    shift_in, shift_mid, shift_out, shift_down = rows_d[6:7], rows_d[8:9], rows_d[9:10], rows_d[10:11]
    gain_branch, shift_branch = branch[1:2], branch[4:5]
    gain_ffn, shift_ffn, shift_up = rows_f[0:1], rows_f[1:2], rows_f[2:3]

    (up_pieces, *cot_send), _ = lax.optimization_barrier(((up_pieces, *cot_own), x_pieces))
    full_out = lax.all_gather(part_out, "batch", axis=0, tiled=True)
    full_down = lax.all_gather(w_down, "batch", axis=0, tiled=True)
    up_pieces = move.sent(up_pieces)

    x_full, input_low, row_stats = enter_attention(x_pieces, gain_in, shift_in)
    query_rot, key_rot, value_low = qkv_project(input_low, full_qkv, qkv_shift, tables)
    cot_pieces = move.gather(*cot_send, late=(query_rot,))
    up_pieces, _ = lax.optimization_barrier((up_pieces, query_rot))
    full_up = lax.all_gather(move.ordered(up_pieces).reshape(d_rows * ranks, units), "batch", axis=0, tiled=True)
    lo, hi, q_lo, q_hi = key_limits(doc_bounds[0], span_starts[0], data_type[0], tokens)
    k_first, k_last, q_first, q_last = block_limits(lo, hi, q_lo, q_hi)
    lo, hi = lo[None], hi[None]
    attn, lse, stat = attention_fwd(
        query_rot, key_rot, value_low, lo, hi, move.slots, k_first, k_last, after=cot_pieces[1:2] + cot_pieces[5:6]
    )
    stat, _ = lax.optimization_barrier((stat, cot_pieces))
    stats2 = move.spread(stat)
    branch_low, parts = out_project(attn, stats2, gain_branch, shift_branch, full_out, move.groups, after=cot_pieces)

    def enter(vectors, values, arrived):
        resid = values[0].astype(f32) + (arrived + vectors[0])
        normed, _ = norm_parts(resid)
        return resid, normed * vectors[1] + vectors[2]

    cot_full = jnp.concatenate(cot_pieces, axis=0)
    *resid, mid_upper, mid_lower = own_rows(
        enter,
        [shift_out, gain_mid, shift_mid],
        [x_own],
        move.scatter(parts),
        [(f32, False), (bf16, False)],
        after=(cot_full,),
        name="enter_ffn",
    )
    mid_pieces = move.gather(mid_upper, mid_lower)
    mid_low, up_proj, grad_ffn, stat = ffn_up(mid_pieces, cot_full, full_up, full_down, shift_up, gain_ffn)
    stats4 = move.spread(stat)
    ffn_low, grad_up, sums_ff, parts = ffn_mid(up_proj, grad_ffn, stats4, gain_ffn, shift_ffn, full_up, move.groups)
    g_down = tn(ffn_low, cot_full).astype(bf16)
    sum_down = lax.psum_scatter(g_down, "batch", scatter_dimension=0, tiled=True)
    arriving = move.scatter(parts, (g_down,))
    grad_up, _ = lax.optimization_barrier((grad_up, move.forwarded))
    g_up = tn(mid_low, grad_up).astype(bf16)
    sum_up = lax.psum_scatter(g_up, "batch", scatter_dimension=0, tiled=True)

    def leave(vectors, values, arrived):
        normed, inverse = norm_parts(values[0])
        cot = values[1].astype(f32)
        grad = cot + norm_lower(normed, inverse, vectors[0], arrived)
        low = grad.astype(bf16)
        return grad, low, arrived * normed, arrived, low.astype(f32), cot

    *grad_resid, resid_upper, resid_lower, sums_mid = own_rows(
        leave,
        [gain_mid],
        [resid, cot_own],
        arriving,
        [(f32, False), (bf16, False)],
        sums=4,
        after=(g_up,),
        name="leave_ffn",
    )
    resid_pieces = move.gather(resid_upper, resid_lower)
    down_parts = down_project(ffn_low, full_down, move.groups, after=(resid_upper,))

    resid_low, grad_branch, stat, sums_branch = branch_back(
        resid_pieces, full_out, attn, stats2, gain_branch, after=down_parts
    )
    down_parts, _ = lax.optimization_barrier((down_parts, resid_pieces))
    stats3 = move.spread(stat)
    g_out = tn(branch_low, resid_low).astype(bf16)
    attn_low, dots = attn_grad(grad_branch, attn, stats2, stats3, gain_branch, after=(g_out,))

    def back(part, after):
        return attention_bwd(
            part, 2, query_rot, key_rot, value_low, attn_low, lse, dots, lo, hi, tables, move.slots, q_first, q_last, after
        )

    grad_first = back(0, (sum_down,))
    arriving = move.scatter(down_parts, (grad_first,))
    forwarded = move.forwarded
    g_first = tn(input_low, grad_first).astype(bf16)
    sum_first = lax.psum_scatter(g_first, "batch", scatter_dimension=0, tiled=True)
    g_out, _ = lax.optimization_barrier((g_out, sum_down))
    sum_out = lax.psum_scatter(g_out, "batch", scatter_dimension=0, tiled=True)
    grad_second = back(1, (g_first, sum_up, sum_out, *forwarded))
    up_rows = move.sent(move.picked(sum_up.reshape(ranks, d_rows, batches, strip), 0))
    out_rows = lax.ppermute(sum_out, EVERY, [(b, a) for a, b in order])
    bias_sums, sums_in, parts = input_back(
        (grad_first, grad_second),
        full_qkv,
        x_full,
        row_stats,
        move.groups,
        after=[terms[-1][0] for terms in arriving] + up_rows + [out_rows],
    )

    def finish(vectors, values, arrived):
        return (values[0] + (arrived + vectors[0]),)

    result = own_rows(
        finish, [shift_down], [resid], arriving, [(bf16, True)], after=(parts[0],), name="finish"
    )[0]
    out_up = jnp.moveaxis(move.ordered(up_rows), 0, 2).reshape(d_rows, batches * ranks * strip).astype(f32)
    first_rows = move.sent(move.picked(sum_first.reshape(ranks, d_rows, 3, cols // 2), 0))
    arriving = move.scatter(parts, (sum_first, result, out_up))
    grad_second, _ = lax.optimization_barrier((grad_second, parts))
    g_second = tn(input_low, grad_second).astype(bf16)
    sum_second = lax.psum_scatter(g_second, "batch", scatter_dimension=0, tiled=True)

    def end(vectors, values, arrived):
        normed, inverse = norm_parts(values[0].astype(f32))
        return (values[1] + norm_lower(normed, inverse, vectors[0], arrived),)

    def placed(value):
        return lax.dynamic_update_slice(jnp.zeros((value.shape[0], D), f32), value, (0, me * cols))

    branch_rows = placed(sums_branch[:2])
    vector_d = jnp.concatenate(
        [
            placed(bias_sums[0].reshape(3, cols)),
            sums_in[:1],
            branch_rows[:1],
            sums_mid[:1],
            sums_in[1:2],
            branch_rows[1:],
            sums_mid[1:4],
        ]
    )
    vector_f = sums_ff[:3].reshape(3, batches, 1, strip)
    vector_f = lax.dynamic_update_slice(jnp.zeros((3, batches, ranks, strip), f32), vector_f, (0, 0, me, 0))
    vector = jnp.concatenate(
        [
            vector_d.reshape(11, batches * ranks, d_rows).swapaxes(0, 1).reshape(batches * ranks, -1),
            vector_f.reshape(3, batches * ranks, strip).swapaxes(0, 1).reshape(batches * ranks, -1),
        ],
        axis=1,
    )
    vector = sum_small(vector, batches, ranks, [terms[-1][0] for terms in arriving])
    second_rows = move.picked(sum_second.reshape(ranks, d_rows, 3, cols // 2), 0)
    grad_total = own_rows(
        end, [gain_in], [x_own, grad_resid], arriving, [(f32, True)], after=second_rows, name="end"
    )[0]

    second_rows = move.sent(second_rows)
    halves = [jnp.moveaxis(move.ordered(r), 0, 2) for r in (first_rows, second_rows)]
    out_qkv = jnp.stack(halves, axis=3).reshape(d_rows, 3 * D).astype(f32)
    out_out = out_rows.astype(f32)
    out_down = sum_down.astype(f32)
    own_d = vector[:cut].reshape(11, d_rows)
    own_f = vector[cut:].reshape(3, strip)
    return (
        result.reshape(1, rows, D),
        grad_total.reshape(1, rows, D),
        out_qkv,
        own_d[:3],
        out_out,
        out_up,
        out_down,
        own_d[3:6],
        own_d[6:],
        own_f[0],
        own_f[1:],
    )


def solution(mesh):
    sizes = dict(mesh.shape)

    def run(*args):
        return local(*args, batches=sizes["batch"], ranks=sizes["seq"])

    return jax.shard_map(
        run,
        mesh=mesh,
        in_specs=(
            P("batch", "seq", None),
            P("batch", "seq", None),
            P(("batch", "seq"), None),
            P(None, ("batch", "seq")),
            P(("batch", "seq"), None),
            P(("batch", "seq"), None),
            P(("batch", "seq"), None),
            P(None, ("batch", "seq")),
            P(None, ("batch", "seq")),
            P(("batch", "seq")),
            P(None, ("batch", "seq")),
            P("batch"),
            P("batch", None),
            P("batch", None),
        ),
        out_specs=(
            P("batch", "seq", None),
            P("batch", "seq", None),
            P(("batch", "seq"), None),
            P(None, ("batch", "seq")),
            P(("batch", "seq"), None),
            P(("batch", "seq"), None),
            P(("batch", "seq"), None),
            P(None, ("batch", "seq")),
            P(None, ("batch", "seq")),
            P(("batch", "seq")),
            P(None, ("batch", "seq")),
        ),
        check_vma=False,
    )
```

```python
import jax
import jax.numpy as jnp
from jax import lax
from jax.experimental import pallas as pl
from jax.experimental.pallas import tpu as pltpu
from jax.sharding import PartitionSpec as P

D = 2048
HEADS = 32
HEAD_DIM = 64
SEQ_LEN = 2048
SPAN = 64
BLK = 256
NEG_FILL = -1e30
NORM_EPS = 1e-05
EVERY = ("batch", "seq")


def nt(a, b):
    return lax.dot_general(a, b, (((1,), (1,)), ((), ())), preferred_element_type=jnp.float32)


def tn(a, b):
    return lax.dot_general(a, b, (((0,), (0,)), ((), ())), preferred_element_type=jnp.float32)


def nn(a, b):
    return jnp.dot(a, b, preferred_element_type=jnp.float32)


TAKES = {
    "enter_attention": 12,
    "qkv_project": 19,
    "attention_forward": 41,
    "out_project": 14,
    "down_project": 200,
    "add_rows": 30,
    "ffn_grad": 24,
    "ffn_up": 33,
    "ffn_mid": 47,
    "branch_back": 150,
    "attn_grad": 38.0,
    "attention_backward": 200.0,
    "input_back": 112.0,
    "enter_ffn": 7,
    "leave_ffn": 100,
    "finish": 6,
    "end": 8,
}


def launch(body, grid, ins, outs, scratch=(), prefetch=(), after=(), name=None):
    n_pre, n_in, n_after = len(prefetch), len(ins), len(after)

    def kernel(*refs):
        body(*refs[: n_pre + n_in], *refs[n_pre + n_in + n_after :])

    return pl.pallas_call(
        kernel,
        out_shape=tuple(jax.ShapeDtypeStruct(s, d) for s, d, _ in outs),
        grid_spec=pltpu.PrefetchScalarGridSpec(
            num_scalar_prefetch=n_pre,
            grid=grid,
            in_specs=[b for _, b in ins] + [pl.BlockSpec(memory_space=pl.ANY)] * n_after,
            out_specs=[b for _, _, b in outs],
            scratch_shapes=list(scratch),
        ),
        compiler_params=pltpu.CompilerParams(vmem_limit_bytes=58 << 20),
        cost_estimate=pl.CostEstimate(flops=int(TAKES[name] * 1e9), bytes_accessed=int(TAKES[name] * 2e6), transcendentals=0),
        name=name,
    )(*prefetch, *(a for a, _ in ins), *after)


def tile(rows, cols):
    return pl.BlockSpec((rows, cols), lambda i, *_: (i, 0))


def fixed(array):
    zeros = (0,) * array.ndim
    return (array, pl.BlockSpec(array.shape, lambda *_: zeros, pipeline_mode=pl.Buffered(1)))


def arrivals(pieces, width):
    counts = [p.shape[0] // BLK for p in pieces]
    starts = [sum(counts[:a]) for a in range(len(counts))]
    inputs = []
    for piece, start, count in zip(pieces, starts, counts):
        if count == 1:
            inputs.append(fixed(piece))
        else:
            spec = pl.BlockSpec((BLK, width), lambda i, *_, s=start, c=count: (jnp.clip(i - s, 0, c - 1), 0))
            inputs.append((piece, spec))

    def read(refs, buffer):
        step = pl.program_id(0)
        for ref, start, count in zip(refs, starts, counts):

            @pl.when((step >= start) & (step < start + count))
            def _():
                buffer[...] = ref[...]

    return inputs, read


def departures(rows, width, groups):
    count = rows // BLK // groups
    outs = []
    for a in range(groups):
        spec = pl.BlockSpec((BLK, width), lambda i, *_, s=a * count: (jnp.clip(i - s, 0, count - 1), 0))
        outs.append(((rows // groups, width), jnp.bfloat16, spec))

    def write(refs, value):
        step = pl.program_id(0)
        for a, ref in enumerate(refs):

            @pl.when(step // count == a)
            def _():
                ref[...] = value

    return outs, write


def columns(lines):
    count, width = len(lines), lines[0].shape[1]
    pad = [jnp.zeros((8 - count, width), jnp.float32)] if count < 8 else []
    flat = jnp.concatenate(list(lines) + pad, axis=0).T
    return [flat[:, i : i + 1] for i in range(count)]


def joined(centers, squares, width):
    count = len(centers)
    center = sum(centers) * (1.0 / count)
    total = sum(squares) + width * sum((c - center) ** 2 for c in centers)
    return center, lax.rsqrt(total * (1.0 / (width * count)) + NORM_EPS)


def rotate(value, tables, sign):
    straight, from_right, from_left = tables
    turned = pltpu.roll(value, 127, 1) * from_right + pltpu.roll(value, 1, 1) * from_left
    return value * straight + turned if sign > 0 else value * straight - turned


def enter_attention(pieces, gain, shift):
    rows, wide = sum(p.shape[0] for p in pieces), pieces[0].shape[1]
    inputs, read = arrivals(pieces, wide)

    def body(g_ref, s_ref, *rest):
        piece_refs, (x_ref, low_ref, stat_ref) = rest[: len(pieces)], rest[len(pieces) :]
        read(piece_refs, x_ref)
        spread = x_ref[...].astype(jnp.float32)
        center = jnp.mean(spread, axis=-1, keepdims=True)
        spread = spread - center
        inverse = lax.rsqrt(jnp.mean(spread * spread, axis=-1, keepdims=True) + NORM_EPS)
        low_ref[...] = (spread * inverse * g_ref[...] + s_ref[...]).astype(jnp.bfloat16)
        lane = lax.broadcasted_iota(jnp.int32, (BLK, 128), 1)
        stat_ref[...] = jnp.where(lane == 0, center, inverse)

    return launch(
        body,
        (rows // BLK,),
        [fixed(gain), fixed(shift)] + inputs,
        [((rows, wide), jnp.bfloat16, tile(BLK, wide))] * 2 + [((rows, 128), jnp.float32, tile(BLK, 128))],
        name="enter_attention",
    )


def qkv_project(low, weight, bias, tables, after=()):
    rows, width = low.shape
    cols = weight.shape[1] // 3

    def body(low_ref, w_ref, b_ref, *rest):
        table_refs, outs = rest[:6], rest[6:]
        for part in range(3):
            span = slice(part * cols, (part + 1) * cols)
            value = nn(low_ref[...], w_ref[:, span]) + b_ref[:, span]
            if part == 2:
                outs[2][...] = value.astype(jnp.bfloat16)
                continue
            own = [t[...] for t in table_refs[3 * part : 3 * part + 3]]
            for at in range(0, cols, 128):
                outs[part][:, at : at + 128] = rotate(value[:, at : at + 128], own, 1).astype(jnp.bfloat16)

    return launch(
        body,
        (rows // BLK,),
        [(low, tile(BLK, width)), fixed(weight), fixed(bias)] + [(t, tile(BLK, 128)) for t in tables],
        [((rows, cols), jnp.bfloat16, tile(BLK, cols))] * 3,
        after=after,
        name="qkv_project",
    )


def attention_fwd(q, k, v, lo, hi, slots, first, last, after=()):
    rows, width = q.shape
    blocks = rows // BLK
    heads = width // HEAD_DIM
    extra = 16

    def body(slots, first, last, q_ref, k_ref, v_ref, lo_ref, hi_ref, o_ref, lse_ref, stat_ref, vt, acc, qt, kept):
        step = pl.program_id(0)

        @pl.when(step == 0)
        def _():
            for i in range(blocks):
                at = slice(i * BLK, (i + 1) * BLK)
                flat = v_ref[at, :].T
                for h in range(heads):
                    vt[h, :HEAD_DIM, at] = flat[h * HEAD_DIM : (h + 1) * HEAD_DIM]
                    vt[h, HEAD_DIM:, at] = jnp.ones((extra, BLK), jnp.bfloat16)

        flat = (q_ref[...] * jnp.bfloat16(HEAD_DIM**-0.5)).T
        zero = jnp.zeros((HEAD_DIM, BLK), jnp.bfloat16)
        for h in range(heads):
            mine = flat[h * HEAD_DIM : (h + 1) * HEAD_DIM, :]
            qt[h] = jnp.concatenate([mine, zero] if h % 2 == 0 else [zero, mine], axis=0)
        low, high = lo_ref[...], hi_ref[...]
        key_row = lax.broadcasted_iota(jnp.int32, (BLK, BLK), 0)

        def scores(kb, peaks):
            at = pl.ds(pl.multiple_of(slots[kb] * BLK, BLK), BLK)
            spot = key_row + kb * BLK
            seen = (spot >= low) & (spot <= high)
            out = []
            for h in range(heads):
                two = slice(h // 2 * 128, h // 2 * 128 + 128)
                s = jnp.where(seen, nn(k_ref[at, two], qt[h]), NEG_FILL)
                kept[kb, h] = s
                out.append(jnp.maximum(peaks[h], jnp.max(s, axis=0, keepdims=True)))
            return tuple(out)

        start = tuple(jnp.full((1, BLK), NEG_FILL, jnp.float32) for _ in range(heads))
        peaks = lax.fori_loop(first[step], last[step], scores, start)
        acc[...] = jnp.zeros_like(acc)

        def weigh(kb, _):
            at = pl.ds(pl.multiple_of(slots[kb] * BLK, BLK), BLK)
            for h in range(heads):
                p = jnp.exp(kept[kb, h] - peaks[h]).astype(jnp.bfloat16)
                acc[h] += nn(vt[h, :, at], p)
            return 0

        lax.fori_loop(first[step], last[step], weigh, 0)
        parts = []
        for h in range(heads):
            total = acc[h, HEAD_DIM : HEAD_DIM + 1, :]
            lse_ref[h : h + 1, :] = peaks[h] + jnp.log(total)
            parts.append(acc[h, :HEAD_DIM] / total)
        flat = jnp.concatenate(parts, axis=0)
        center = jnp.mean(flat, axis=0, keepdims=True)
        stat_ref[0:1, :] = center
        stat_ref[1:2, :] = jnp.sum((flat - center) ** 2, axis=0, keepdims=True)
        stat_ref[2:8, :] = jnp.zeros((6, BLK), jnp.float32)
        o_ref[...] = flat.T

    by_slot = pl.BlockSpec((BLK, width), lambda i, s, *_: (s[i], 0))
    line = pl.BlockSpec((1, BLK), lambda i, *_: (0, i))
    return launch(
        body,
        (blocks,),
        [(q, by_slot), fixed(k), fixed(v), (lo, line), (hi, line)],
        [
            ((rows, width), jnp.float32, by_slot),
            ((heads, rows), jnp.float32, pl.BlockSpec((heads, BLK), lambda i, s, *_: (0, s[i]))),
            ((8, rows), jnp.float32, pl.BlockSpec((8, BLK), lambda i, s, *_: (0, s[i]))),
        ],
        scratch=[
            pltpu.VMEM((heads, HEAD_DIM + extra, rows), jnp.bfloat16),
            pltpu.VMEM((heads, HEAD_DIM + extra, BLK), jnp.float32),
            pltpu.VMEM((heads, 128, BLK), jnp.bfloat16),
            pltpu.VMEM((blocks, heads, BLK, BLK), jnp.float32),
        ],
        prefetch=(slots, first, last),
        after=after,
        name="attention_forward",
    )


def out_project(attn, stats, gain, shift, weight, groups, after=()):
    rows, width = attn.shape
    wide = weight.shape[1]
    outs, write = departures(rows, wide, groups)

    def body(a_ref, g_ref, s_ref, w_ref, *rest):
        stat_refs, (low_ref, *part_refs) = rest[: len(stats)], rest[len(stats) :]
        center, inverse = columns(joined([r[0:1] for r in stat_refs], [r[1:2] for r in stat_refs], width))
        low = ((a_ref[...] - center) * inverse * g_ref[...] + s_ref[...]).astype(jnp.bfloat16)
        low_ref[...] = low
        write(part_refs, nn(low, w_ref[...]).astype(jnp.bfloat16))

    low, *parts = launch(
        body,
        (rows // BLK,),
        [(attn, tile(BLK, width)), fixed(gain), fixed(shift), fixed(weight)] + list(stats),
        [((rows, width), jnp.bfloat16, tile(BLK, width))] + outs,
        after=after,
        name="out_project",
    )
    return low, parts


def down_project(low, weight, groups, after=()):
    rows, width = low.shape
    wide = weight.shape[1]
    outs, write = departures(rows, wide, groups)

    def body(l_ref, w_ref, *part_refs):
        write(part_refs, nn(l_ref[...], w_ref[...]).astype(jnp.bfloat16))

    return launch(
        body,
        (rows // BLK,),
        [(low, tile(BLK, width)), fixed(weight)],
        outs,
        after=after,
        name="down_project",
    )


def add_rows(pairs, after=()):
    wide = pairs[0][0].shape[1]
    half = pairs[0][0].shape[0] // 2
    piece = min(128, half)

    def body(*refs):
        ins, outs = refs[: 2 * len(pairs)], refs[2 * len(pairs) :]
        for i, ref in enumerate(outs):
            ref[...] = (ins[2 * i][...].astype(jnp.float32) + ins[2 * i + 1][...].astype(jnp.float32)).astype(jnp.bfloat16)

    spec = pl.BlockSpec((piece, wide), lambda i: (half // piece + i, 0))
    return launch(
        body,
        (half // piece,),
        [(x, spec) for pair in pairs for x in pair],
        [((half, wide), jnp.bfloat16, tile(piece, wide))] * len(pairs),
        after=after,
        name="add_rows",
    )


def own_rows(body, wholes, rows_in, terms, outs, sums=0, after=(), name=None):
    half, wide = rows_in[0][0].shape
    piece = min(128, half)
    count = len(terms[0])

    def kernel(*refs):
        whole_refs, refs = refs[: len(wholes)], refs[len(wholes) :]
        row_refs, refs = refs[: 2 * len(rows_in)], refs[2 * len(rows_in) :]
        term_refs, out_refs = refs[: 2 * count], list(refs[2 * count :])
        targets = []
        for _, stacked in outs:
            if stacked:
                ref = out_refs.pop(0)
                targets.append((ref.at[0], ref.at[1]))
            else:
                targets.append((out_refs.pop(0), out_refs.pop(0)))
        vectors = [r[...] for r in whole_refs]
        added = [0.0] * sums
        for side in range(2):
            total = term_refs[side * count][...].astype(jnp.float32)
            for r in term_refs[side * count + 1 : (side + 1) * count]:
                total = total + r[...].astype(jnp.float32)
            values = body(vectors, [r[...] for r in row_refs[side::2]], total)
            for target, value in zip(targets, values[: len(outs)]):
                target[side][...] = value.astype(target[side].dtype)
            added = [a + jnp.sum(v, axis=0, keepdims=True) for a, v in zip(added, values[len(outs) :])]
        if sums:
            sum_ref = out_refs[0]

            @pl.when(pl.program_id(0) == 0)
            def _():
                sum_ref[...] = jnp.zeros_like(sum_ref)

            for i, a in enumerate(added):
                sum_ref[i : i + 1, :] += a

    pieces = []
    for side in range(2):
        for array, start in terms[side]:
            pieces.append((array, pl.BlockSpec((piece, wide), lambda i, at=start // piece: (at + i, 0))))
    results = []
    for d, stacked in outs:
        if stacked:
            results.append(((2, half, wide), d, pl.BlockSpec((2, piece, wide), lambda i: (0, i, 0))))
        else:
            results += [((half, wide), d, tile(piece, wide))] * 2
    if sums:
        results.append(((8, wide), jnp.float32, pl.BlockSpec((8, wide), lambda i: (0, 0))))
    return launch(
        kernel,
        (half // piece,),
        [fixed(w) for w in wholes] + [(r, tile(piece, wide)) for pair in rows_in for r in pair] + pieces,
        results,
        after=after,
        name=name,
    )


def norm_parts(values):
    center = jnp.mean(values, axis=-1, keepdims=True)
    spread = values - center
    inverse = lax.rsqrt(jnp.mean(spread * spread, axis=-1, keepdims=True) + NORM_EPS)
    return spread * inverse, inverse


def norm_lower(normed, inverse, gain, upper):
    scaled = upper * gain
    first_mean = jnp.mean(scaled, axis=-1, keepdims=True)
    second_mean = jnp.mean(scaled * normed, axis=-1, keepdims=True)
    return inverse * (scaled - first_mean - normed * second_mean)


GELU_A = 0.044715
GELU_C = 0.7978845608028654


def ffn_grad(cot, w_down, gain):
    rows, wide = cot.shape
    units = w_down.shape[0]
    chunk = min(512, units)

    def body(c_ref, d_w, g_ref, grad_ref, stat_ref, sum_ref):
        @pl.when(pl.program_id(0) == 0)
        def _():
            sum_ref[...] = jnp.zeros_like(sum_ref)

        total = 0.0
        for at in range(0, units, chunk):
            span = slice(at, at + chunk)
            grad = nt(c_ref[...], d_w[span, :])
            scaled = grad * g_ref[:, span]
            grad_ref[:, span] = scaled
            sum_ref[0:1, span] += jnp.sum(grad, axis=0, keepdims=True)
            total = total + jnp.sum(scaled, axis=1, keepdims=True)
        lane = lax.broadcasted_iota(jnp.int32, (BLK, 128), 1)
        stat_ref[...] = jnp.where(lane == 0, total, 0.0).T[0:8, :]

    return launch(
        body,
        (rows // BLK,),
        [(cot, tile(BLK, wide)), fixed(w_down), fixed(gain)],
        [
            ((rows, units), jnp.float32, tile(BLK, units)),
            ((8, rows), jnp.float32, pl.BlockSpec((8, BLK), lambda i, *_: (0, i))),
            ((8, units), jnp.float32, pl.BlockSpec((8, units), lambda i, *_: (0, 0))),
        ],
        name="ffn_grad",
    )


def ffn_up(pieces, grad, grad_sums, w_up, bias):
    rows, units = grad.shape
    wide = w_up.shape[0]
    inputs, read = arrivals(pieces, wide)
    chunk = min(512, units)
    share = 1.0 / chunk

    def body(f_ref, t_ref, u_w, b_ref, *rest):
        m_ref, up_ref, stat_ref = rest[len(pieces) :]
        read(rest[: len(pieces)], m_ref)
        parts = []

        def figures(at, up):
            span = slice(at, at + chunk)
            gel = 0.5 * up * (1.0 + jnp.tanh(GELU_C * up * (1.0 + GELU_A * up * up)))
            center = jnp.sum(gel, axis=1, keepdims=True) * share
            spread = gel - center
            scaled = f_ref[:, span]
            parts.append(
                (
                    center,
                    jnp.sum(spread * spread, axis=1, keepdims=True),
                    jnp.sum(scaled * spread, axis=1, keepdims=True),
                    jnp.sum(scaled, axis=1, keepdims=True),
                )
            )

        last = None
        for at in range(0, units, chunk):
            span = slice(at, at + chunk)
            up = nn(m_ref[...], u_w[:, span]) + b_ref[:, span]
            up_ref[:, span] = up
            if last is not None:
                figures(*last)
            last = at, up
        figures(*last)
        center = sum(p[0] for p in parts) * (1.0 / len(parts))
        square = sum(p[1] + chunk * (p[0] - center) ** 2 for p in parts)
        product = sum(p[2] + (p[0] - center) * p[3] for p in parts)
        lane = lax.broadcasted_iota(jnp.int32, (BLK, 128), 1)
        flat = jnp.zeros((BLK, 128), jnp.float32)
        for i, value in enumerate((center, square, product)):
            flat = jnp.where(lane == i, value, flat)
        flat = flat.T
        stat_ref[...] = jnp.concatenate([flat[0:2], t_ref[0:1, :], flat[2:7]], axis=0)

    return launch(
        body,
        (rows // BLK,),
        [
            (grad, tile(BLK, units)),
            (grad_sums, pl.BlockSpec((8, BLK), lambda i, *_: (0, i))),
            fixed(w_up),
            fixed(bias),
        ]
        + inputs,
        [
            ((rows, wide), jnp.bfloat16, tile(BLK, wide)),
            ((rows, units), jnp.float32, tile(BLK, units)),
            ((8, rows), jnp.float32, pl.BlockSpec((8, BLK), lambda i, *_: (0, i))),
        ],
        name="ffn_up",
    )


def ffn_mid(up, grad, stats, gain, shift, w_up, groups):
    rows, units = up.shape
    wide = w_up.shape[0]
    chunk = min(512, units)
    ranks = len(stats)
    outs, write = departures(rows, wide, groups)

    def body(u_ref, f_ref, g_ref, s_ref, w_ref, *rest):
        stat_refs, (low_ref, gup_ref, sum_ref, *part_refs) = rest[:ranks], rest[ranks:]
        centers = [r[0:1] for r in stat_refs]
        center, inverse = joined(centers, [r[1:2] for r in stat_refs], units)
        share = 1.0 / (units * ranks)
        first = sum(r[2:3] for r in stat_refs) * share
        second = inverse * share * sum(r[3:4] + (c - center) * r[2:3] for r, c in zip(stat_refs, centers))
        center, inverse, first, second = columns([center, inverse, first, second])

        @pl.when(pl.program_id(0) == 0)
        def _():
            sum_ref[...] = jnp.zeros_like(sum_ref)

        for at in range(0, units, chunk):
            span = slice(at, at + chunk)
            u, f = u_ref[:, span], f_ref[:, span]
            squared = u * u
            t = jnp.tanh(GELU_C * u * (1.0 + GELU_A * squared))
            one = 0.5 * (1.0 + t)
            slope = one + 0.5 * u * (1.0 - t * t) * (GELU_C * (1.0 + 3.0 * GELU_A * squared))
            normed = (u * one - center) * inverse
            low_ref[:, span] = (normed * g_ref[:, span] + s_ref[:, span]).astype(jnp.bfloat16)
            lower = inverse * (f - first - normed * second)
            gup = (lower * slope).astype(jnp.bfloat16)
            gup_ref[:, span] = gup
            sum_ref[0:1, span] += jnp.sum(f * normed, axis=0, keepdims=True)
            sum_ref[1:2, span] += jnp.sum(gup.astype(jnp.float32), axis=0, keepdims=True)
        write(part_refs, nt(gup_ref[...], w_ref[...]).astype(jnp.bfloat16))

    low, gup, sums, *parts = launch(
        body,
        (rows // BLK,),
        [(up, tile(BLK, units)), (grad, tile(BLK, units)), fixed(gain), fixed(shift), fixed(w_up)] + list(stats),
        [
            ((rows, units), jnp.bfloat16, tile(BLK, units)),
            ((rows, units), jnp.bfloat16, tile(BLK, units)),
            ((8, units), jnp.float32, pl.BlockSpec((8, units), lambda i, *_: (0, 0))),
        ]
        + outs,
        name="ffn_mid",
    )
    return low, gup, sums, parts


def branch_back(pieces, w_out, attn, stats, gain, after=()):
    rows, width = attn.shape
    wide = w_out.shape[1]
    ranks = len(stats)
    inputs, read = arrivals(pieces, wide)

    def body(w_ref, a_ref, g_ref, *rest):
        stat_refs, rest = rest[:ranks], rest[ranks:]
        r_ref, grad_ref, stat_ref, sum_ref = rest[len(pieces) :]
        read(rest[: len(pieces)], r_ref)
        center, inverse = columns(joined([r[0:1] for r in stat_refs], [r[1:2] for r in stat_refs], width))

        @pl.when(pl.program_id(0) == 0)
        def _():
            sum_ref[...] = jnp.zeros_like(sum_ref)

        grad = nt(r_ref[...], w_ref[...])
        grad_ref[...] = grad
        normed = (a_ref[...] - center) * inverse
        scaled = grad * g_ref[...]
        sum_ref[0:1, :] += jnp.sum(grad * normed, axis=0, keepdims=True)
        sum_ref[1:2, :] += jnp.sum(grad, axis=0, keepdims=True)
        lane = lax.broadcasted_iota(jnp.int32, (BLK, 128), 1)
        flat = jnp.where(lane == 0, jnp.sum(scaled, axis=1, keepdims=True), 0.0)
        flat = jnp.where(lane == 1, jnp.sum(scaled * normed, axis=1, keepdims=True), flat)
        stat_ref[...] = flat.T[0:8, :]

    return launch(
        body,
        (rows // BLK,),
        [fixed(w_out), (attn, tile(BLK, width)), fixed(gain)] + list(stats) + inputs,
        [
            ((rows, wide), jnp.bfloat16, tile(BLK, wide)),
            ((rows, width), jnp.float32, tile(BLK, width)),
            ((8, rows), jnp.float32, pl.BlockSpec((8, BLK), lambda i, *_: (0, i))),
            ((8, width), jnp.float32, pl.BlockSpec((8, width), lambda i, *_: (0, 0))),
        ],
        after=after,
        name="branch_back",
    )


def attn_grad(grad, attn, stats, sums, gain, after=()):
    rows, width = attn.shape
    ranks = len(stats)
    heads = width // HEAD_DIM

    def body(f_ref, a_ref, g_ref, *rest):
        stat_refs, sum_refs = rest[:ranks], rest[ranks : 2 * ranks]
        out_ref, dot_ref = rest[2 * ranks :]
        center, inverse = joined([r[0:1] for r in stat_refs], [r[1:2] for r in stat_refs], width)
        share = 1.0 / (width * ranks)
        first = sum(r[0:1] for r in sum_refs) * share
        second = sum(r[1:2] for r in sum_refs) * share
        center, inverse, first, second = columns([center, inverse, first, second])
        attn_here = a_ref[...]
        normed = (attn_here - center) * inverse
        out = (inverse * (f_ref[...] * g_ref[...] - first - normed * second)).astype(jnp.bfloat16)
        out_ref[...] = out
        product = (out.astype(jnp.float32) * attn_here).T
        for h in range(heads):
            dot_ref[h : h + 1, :] = jnp.sum(product[h * HEAD_DIM : (h + 1) * HEAD_DIM], axis=0, keepdims=True)

    return launch(
        body,
        (rows // BLK,),
        [(grad, tile(BLK, width)), (attn, tile(BLK, width)), fixed(gain)] + list(stats) + list(sums),
        [
            ((rows, width), jnp.bfloat16, tile(BLK, width)),
            ((heads, rows), jnp.float32, pl.BlockSpec((heads, BLK), lambda i, *_: (0, i))),
        ],
        after=after,
        name="attn_grad",
    )


def attention_bwd(part, parts, q, k, v, g, lse, dot, lo, hi, tables, slots, first, last, after=()):
    rows, width = q.shape
    width //= parts
    blocks = rows // BLK
    heads = width // HEAD_DIM
    base = part * heads
    scale = HEAD_DIM**-0.5
    own_columns = pl.BlockSpec((rows, width), lambda *_: (0, part), pipeline_mode=pl.Buffered(1))

    def body(slots, first, last, q_ref, k_ref, v_ref, g_ref, lse_ref, dot_ref, lo_ref, hi_ref, *rest):
        table_refs, (out_ref, dqt, qt, gt, accs) = rest[:6], rest[6:]
        key_row = lax.broadcasted_iota(jnp.int32, (BLK, BLK), 0)
        lane = lax.broadcasted_iota(jnp.int32, (BLK, 128), 1)
        zero = jnp.zeros((), jnp.bfloat16)
        dqt[...] = jnp.zeros_like(dqt)
        for i in range(blocks):
            at = slice(i * BLK, (i + 1) * BLK)
            qt[:, at] = q_ref[at, :].T
            gt[:, at] = g_ref[at, :].T

        def outer(kb, _):
            rows_k = pl.ds(pl.multiple_of(slots[kb] * BLK, BLK), BLK)
            k, v = k_ref[rows_k, :] * jnp.bfloat16(scale), v_ref[rows_k, :]
            kts = k.T
            spot = key_row + kb * BLK

            def halves(x, h):
                x = x[:, h // 2 * 128 : h // 2 * 128 + 128]
                return jnp.where((lane < HEAD_DIM) == (h % 2 == 0), x, zero)

            ks = [halves(k, h) for h in range(heads)]
            vs = [halves(v, h) for h in range(heads)]
            accs[...] = jnp.zeros_like(accs)

            def inner(qb, _):
                at = pl.ds(pl.multiple_of(slots[qb] * BLK, BLK), BLK)
                here = pl.ds(pl.multiple_of(qb * BLK, BLK), BLK)
                seen = (spot >= lo_ref[0:1, here]) & (spot <= hi_ref[0:1, here])
                def products(h):
                    two = slice(h // 2 * 128, h // 2 * 128 + 128)
                    return nn(ks[h], qt[two, at]), nn(vs[h], gt[two, at])

                def factors(h, s, dp):
                    p = jnp.where(seen, jnp.exp(s - lse_ref[base + h : base + h + 1, at]), 0.0)
                    ds = (p * (dp - dot_ref[base + h : base + h + 1, at])).astype(jnp.bfloat16)
                    return p.astype(jnp.bfloat16), ds

                def add(h, p, ds):
                    two = slice(h // 2 * 128, h // 2 * 128 + 128)
                    span = slice(h * HEAD_DIM, (h + 1) * HEAD_DIM)
                    accs[1, h] += nn(p, g_ref[at, two])
                    accs[0, h] += nn(ds, q_ref[at, two])
                    dqt[span, at] += nn(kts[span, :], ds)

                made, ready = {}, {}
                for h in range(heads + 2):
                    if h < heads:
                        made[h] = products(h)
                    if 0 <= h - 1 < heads:
                        ready[h - 1] = factors(h - 1, *made[h - 1])
                    if 0 <= h - 2 < heads:
                        add(h - 2, *ready[h - 2])
                return 0

            lax.fori_loop(first[kb], last[kb], inner, 0)
            own = [t[rows_k, :] for t in table_refs[3:]]
            for h in range(0, heads, 2):
                at = h * HEAD_DIM
                grad_k = jnp.where(lane < HEAD_DIM, accs[0, h], accs[0, h + 1]) * scale
                grad_v = jnp.where(lane < HEAD_DIM, accs[1, h], accs[1, h + 1])
                out_ref[rows_k, width + at : width + at + 128] = rotate(grad_k, own, -1).astype(jnp.bfloat16)
                out_ref[rows_k, 2 * width + at : 2 * width + at + 128] = grad_v.astype(jnp.bfloat16)
            return 0

        lax.fori_loop(0, blocks, outer, 0)
        for i in range(blocks):
            at = slice(i * BLK, (i + 1) * BLK)
            grad_q = dqt[:, at].T
            own = [t[at, :] for t in table_refs[:3]]
            for col in range(0, width, 128):
                out_ref[at, col : col + 128] = rotate(grad_q[:, col : col + 128], own, -1).astype(jnp.bfloat16)

    return launch(
        body,
        (1,),
        [(a, own_columns) for a in (q, k, v, g)] + [fixed(a) for a in (lse, dot, lo, hi, *tables)],
        [((rows, 3 * width), jnp.bfloat16, pl.BlockSpec((rows, 3 * width), lambda *_: (0, 0), pipeline_mode=pl.Buffered(1)))],
        scratch=[
            pltpu.VMEM((width, rows), jnp.float32),
            pltpu.VMEM((width, rows), jnp.bfloat16),
            pltpu.VMEM((width, rows), jnp.bfloat16),
            pltpu.VMEM((2, heads, BLK, 128), jnp.float32),
        ],
        prefetch=(slots, first, last),
        after=after,
        name="attention_backward",
    )[0]


def input_back(grads, weight, x, row_stats, groups, after=()):
    rows, wide = x.shape
    cols = weight.shape[1]
    parts = len(grads)
    small = cols // parts // 3
    outs, write = departures(rows, wide, groups)

    def body(w_ref, x_ref, stat_ref, *rest):
        grad_refs, (bias_ref, sum_ref, *part_refs), g_ref = rest[:parts], rest[parts:-1], rest[-1]

        @pl.when(pl.program_id(0) == 0)
        def _():
            sum_ref[...] = jnp.zeros_like(sum_ref)
            bias_ref[...] = jnp.zeros_like(bias_ref)

        for p, ref in enumerate(grad_refs):
            for j in range(3):
                at = (j * parts + p) * small
                g_ref[:, at : at + small] = ref[:, j * small : (j + 1) * small]
        value = nt(g_ref[...], w_ref[...])
        write(part_refs, value.astype(jnp.bfloat16))
        bias_ref[0:1, :] += jnp.sum(g_ref[...].astype(jnp.float32), axis=0, keepdims=True)
        normed = (x_ref[...].astype(jnp.float32) - stat_ref[:, 0:1]) * stat_ref[:, 1:2]
        sum_ref[0:1, :] += jnp.sum(value * normed, axis=0, keepdims=True)
        sum_ref[1:2, :] += jnp.sum(value, axis=0, keepdims=True)

    bias_sums, sums, *parts_out = launch(
        body,
        (rows // BLK,),
        [fixed(weight), (x, tile(BLK, wide)), (row_stats, tile(BLK, 128))]
        + [(g, tile(BLK, cols // parts)) for g in grads],
        [
            ((8, cols), jnp.float32, pl.BlockSpec((8, cols), lambda i, *_: (0, 0))),
            ((8, wide), jnp.float32, pl.BlockSpec((8, wide), lambda i, *_: (0, 0))),
        ]
        + outs,
        scratch=[pltpu.VMEM((BLK, cols), jnp.bfloat16)],
        after=after,
        name="input_back",
    )
    return bias_sums, sums, parts_out


def key_limits(bounds, spans, kind, total):
    places = jnp.arange(total, dtype=jnp.int32)
    below = bounds[:, None] <= places[None, :]
    doc_first = jnp.max(jnp.where(below, bounds[:, None], 0), axis=0)
    doc_last = jnp.min(jnp.where(below, total, bounds[:, None]), axis=0) - 1
    doc_last = jnp.minimum(doc_last, total - 1)
    inside = (spans[:, None] <= places[None, :]) & (places[None, :] < spans[:, None] + SPAN) & (kind > 0)
    span_last = jnp.max(jnp.where(inside, spans[:, None] + SPAN - 1, 0), axis=0)
    span_first = jnp.min(jnp.where(inside, spans[:, None], total), axis=0)
    hi = jnp.minimum(jnp.maximum(places, span_last), doc_last)
    q_first = jnp.maximum(jnp.minimum(places, span_first), doc_first)
    return doc_first, hi, q_first, doc_last


def block_limits(lo, hi, qf, ql):
    low = lo.reshape(-1, BLK)[:, 0] // BLK
    high = hi.reshape(-1, BLK)[:, -1] // BLK + 1
    qlow = qf.reshape(-1, BLK)[:, 0] // BLK
    qhigh = ql.reshape(-1, BLK)[:, -1] // BLK + 1
    return low, high, qlow, qhigh


class Exchange:
    def __init__(self, ranks, batches, rows, me):
        self.ranks, self.batches, self.rows, self.me = ranks, batches, rows, me
        self.square = ranks == 4 and rows == 2 * BLK
        self.half = rows // 2
        self.groups = 4 if self.square else 1
        self.forwarded = ()
        self.order = ((0, 1, 2, 3), (0, 2, 1, 3))
        total = ranks * rows
        block = jnp.arange(total // BLK, dtype=jnp.int32)
        if self.square:
            owner, part = block // 2, block % 2
            near = owner ^ me
            swapped = (near >> 1) | ((near & 1) << 1)
            self.slots = (part * 4 + jnp.where(part == 0, near, swapped)).astype(jnp.int32)
            owners = jnp.stack([me ^ r for half in self.order for r in half])
            firsts = owners * rows + jnp.repeat(jnp.arange(2), 4) * self.half
            self.places = (firsts[:, None] + jnp.arange(self.half)[None, :]).reshape(total).astype(jnp.int32)
        else:
            self.slots = block
            self.places = jnp.arange(total, dtype=jnp.int32)

    def swap(self, value, bit):
        return lax.ppermute(value, "seq", [(r, r ^ bit) for r in range(self.ranks)])

    def gather(self, upper, lower, late=None):
        if not self.square:
            return [lax.all_gather(jnp.concatenate([upper, lower], axis=0), "seq", axis=0, tiled=True)]
        near_upper, near_lower = self.swap(upper, 1), self.swap(lower, 2)
        again = (upper, lower, near_upper, near_lower)
        if late is not None:
            again, _ = lax.optimization_barrier((again, late))
        return [upper, near_upper, self.swap(again[0], 2), self.swap(again[2], 2)] + [
            lower,
            near_lower,
            self.swap(again[1], 1),
            self.swap(again[3], 1),
        ]

    def scatter(self, parts, after=()):
        if not self.square:
            own = lax.psum_scatter(parts[0], "seq", scatter_dimension=0, tiled=True)
            return [[(own, 0)], [(own, self.half)]]
        keep_upper, send_upper, keep_lower, send_lower = parts
        near_upper, near_lower = self.swap(send_upper, 2), self.swap(send_lower, 1)
        far_upper, far_lower = add_rows([(keep_upper, near_upper), (keep_lower, near_lower)], after)
        sums = (far_upper, far_lower)
        far_upper, far_lower = self.swap(far_upper, 1), self.swap(far_lower, 2)
        self.forwarded = sums
        return [[(keep_upper, 0), (near_upper, 0), (far_upper, 0)], [(keep_lower, 0), (near_lower, 0), (far_lower, 0)]]

    def picked(self, value, axis):
        if not self.square:
            return [jnp.moveaxis(value, axis, 0)]
        return [lax.dynamic_index_in_dim(value, self.me ^ r, axis, False) for r in range(self.ranks)]

    def sent(self, pieces):
        if not self.square:
            return [lax.all_to_all(pieces[0], "seq", 0, 0)]
        return [pieces[0]] + [self.swap(pieces[r], r) for r in range(1, self.ranks)]

    def ordered(self, pieces):
        return flipped(jnp.stack(pieces), self.me, 2) if self.square else pieces[0]

    def spread(self, value):
        lines = value.shape[0]
        if not self.square:
            every = lax.all_gather(value, "seq", axis=0)
            return [(every[r], pl.BlockSpec((lines, BLK), lambda i, *_: (0, i))) for r in range(self.ranks)]
        out = [(value, pl.BlockSpec((lines, BLK), lambda i, *_: (0, i)))]
        for bit, other in ((1, 2), (2, 1), (3, 3)):
            spec = pl.BlockSpec(
                (lines, BLK), lambda i, *_, a=bit, b=other: (0, (i // 4) * 4 + ((i % 4) ^ (a + (i // 4) * (b - a))))
            )
            out.append((self.swap(value, bit), spec))
        return out


def flipped(value, device, bits):
    shape = value.shape
    for bit in range(bits):
        two = value.reshape((-1, 2, 1 << bit) + shape[1:])
        value = jnp.where((device >> bit) & 1, two[:, ::-1], two).reshape(shape)
    return value


def share_small(value, batches, ranks):
    if (batches, ranks) != (8, 4):
        return lax.all_gather(value, EVERY, axis=0)
    batch, me = lax.axis_index("batch"), lax.axis_index("seq")
    parts = value[None]
    for axis, count, steps in (("seq", ranks, (1, 2, 3)), ("batch", batches, (1,)), ("batch", batches, (2, 4, 6))):
        parts = jnp.concatenate(
            [parts] + [lax.ppermute(parts, axis, [(r, r ^ s) for r in range(count)]) for s in steps], axis=0
        )
    return flipped(parts, batch * ranks + me, 5)


def sum_small(value, batches, ranks, late):
    if (batches, ranks) != (8, 4):
        return lax.psum_scatter(value, EVERY, scatter_dimension=0, tiled=True)[0]
    batch, me = lax.axis_index("batch"), lax.axis_index("seq")
    value = flipped(value, batch * ranks + me, 5)
    for axis, count, steps, left in (("batch", batches, (2, 4, 6), 8), ("batch", batches, (1,), 4), ("seq", ranks, (1, 2, 3), 1)):
        if axis == "seq":
            value, _ = lax.optimization_barrier((value, late))
        total = value[:left]
        for i, s in enumerate(steps):
            at = (i + 1) * left
            total = total + lax.ppermute(value[at : at + left], axis, [(r, r ^ s) for r in range(count)])
        value = total
    return value[0]


def rot_tables(places):
    column = jnp.arange(128) % HEAD_DIM
    pair_idx = (column // 2).astype(jnp.float32)
    frequency = jnp.power(10000.0, -2.0 * pair_idx / HEAD_DIM)
    place_float = places.astype(jnp.float32)
    angles = place_float[:, None] * frequency[None, :]
    zeta_base = (2.0 * pair_idx + 0.4 * HEAD_DIM) / (1.4 * HEAD_DIM)
    exponent = (place_float - SEQ_LEN // 2) / 512.0
    scales = jnp.power(zeta_base[None, :], exponent[:, None])
    cosine, sine = jnp.cos(angles), jnp.sin(angles)
    even = (column % 2 == 0)[None, :]
    right, left = jnp.where(even, -sine, 0.0), jnp.where(even, 0.0, sine)
    return tuple(t * s for s in (scales, 1.0 / scales) for t in (cosine, right, left))


def local(
    layer_input,
    cotangent,
    w_qkv,
    bias_qkv,
    w_out,
    w_up,
    w_down,
    gains_d,
    biases_d,
    gain_ff,
    biases_ff,
    data_type,
    doc_bounds,
    span_starts,
    *,
    batches,
    ranks,
):
    me = lax.axis_index("seq")
    rows = layer_input.shape[1]
    half = rows // 2
    move = Exchange(ranks, batches, rows, me)
    tokens = rows * ranks
    cols = D // ranks
    strip, d_rows = w_down.shape[0], w_up.shape[0]
    units = strip * batches
    f32, bf16 = jnp.float32, jnp.bfloat16
    x_own = [layer_input.reshape(2, half, D)[i] for i in range(2)]
    cot_own = [cotangent.reshape(2, half, D)[i] for i in range(2)]

    x_pieces = move.gather(*x_own, late=())
    small = jnp.concatenate(
        [bias_qkv.reshape(-1), gains_d.reshape(-1), biases_d.reshape(-1), gain_ff, biases_ff.reshape(-1)]
    )

    small = share_small(small, batches, ranks)

    w_qkv, _ = lax.optimization_barrier((w_qkv, x_own))
    part_qkv = move.ordered(move.sent(move.picked(w_qkv.reshape(d_rows, 3, ranks, cols), 2)))
    up_pieces = move.picked(w_up.reshape(d_rows, batches, ranks, strip), 2)
    order = [(i, (i % batches) * ranks + i // batches) for i in range(batches * ranks)]
    part_out = lax.ppermute(w_out, EVERY, order)
    tables = rot_tables(move.places)
    early = (small, part_out, up_pieces, tables, x_pieces[1:2] + x_pieces[5:6])
    part_qkv, (small, part_out, up_pieces, tables, _) = lax.optimization_barrier((part_qkv, early))
    full_qkv = lax.all_gather(part_qkv.reshape(d_rows * ranks, 3 * cols), "batch", axis=0, tiled=True)
    cut = 11 * d_rows
    rows_d = small[:, :cut].reshape(-1, 11, d_rows).swapaxes(0, 1).reshape(11, D).astype(f32)
    rows_f = small[:, cut:].reshape(batches, ranks, 3, strip)
    rows_f = lax.dynamic_index_in_dim(rows_f, me, 1, False).swapaxes(0, 1).reshape(3, units).astype(f32)
    qkv_shift = lax.dynamic_slice_in_dim(rows_d[:3], me * cols, cols, 1).reshape(1, 3 * cols)
    branch = lax.dynamic_slice_in_dim(rows_d[3:], me * cols, cols, 1)
    gain_in, gain_mid = rows_d[3:4], rows_d[5:6]
    shift_in, shift_mid, shift_out, shift_down = rows_d[6:7], rows_d[8:9], rows_d[9:10], rows_d[10:11]
    gain_branch, shift_branch = branch[1:2], branch[4:5]
    gain_ffn, shift_ffn, shift_up = rows_f[0:1], rows_f[1:2], rows_f[2:3]

    (up_pieces, *cot_send), _ = lax.optimization_barrier(((up_pieces, *cot_own), x_pieces))
    full_out = lax.all_gather(part_out, "batch", axis=0, tiled=True)
    full_down = lax.all_gather(w_down, "batch", axis=0, tiled=True)
    up_pieces = move.sent(up_pieces)

    x_full, input_low, row_stats = enter_attention(x_pieces, gain_in, shift_in)
    query_rot, key_rot, value_low = qkv_project(input_low, full_qkv, qkv_shift, tables)
    cot_pieces = move.gather(*cot_send, late=(query_rot,))
    up_pieces, _ = lax.optimization_barrier((up_pieces, query_rot))
    full_up = lax.all_gather(move.ordered(up_pieces).reshape(d_rows * ranks, units), "batch", axis=0, tiled=True)
    lo, hi, q_lo, q_hi = key_limits(doc_bounds[0], span_starts[0], data_type[0], tokens)
    k_first, k_last, q_first, q_last = block_limits(lo, hi, q_lo, q_hi)
    lo, hi = lo[None], hi[None]
    attn, lse, stat = attention_fwd(
        query_rot, key_rot, value_low, lo, hi, move.slots, k_first, k_last, after=cot_pieces[1:2] + cot_pieces[5:6]
    )
    stat, _ = lax.optimization_barrier((stat, cot_pieces))
    stats2 = move.spread(stat)
    branch_low, parts = out_project(attn, stats2, gain_branch, shift_branch, full_out, move.groups, after=cot_pieces)

    def enter(vectors, values, arrived):
        resid = values[0].astype(f32) + (arrived + vectors[0])
        normed, _ = norm_parts(resid)
        return resid, normed * vectors[1] + vectors[2]

    cot_full = jnp.concatenate(cot_pieces, axis=0)
    *resid, mid_upper, mid_lower = own_rows(
        enter,
        [shift_out, gain_mid, shift_mid],
        [x_own],
        move.scatter(parts),
        [(f32, False), (bf16, False)],
        after=(cot_full,),
        name="enter_ffn",
    )
    mid_pieces = move.gather(mid_upper, mid_lower)
    (cot_here, *_) = lax.optimization_barrier((cot_full, mid_upper))
    scaled_grad, grad_sums, shift_sums = ffn_grad(cot_here, full_down, gain_ffn)
    mid_low, up_proj, stat = ffn_up(mid_pieces, scaled_grad, grad_sums, full_up, shift_up)
    stats4 = move.spread(stat)
    ffn_low, grad_up, sums_ff, parts = ffn_mid(up_proj, scaled_grad, stats4, gain_ffn, shift_ffn, full_up, move.groups)
    g_down = tn(ffn_low, cot_full).astype(bf16)
    sum_down = lax.psum_scatter(g_down, "batch", scatter_dimension=0, tiled=True)
    arriving = move.scatter(parts, (g_down,))
    grad_up, _ = lax.optimization_barrier((grad_up, move.forwarded))
    g_up = tn(mid_low, grad_up).astype(bf16)
    sum_up = lax.psum_scatter(g_up, "batch", scatter_dimension=0, tiled=True)

    def leave(vectors, values, arrived):
        normed, inverse = norm_parts(values[0])
        cot = values[1].astype(f32)
        grad = cot + norm_lower(normed, inverse, vectors[0], arrived)
        low = grad.astype(bf16)
        return grad, low, arrived * normed, arrived, low.astype(f32), cot

    *grad_resid, resid_upper, resid_lower, sums_mid = own_rows(
        leave,
        [gain_mid],
        [resid, cot_own],
        arriving,
        [(f32, False), (bf16, False)],
        sums=4,
        after=(g_up,),
        name="leave_ffn",
    )
    resid_pieces = move.gather(resid_upper, resid_lower)
    down_parts = down_project(ffn_low, full_down, move.groups, after=(resid_upper,))

    resid_low, grad_branch, stat, sums_branch = branch_back(
        resid_pieces, full_out, attn, stats2, gain_branch, after=down_parts
    )
    down_parts, _ = lax.optimization_barrier((down_parts, resid_pieces))
    stats3 = move.spread(stat)
    g_out = tn(branch_low, resid_low).astype(bf16)
    attn_low, dots = attn_grad(grad_branch, attn, stats2, stats3, gain_branch, after=(g_out,))

    def back(part, after):
        return attention_bwd(
            part, 2, query_rot, key_rot, value_low, attn_low, lse, dots, lo, hi, tables, move.slots, q_first, q_last, after
        )

    grad_first = back(0, (sum_down,))
    arriving = move.scatter(down_parts, (grad_first,))
    forwarded = move.forwarded
    g_first = tn(input_low, grad_first).astype(bf16)
    sum_first = lax.psum_scatter(g_first, "batch", scatter_dimension=0, tiled=True)
    g_out, _ = lax.optimization_barrier((g_out, sum_down))
    sum_out = lax.psum_scatter(g_out, "batch", scatter_dimension=0, tiled=True)
    grad_second = back(1, (g_first, sum_up, *forwarded))
    bias_sums, sums_in, parts = input_back(
        (grad_first, grad_second),
        full_qkv,
        x_full,
        row_stats,
        move.groups,
        after=[terms[-1][0] for terms in arriving],
    )

    def finish(vectors, values, arrived):
        return (values[0] + (arrived + vectors[0]),)

    result = own_rows(
        finish, [shift_down], [resid], arriving, [(bf16, True)], after=(parts[0],), name="finish"
    )[0]
    sum_up, _ = lax.optimization_barrier((sum_up, parts))
    up_rows = move.sent(move.picked(sum_up.reshape(ranks, d_rows, batches, strip), 0))
    arriving = move.scatter(parts, (sum_first, sum_out, result, *up_rows))
    out_up = jnp.moveaxis(move.ordered(up_rows), 0, 2).reshape(d_rows, batches * ranks * strip).astype(f32)
    grad_second, _ = lax.optimization_barrier((grad_second, parts))
    g_second = tn(input_low, grad_second).astype(bf16)
    sum_second = lax.psum_scatter(g_second, "batch", scatter_dimension=0, tiled=True)
    sums_qkv = jnp.stack([s.reshape(ranks, d_rows, 3, cols // 2) for s in (sum_first, sum_second)], axis=3)
    qkv_rows = move.sent(move.picked(sums_qkv.reshape(ranks, d_rows, 3, cols), 0))
    sum_out, _ = lax.optimization_barrier((sum_out, sums_qkv))
    out_rows = lax.ppermute(sum_out, EVERY, [(b, a) for a, b in order])

    def end(vectors, values, arrived):
        normed, inverse = norm_parts(values[0].astype(f32))
        return (values[1] + norm_lower(normed, inverse, vectors[0], arrived),)

    def placed(value):
        return lax.dynamic_update_slice(jnp.zeros((value.shape[0], D), f32), value, (0, me * cols))

    branch_rows = placed(sums_branch[:2])
    vector_d = jnp.concatenate(
        [
            placed(bias_sums[0].reshape(3, cols)),
            sums_in[:1],
            branch_rows[:1],
            sums_mid[:1],
            sums_in[1:2],
            branch_rows[1:],
            sums_mid[1:4],
        ]
    )
    vector_f = jnp.concatenate([sums_ff[:1] / gain_ffn, shift_sums[:1], sums_ff[1:2]]).reshape(3, batches, 1, strip)
    vector_f = lax.dynamic_update_slice(jnp.zeros((3, batches, ranks, strip), f32), vector_f, (0, 0, me, 0))
    vector = jnp.concatenate(
        [
            vector_d.reshape(11, batches * ranks, d_rows).swapaxes(0, 1).reshape(batches * ranks, -1),
            vector_f.reshape(3, batches * ranks, strip).swapaxes(0, 1).reshape(batches * ranks, -1),
        ],
        axis=1,
    )
    vector = sum_small(vector, batches, ranks, [terms[-1][0] for terms in arriving] + qkv_rows)
    out_qkv = jnp.moveaxis(move.ordered(qkv_rows), 0, 2).reshape(d_rows, 3 * D).astype(f32)
    out_out = out_rows.astype(f32)
    out_down = sum_down.astype(f32)
    grad_total = own_rows(
        end, [gain_in], [x_own, grad_resid], arriving, [(f32, True)], after=(out_qkv, out_up), name="end"
    )[0]
    own_d = vector[:cut].reshape(11, d_rows)
    own_f = vector[cut:].reshape(3, strip)
    return (
        result.reshape(1, rows, D),
        grad_total.reshape(1, rows, D),
        out_qkv,
        own_d[:3],
        out_out,
        out_up,
        out_down,
        own_d[3:6],
        own_d[6:],
        own_f[0],
        own_f[1:],
    )


def solution(mesh):
    sizes = dict(mesh.shape)

    def run(*args):
        return local(*args, batches=sizes["batch"], ranks=sizes["seq"])

    return jax.shard_map(
        run,
        mesh=mesh,
        in_specs=(
            P("batch", "seq", None),
            P("batch", "seq", None),
            P(("batch", "seq"), None),
            P(None, ("batch", "seq")),
            P(("batch", "seq"), None),
            P(("batch", "seq"), None),
            P(("batch", "seq"), None),
            P(None, ("batch", "seq")),
            P(None, ("batch", "seq")),
            P(("batch", "seq")),
            P(None, ("batch", "seq")),
            P("batch"),
            P("batch", None),
            P("batch", None),
        ),
        out_specs=(
            P("batch", "seq", None),
            P("batch", "seq", None),
            P(("batch", "seq"), None),
            P(None, ("batch", "seq")),
            P(("batch", "seq"), None),
            P(("batch", "seq"), None),
            P(("batch", "seq"), None),
            P(None, ("batch", "seq")),
            P(None, ("batch", "seq")),
            P(("batch", "seq")),
            P(None, ("batch", "seq")),
        ),
        check_vma=False,
    )
```

```python
import jax
import jax.numpy as jnp
from jax import lax
from jax.experimental import pallas as pl
from jax.experimental.pallas import tpu as pltpu
from jax.sharding import PartitionSpec as P

D = 2048
HEADS = 32
HEAD_DIM = 64
SEQ_LEN = 2048
SPAN = 64
BLK = 256
NEG_FILL = -1e30
NORM_EPS = 1e-05
EVERY = ("batch", "seq")


def nt(a, b):
    return lax.dot_general(a, b, (((1,), (1,)), ((), ())), preferred_element_type=jnp.float32)


def tn(a, b):
    return lax.dot_general(a, b, (((0,), (0,)), ((), ())), preferred_element_type=jnp.float32)


def nn(a, b):
    return jnp.dot(a, b, preferred_element_type=jnp.float32)


TAKES = {
    "enter_attention": 12,
    "qkv_project": 19,
    "attention_forward": 41,
    "out_project": 14,
    "down_project": 200,
    "add_rows": 30,
    "ffn_grad": 24,
    "ffn_up": 33,
    "ffn_mid": 47,
    "branch_back": 150,
    "attn_grad": 38.0,
    "attention_backward": 200.0,
    "input_back": 112.0,
    "enter_ffn": 7,
    "leave_ffn": 100,
    "finish": 6,
    "end": 8,
}


def launch(body, grid, ins, outs, scratch=(), prefetch=(), after=(), name=None):
    n_pre, n_in, n_after = len(prefetch), len(ins), len(after)

    def kernel(*refs):
        body(*refs[: n_pre + n_in], *refs[n_pre + n_in + n_after :])

    return pl.pallas_call(
        kernel,
        out_shape=tuple(jax.ShapeDtypeStruct(s, d) for s, d, _ in outs),
        grid_spec=pltpu.PrefetchScalarGridSpec(
            num_scalar_prefetch=n_pre,
            grid=grid,
            in_specs=[b for _, b in ins] + [pl.BlockSpec(memory_space=pl.ANY)] * n_after,
            out_specs=[b for _, _, b in outs],
            scratch_shapes=list(scratch),
        ),
        compiler_params=pltpu.CompilerParams(vmem_limit_bytes=58 << 20),
        cost_estimate=pl.CostEstimate(flops=int(TAKES[name] * 1e9), bytes_accessed=int(TAKES[name] * 2e6), transcendentals=0),
        name=name,
    )(*prefetch, *(a for a, _ in ins), *after)


def tile(rows, cols):
    return pl.BlockSpec((rows, cols), lambda i, *_: (i, 0))


def fixed(array):
    zeros = (0,) * array.ndim
    return (array, pl.BlockSpec(array.shape, lambda *_: zeros, pipeline_mode=pl.Buffered(1)))


def arrivals(pieces, width):
    if len(pieces) == 1:

        def read_block(refs, buffer):
            buffer[...] = refs[0][...]

        return [(pieces[0], tile(BLK, width))], [], read_block

    def read(refs, buffer, landing, sems):
        step = pl.program_id(0)
        copies = [pltpu.make_async_copy(ref, landing.at[a % 2], sems.at[a % 2]) for a, ref in enumerate(refs)]

        @pl.when(step == 0)
        def _():
            copies[0].start()

        for a in range(len(copies)):

            @pl.when(step == a)
            def _():
                if a + 1 < len(copies):
                    copies[a + 1].start()
                copies[a].wait()
                buffer[...] = landing[a % 2]

    inputs = [(p, pl.BlockSpec(memory_space=pl.ANY)) for p in pieces]
    return inputs, [pltpu.VMEM((2, BLK, width), jnp.bfloat16), pltpu.SemaphoreType.DMA((2,))], read


def departures(rows, width, groups):
    count = rows // BLK // groups
    outs = []
    for a in range(groups):
        spec = pl.BlockSpec((BLK, width), lambda i, *_, s=a * count: (jnp.clip(i - s, 0, count - 1), 0))
        outs.append(((rows // groups, width), jnp.bfloat16, spec))

    def write(refs, value):
        step = pl.program_id(0)
        for a, ref in enumerate(refs):

            @pl.when(step // count == a)
            def _():
                ref[...] = value

    return outs, write


def columns(lines):
    count, width = len(lines), lines[0].shape[1]
    pad = [jnp.zeros((8 - count, width), jnp.float32)] if count < 8 else []
    flat = jnp.concatenate(list(lines) + pad, axis=0).T
    return [flat[:, i : i + 1] for i in range(count)]


def joined(centers, squares, width):
    count = len(centers)
    center = sum(centers) * (1.0 / count)
    total = sum(squares) + width * sum((c - center) ** 2 for c in centers)
    return center, lax.rsqrt(total * (1.0 / (width * count)) + NORM_EPS)


def rotate(value, tables, sign):
    straight, from_right, from_left = tables
    turned = pltpu.roll(value, 127, 1) * from_right + pltpu.roll(value, 1, 1) * from_left
    return value * straight + turned if sign > 0 else value * straight - turned


def enter_attention(pieces, gain, shift):
    rows, wide = sum(p.shape[0] for p in pieces), pieces[0].shape[1]
    inputs, landing, read = arrivals(pieces, wide)

    def body(g_ref, s_ref, *rest):
        piece_refs, (x_ref, low_ref, stat_ref, *scratch) = rest[: len(pieces)], rest[len(pieces) :]
        read(piece_refs, x_ref, *scratch)
        spread = x_ref[...].astype(jnp.float32)
        center = jnp.mean(spread, axis=-1, keepdims=True)
        spread = spread - center
        inverse = lax.rsqrt(jnp.mean(spread * spread, axis=-1, keepdims=True) + NORM_EPS)
        low_ref[...] = (spread * inverse * g_ref[...] + s_ref[...]).astype(jnp.bfloat16)
        lane = lax.broadcasted_iota(jnp.int32, (BLK, 128), 1)
        stat_ref[...] = jnp.where(lane == 0, center, inverse)

    return launch(
        body,
        (rows // BLK,),
        [fixed(gain), fixed(shift)] + inputs,
        [((rows, wide), jnp.bfloat16, tile(BLK, wide))] * 2 + [((rows, 128), jnp.float32, tile(BLK, 128))],
        scratch=landing,
        name="enter_attention",
    )


def qkv_project(low, weight, bias, tables, after=()):
    rows, width = low.shape
    cols = weight.shape[1] // 3

    def body(low_ref, w_ref, b_ref, *rest):
        table_refs, outs = rest[:6], rest[6:]
        for part in range(3):
            span = slice(part * cols, (part + 1) * cols)
            value = nn(low_ref[...], w_ref[:, span]) + b_ref[:, span]
            if part == 2:
                outs[2][...] = value.astype(jnp.bfloat16)
                continue
            own = [t[...] for t in table_refs[3 * part : 3 * part + 3]]
            for at in range(0, cols, 128):
                outs[part][:, at : at + 128] = rotate(value[:, at : at + 128], own, 1).astype(jnp.bfloat16)

    return launch(
        body,
        (rows // BLK,),
        [(low, tile(BLK, width)), fixed(weight), fixed(bias)] + [(t, tile(BLK, 128)) for t in tables],
        [((rows, cols), jnp.bfloat16, tile(BLK, cols))] * 3,
        after=after,
        name="qkv_project",
    )


def attention_fwd(q, k, v, lo, hi, slots, first, last, after=()):
    rows, width = q.shape
    blocks = rows // BLK
    heads = width // HEAD_DIM
    extra = 16

    def body(slots, first, last, q_ref, k_ref, v_ref, lo_ref, hi_ref, o_ref, lse_ref, stat_ref, vt, acc, qt, kept):
        step = pl.program_id(0)

        @pl.when(step == 0)
        def _():
            for i in range(blocks):
                at = slice(i * BLK, (i + 1) * BLK)
                flat = v_ref[at, :].T
                for h in range(heads):
                    vt[h, :HEAD_DIM, at] = flat[h * HEAD_DIM : (h + 1) * HEAD_DIM]
                    vt[h, HEAD_DIM:, at] = jnp.ones((extra, BLK), jnp.bfloat16)

        flat = (q_ref[...] * jnp.bfloat16(HEAD_DIM**-0.5)).T
        zero = jnp.zeros((HEAD_DIM, BLK), jnp.bfloat16)
        for h in range(heads):
            mine = flat[h * HEAD_DIM : (h + 1) * HEAD_DIM, :]
            qt[h] = jnp.concatenate([mine, zero] if h % 2 == 0 else [zero, mine], axis=0)
        low, high = lo_ref[...], hi_ref[...]
        key_row = lax.broadcasted_iota(jnp.int32, (BLK, BLK), 0)

        def scores(kb, peaks):
            at = pl.ds(pl.multiple_of(slots[kb] * BLK, BLK), BLK)
            spot = key_row + kb * BLK
            seen = (spot >= low) & (spot <= high)
            out = []
            for h in range(heads):
                two = slice(h // 2 * 128, h // 2 * 128 + 128)
                s = jnp.where(seen, nn(k_ref[at, two], qt[h]), NEG_FILL)
                kept[kb, h] = s
                out.append(jnp.maximum(peaks[h], jnp.max(s, axis=0, keepdims=True)))
            return tuple(out)

        start = tuple(jnp.full((1, BLK), NEG_FILL, jnp.float32) for _ in range(heads))
        peaks = lax.fori_loop(first[step], last[step], scores, start)
        acc[...] = jnp.zeros_like(acc)

        def weigh(kb, _):
            at = pl.ds(pl.multiple_of(slots[kb] * BLK, BLK), BLK)
            for h in range(heads):
                p = jnp.exp(kept[kb, h] - peaks[h]).astype(jnp.bfloat16)
                acc[h] += nn(vt[h, :, at], p)
            return 0

        lax.fori_loop(first[step], last[step], weigh, 0)
        parts = []
        for h in range(heads):
            total = acc[h, HEAD_DIM : HEAD_DIM + 1, :]
            lse_ref[h : h + 1, :] = peaks[h] + jnp.log(total)
            parts.append(acc[h, :HEAD_DIM] / total)
        flat = jnp.concatenate(parts, axis=0)
        center = jnp.mean(flat, axis=0, keepdims=True)
        stat_ref[0:1, :] = center
        stat_ref[1:2, :] = jnp.sum((flat - center) ** 2, axis=0, keepdims=True)
        stat_ref[2:8, :] = jnp.zeros((6, BLK), jnp.float32)
        o_ref[...] = flat.T

    by_slot = pl.BlockSpec((BLK, width), lambda i, s, *_: (s[i], 0))
    line = pl.BlockSpec((1, BLK), lambda i, *_: (0, i))
    return launch(
        body,
        (blocks,),
        [(q, by_slot), fixed(k), fixed(v), (lo, line), (hi, line)],
        [
            ((rows, width), jnp.float32, by_slot),
            ((heads, rows), jnp.float32, pl.BlockSpec((heads, BLK), lambda i, s, *_: (0, s[i]))),
            ((8, rows), jnp.float32, pl.BlockSpec((8, BLK), lambda i, s, *_: (0, s[i]))),
        ],
        scratch=[
            pltpu.VMEM((heads, HEAD_DIM + extra, rows), jnp.bfloat16),
            pltpu.VMEM((heads, HEAD_DIM + extra, BLK), jnp.float32),
            pltpu.VMEM((heads, 128, BLK), jnp.bfloat16),
            pltpu.VMEM((blocks, heads, BLK, BLK), jnp.float32),
        ],
        prefetch=(slots, first, last),
        after=after,
        name="attention_forward",
    )


def out_project(attn, stats, gain, shift, weight, groups, after=()):
    rows, width = attn.shape
    wide = weight.shape[1]
    outs, write = departures(rows, wide, groups)

    def body(a_ref, g_ref, s_ref, w_ref, *rest):
        stat_refs, (low_ref, *part_refs) = rest[: len(stats)], rest[len(stats) :]
        center, inverse = columns(joined([r[0:1] for r in stat_refs], [r[1:2] for r in stat_refs], width))
        low = ((a_ref[...] - center) * inverse * g_ref[...] + s_ref[...]).astype(jnp.bfloat16)
        low_ref[...] = low
        write(part_refs, nn(low, w_ref[...]).astype(jnp.bfloat16))

    low, *parts = launch(
        body,
        (rows // BLK,),
        [(attn, tile(BLK, width)), fixed(gain), fixed(shift), fixed(weight)] + list(stats),
        [((rows, width), jnp.bfloat16, tile(BLK, width))] + outs,
        after=after,
        name="out_project",
    )
    return low, parts


def down_project(low, weight, groups, after=()):
    rows, width = low.shape
    wide = weight.shape[1]
    outs, write = departures(rows, wide, groups)

    def body(l_ref, w_ref, *part_refs):
        write(part_refs, nn(l_ref[...], w_ref[...]).astype(jnp.bfloat16))

    return launch(
        body,
        (rows // BLK,),
        [(low, tile(BLK, width)), fixed(weight)],
        outs,
        after=after,
        name="down_project",
    )


def add_rows(pairs, after=()):
    wide = pairs[0][0].shape[1]
    half = pairs[0][0].shape[0] // 2
    piece = min(128, half)

    def body(*refs):
        ins, outs = refs[: 2 * len(pairs)], refs[2 * len(pairs) :]
        for i, ref in enumerate(outs):
            ref[...] = (ins[2 * i][...].astype(jnp.float32) + ins[2 * i + 1][...].astype(jnp.float32)).astype(jnp.bfloat16)

    spec = pl.BlockSpec((piece, wide), lambda i: (half // piece + i, 0))
    return launch(
        body,
        (half // piece,),
        [(x, spec) for pair in pairs for x in pair],
        [((half, wide), jnp.bfloat16, tile(piece, wide))] * len(pairs),
        after=after,
        name="add_rows",
    )


def own_rows(body, wholes, rows_in, terms, outs, sums=0, after=(), name=None):
    half, wide = rows_in[0][0].shape
    piece = min(128, half)
    count = len(terms[0])

    def kernel(*refs):
        whole_refs, refs = refs[: len(wholes)], refs[len(wholes) :]
        row_refs, refs = refs[: 2 * len(rows_in)], refs[2 * len(rows_in) :]
        term_refs, out_refs = refs[: 2 * count], list(refs[2 * count :])
        targets = []
        for _, stacked in outs:
            if stacked:
                ref = out_refs.pop(0)
                targets.append((ref.at[0], ref.at[1]))
            else:
                targets.append((out_refs.pop(0), out_refs.pop(0)))
        vectors = [r[...] for r in whole_refs]
        added = [0.0] * sums
        for side in range(2):
            total = term_refs[side * count][...].astype(jnp.float32)
            for r in term_refs[side * count + 1 : (side + 1) * count]:
                total = total + r[...].astype(jnp.float32)
            values = body(vectors, [r[...] for r in row_refs[side::2]], total)
            for target, value in zip(targets, values[: len(outs)]):
                target[side][...] = value.astype(target[side].dtype)
            added = [a + jnp.sum(v, axis=0, keepdims=True) for a, v in zip(added, values[len(outs) :])]
        if sums:
            sum_ref = out_refs[0]

            @pl.when(pl.program_id(0) == 0)
            def _():
                sum_ref[...] = jnp.zeros_like(sum_ref)

            for i, a in enumerate(added):
                sum_ref[i : i + 1, :] += a

    pieces = []
    for side in range(2):
        for array, start in terms[side]:
            pieces.append((array, pl.BlockSpec((piece, wide), lambda i, at=start // piece: (at + i, 0))))
    results = []
    for d, stacked in outs:
        if stacked:
            results.append(((2, half, wide), d, pl.BlockSpec((2, piece, wide), lambda i: (0, i, 0))))
        else:
            results += [((half, wide), d, tile(piece, wide))] * 2
    if sums:
        results.append(((8, wide), jnp.float32, pl.BlockSpec((8, wide), lambda i: (0, 0))))
    return launch(
        kernel,
        (half // piece,),
        [fixed(w) for w in wholes] + [(r, tile(piece, wide)) for pair in rows_in for r in pair] + pieces,
        results,
        after=after,
        name=name,
    )


def norm_parts(values):
    center = jnp.mean(values, axis=-1, keepdims=True)
    spread = values - center
    inverse = lax.rsqrt(jnp.mean(spread * spread, axis=-1, keepdims=True) + NORM_EPS)
    return spread * inverse, inverse


def norm_lower(normed, inverse, gain, upper):
    scaled = upper * gain
    first_mean = jnp.mean(scaled, axis=-1, keepdims=True)
    second_mean = jnp.mean(scaled * normed, axis=-1, keepdims=True)
    return inverse * (scaled - first_mean - normed * second_mean)


GELU_A = 0.044715
GELU_C = 0.7978845608028654


def ffn_grad(cot, w_down, gain):
    rows, wide = cot.shape
    units = w_down.shape[0]
    chunk = min(512, units)

    def body(c_ref, d_w, g_ref, grad_ref, stat_ref, sum_ref):
        @pl.when(pl.program_id(0) == 0)
        def _():
            sum_ref[...] = jnp.zeros_like(sum_ref)

        total = 0.0
        for at in range(0, units, chunk):
            span = slice(at, at + chunk)
            grad = nt(c_ref[...], d_w[span, :])
            scaled = grad * g_ref[:, span]
            grad_ref[:, span] = scaled
            sum_ref[0:1, span] += jnp.sum(grad, axis=0, keepdims=True)
            total = total + jnp.sum(scaled, axis=1, keepdims=True)
        lane = lax.broadcasted_iota(jnp.int32, (BLK, 128), 1)
        stat_ref[...] = jnp.where(lane == 0, total, 0.0).T[0:8, :]

    return launch(
        body,
        (rows // BLK,),
        [(cot, tile(BLK, wide)), fixed(w_down), fixed(gain)],
        [
            ((rows, units), jnp.float32, tile(BLK, units)),
            ((8, rows), jnp.float32, pl.BlockSpec((8, BLK), lambda i, *_: (0, i))),
            ((8, units), jnp.float32, pl.BlockSpec((8, units), lambda i, *_: (0, 0))),
        ],
        name="ffn_grad",
    )


def ffn_up(pieces, grad, grad_sums, w_up, bias):
    rows, units = grad.shape
    wide = w_up.shape[0]
    inputs, landing, read = arrivals(pieces, wide)
    chunk = min(512, units)
    share = 1.0 / chunk

    def body(f_ref, t_ref, u_w, b_ref, *rest):
        m_ref, up_ref, stat_ref, *scratch = rest[len(pieces) :]
        read(rest[: len(pieces)], m_ref, *scratch)
        parts = []

        def figures(at, up):
            span = slice(at, at + chunk)
            gel = 0.5 * up * (1.0 + jnp.tanh(GELU_C * up * (1.0 + GELU_A * up * up)))
            center = jnp.sum(gel, axis=1, keepdims=True) * share
            spread = gel - center
            scaled = f_ref[:, span]
            parts.append(
                (
                    center,
                    jnp.sum(spread * spread, axis=1, keepdims=True),
                    jnp.sum(scaled * spread, axis=1, keepdims=True),
                    jnp.sum(scaled, axis=1, keepdims=True),
                )
            )

        last = None
        for at in range(0, units, chunk):
            span = slice(at, at + chunk)
            up = nn(m_ref[...], u_w[:, span]) + b_ref[:, span]
            up_ref[:, span] = up
            if last is not None:
                figures(*last)
            last = at, up
        figures(*last)
        center = sum(p[0] for p in parts) * (1.0 / len(parts))
        square = sum(p[1] + chunk * (p[0] - center) ** 2 for p in parts)
        product = sum(p[2] + (p[0] - center) * p[3] for p in parts)
        lane = lax.broadcasted_iota(jnp.int32, (BLK, 128), 1)
        flat = jnp.zeros((BLK, 128), jnp.float32)
        for i, value in enumerate((center, square, product)):
            flat = jnp.where(lane == i, value, flat)
        flat = flat.T
        stat_ref[...] = jnp.concatenate([flat[0:2], t_ref[0:1, :], flat[2:7]], axis=0)

    return launch(
        body,
        (rows // BLK,),
        [
            (grad, tile(BLK, units)),
            (grad_sums, pl.BlockSpec((8, BLK), lambda i, *_: (0, i))),
            fixed(w_up),
            fixed(bias),
        ]
        + inputs,
        [
            ((rows, wide), jnp.bfloat16, tile(BLK, wide)),
            ((rows, units), jnp.float32, tile(BLK, units)),
            ((8, rows), jnp.float32, pl.BlockSpec((8, BLK), lambda i, *_: (0, i))),
        ],
        scratch=landing,
        name="ffn_up",
    )


def ffn_mid(up, grad, stats, gain, shift, w_up, groups):
    rows, units = up.shape
    wide = w_up.shape[0]
    chunk = min(512, units)
    ranks = len(stats)
    outs, write = departures(rows, wide, groups)

    def body(u_ref, f_ref, g_ref, s_ref, w_ref, *rest):
        stat_refs, (low_ref, gup_ref, sum_ref, *part_refs) = rest[:ranks], rest[ranks:]
        centers = [r[0:1] for r in stat_refs]
        center, inverse = joined(centers, [r[1:2] for r in stat_refs], units)
        share = 1.0 / (units * ranks)
        first = sum(r[2:3] for r in stat_refs) * share
        second = inverse * share * sum(r[3:4] + (c - center) * r[2:3] for r, c in zip(stat_refs, centers))
        center, inverse, first, second = columns([center, inverse, first, second])

        @pl.when(pl.program_id(0) == 0)
        def _():
            sum_ref[...] = jnp.zeros_like(sum_ref)

        for at in range(0, units, chunk):
            span = slice(at, at + chunk)
            u, f = u_ref[:, span], f_ref[:, span]
            squared = u * u
            t = jnp.tanh(GELU_C * u * (1.0 + GELU_A * squared))
            one = 0.5 * (1.0 + t)
            slope = one + 0.5 * u * (1.0 - t * t) * (GELU_C * (1.0 + 3.0 * GELU_A * squared))
            normed = (u * one - center) * inverse
            low_ref[:, span] = (normed * g_ref[:, span] + s_ref[:, span]).astype(jnp.bfloat16)
            lower = inverse * (f - first - normed * second)
            gup = (lower * slope).astype(jnp.bfloat16)
            gup_ref[:, span] = gup
            sum_ref[0:1, span] += jnp.sum(f * normed, axis=0, keepdims=True)
            sum_ref[1:2, span] += jnp.sum(gup.astype(jnp.float32), axis=0, keepdims=True)
        write(part_refs, nt(gup_ref[...], w_ref[...]).astype(jnp.bfloat16))

    low, gup, sums, *parts = launch(
        body,
        (rows // BLK,),
        [(up, tile(BLK, units)), (grad, tile(BLK, units)), fixed(gain), fixed(shift), fixed(w_up)] + list(stats),
        [
            ((rows, units), jnp.bfloat16, tile(BLK, units)),
            ((rows, units), jnp.bfloat16, tile(BLK, units)),
            ((8, units), jnp.float32, pl.BlockSpec((8, units), lambda i, *_: (0, 0))),
        ]
        + outs,
        name="ffn_mid",
    )
    return low, gup, sums, parts


def branch_back(pieces, w_out, attn, stats, gain, after=()):
    rows, width = attn.shape
    wide = w_out.shape[1]
    ranks = len(stats)
    inputs, landing, read = arrivals(pieces, wide)

    def body(w_ref, a_ref, g_ref, *rest):
        stat_refs, rest = rest[:ranks], rest[ranks:]
        r_ref, grad_ref, stat_ref, sum_ref, *scratch = rest[len(pieces) :]
        read(rest[: len(pieces)], r_ref, *scratch)
        center, inverse = columns(joined([r[0:1] for r in stat_refs], [r[1:2] for r in stat_refs], width))

        @pl.when(pl.program_id(0) == 0)
        def _():
            sum_ref[...] = jnp.zeros_like(sum_ref)

        grad = nt(r_ref[...], w_ref[...])
        grad_ref[...] = grad
        normed = (a_ref[...] - center) * inverse
        scaled = grad * g_ref[...]
        sum_ref[0:1, :] += jnp.sum(grad * normed, axis=0, keepdims=True)
        sum_ref[1:2, :] += jnp.sum(grad, axis=0, keepdims=True)
        lane = lax.broadcasted_iota(jnp.int32, (BLK, 128), 1)
        flat = jnp.where(lane == 0, jnp.sum(scaled, axis=1, keepdims=True), 0.0)
        flat = jnp.where(lane == 1, jnp.sum(scaled * normed, axis=1, keepdims=True), flat)
        stat_ref[...] = flat.T[0:8, :]

    return launch(
        body,
        (rows // BLK,),
        [fixed(w_out), (attn, tile(BLK, width)), fixed(gain)] + list(stats) + inputs,
        [
            ((rows, wide), jnp.bfloat16, tile(BLK, wide)),
            ((rows, width), jnp.float32, tile(BLK, width)),
            ((8, rows), jnp.float32, pl.BlockSpec((8, BLK), lambda i, *_: (0, i))),
            ((8, width), jnp.float32, pl.BlockSpec((8, width), lambda i, *_: (0, 0))),
        ],
        after=after,
        scratch=landing,
        name="branch_back",
    )


def attn_grad(grad, attn, stats, sums, gain, after=()):
    rows, width = attn.shape
    ranks = len(stats)
    heads = width // HEAD_DIM

    def body(f_ref, a_ref, g_ref, *rest):
        stat_refs, sum_refs = rest[:ranks], rest[ranks : 2 * ranks]
        out_ref, dot_ref = rest[2 * ranks :]
        center, inverse = joined([r[0:1] for r in stat_refs], [r[1:2] for r in stat_refs], width)
        share = 1.0 / (width * ranks)
        first = sum(r[0:1] for r in sum_refs) * share
        second = sum(r[1:2] for r in sum_refs) * share
        center, inverse, first, second = columns([center, inverse, first, second])
        attn_here = a_ref[...]
        normed = (attn_here - center) * inverse
        out = (inverse * (f_ref[...] * g_ref[...] - first - normed * second)).astype(jnp.bfloat16)
        out_ref[...] = out
        product = (out.astype(jnp.float32) * attn_here).T
        for h in range(heads):
            dot_ref[h : h + 1, :] = jnp.sum(product[h * HEAD_DIM : (h + 1) * HEAD_DIM], axis=0, keepdims=True)

    return launch(
        body,
        (rows // BLK,),
        [(grad, tile(BLK, width)), (attn, tile(BLK, width)), fixed(gain)] + list(stats) + list(sums),
        [
            ((rows, width), jnp.bfloat16, tile(BLK, width)),
            ((heads, rows), jnp.float32, pl.BlockSpec((heads, BLK), lambda i, *_: (0, i))),
        ],
        after=after,
        name="attn_grad",
    )


def attention_bwd(part, parts, q, k, v, g, lse, dot, lo, hi, tables, slots, first, last, after=()):
    rows, width = q.shape
    width //= parts
    blocks = rows // BLK
    heads = width // HEAD_DIM
    base = part * heads
    scale = HEAD_DIM**-0.5
    own_columns = pl.BlockSpec((rows, width), lambda *_: (0, part), pipeline_mode=pl.Buffered(1))

    def body(slots, first, last, q_ref, k_ref, v_ref, g_ref, lse_ref, dot_ref, lo_ref, hi_ref, *rest):
        table_refs, (out_ref, dqt, qt, gt, accs) = rest[:6], rest[6:]
        key_row = lax.broadcasted_iota(jnp.int32, (BLK, BLK), 0)
        lane = lax.broadcasted_iota(jnp.int32, (BLK, 128), 1)
        zero = jnp.zeros((), jnp.bfloat16)
        dqt[...] = jnp.zeros_like(dqt)
        for i in range(blocks):
            at = slice(i * BLK, (i + 1) * BLK)
            qt[:, at] = q_ref[at, :].T
            gt[:, at] = g_ref[at, :].T

        def outer(kb, _):
            rows_k = pl.ds(pl.multiple_of(slots[kb] * BLK, BLK), BLK)
            k, v = k_ref[rows_k, :] * jnp.bfloat16(scale), v_ref[rows_k, :]
            kts = k.T
            spot = key_row + kb * BLK

            def halves(x, h):
                x = x[:, h // 2 * 128 : h // 2 * 128 + 128]
                return jnp.where((lane < HEAD_DIM) == (h % 2 == 0), x, zero)

            ks = [halves(k, h) for h in range(heads)]
            vs = [halves(v, h) for h in range(heads)]
            accs[...] = jnp.zeros_like(accs)

            def inner(qb, _):
                at = pl.ds(pl.multiple_of(slots[qb] * BLK, BLK), BLK)
                here = pl.ds(pl.multiple_of(qb * BLK, BLK), BLK)
                seen = (spot >= lo_ref[0:1, here]) & (spot <= hi_ref[0:1, here])
                def products(h):
                    two = slice(h // 2 * 128, h // 2 * 128 + 128)
                    return nn(ks[h], qt[two, at]), nn(vs[h], gt[two, at])

                def factors(h, s, dp):
                    p = jnp.where(seen, jnp.exp(s - lse_ref[base + h : base + h + 1, at]), 0.0)
                    ds = (p * (dp - dot_ref[base + h : base + h + 1, at])).astype(jnp.bfloat16)
                    return p.astype(jnp.bfloat16), ds

                def add(h, p, ds):
                    two = slice(h // 2 * 128, h // 2 * 128 + 128)
                    span = slice(h * HEAD_DIM, (h + 1) * HEAD_DIM)
                    accs[1, h] += nn(p, g_ref[at, two])
                    accs[0, h] += nn(ds, q_ref[at, two])
                    dqt[span, at] += nn(kts[span, :], ds)

                made, ready = {}, {}
                for h in range(heads + 2):
                    if h < heads:
                        made[h] = products(h)
                    if 0 <= h - 1 < heads:
                        ready[h - 1] = factors(h - 1, *made[h - 1])
                    if 0 <= h - 2 < heads:
                        add(h - 2, *ready[h - 2])
                return 0

            lax.fori_loop(first[kb], last[kb], inner, 0)
            own = [t[rows_k, :] for t in table_refs[3:]]
            for h in range(0, heads, 2):
                at = h * HEAD_DIM
                grad_k = jnp.where(lane < HEAD_DIM, accs[0, h], accs[0, h + 1]) * scale
                grad_v = jnp.where(lane < HEAD_DIM, accs[1, h], accs[1, h + 1])
                out_ref[rows_k, width + at : width + at + 128] = rotate(grad_k, own, -1).astype(jnp.bfloat16)
                out_ref[rows_k, 2 * width + at : 2 * width + at + 128] = grad_v.astype(jnp.bfloat16)
            return 0

        lax.fori_loop(0, blocks, outer, 0)
        for i in range(blocks):
            at = slice(i * BLK, (i + 1) * BLK)
            grad_q = dqt[:, at].T
            own = [t[at, :] for t in table_refs[:3]]
            for col in range(0, width, 128):
                out_ref[at, col : col + 128] = rotate(grad_q[:, col : col + 128], own, -1).astype(jnp.bfloat16)

    return launch(
        body,
        (1,),
        [(a, own_columns) for a in (q, k, v, g)] + [fixed(a) for a in (lse, dot, lo, hi, *tables)],
        [((rows, 3 * width), jnp.bfloat16, pl.BlockSpec((rows, 3 * width), lambda *_: (0, 0), pipeline_mode=pl.Buffered(1)))],
        scratch=[
            pltpu.VMEM((width, rows), jnp.float32),
            pltpu.VMEM((width, rows), jnp.bfloat16),
            pltpu.VMEM((width, rows), jnp.bfloat16),
            pltpu.VMEM((2, heads, BLK, 128), jnp.float32),
        ],
        prefetch=(slots, first, last),
        after=after,
        name="attention_backward",
    )[0]


def input_back(grads, weight, x, row_stats, groups, after=()):
    rows, wide = x.shape
    cols = weight.shape[1]
    parts = len(grads)
    small = cols // parts // 3
    outs, write = departures(rows, wide, groups)

    def body(w_ref, x_ref, stat_ref, *rest):
        grad_refs, (bias_ref, sum_ref, *part_refs), g_ref = rest[:parts], rest[parts:-1], rest[-1]

        @pl.when(pl.program_id(0) == 0)
        def _():
            sum_ref[...] = jnp.zeros_like(sum_ref)
            bias_ref[...] = jnp.zeros_like(bias_ref)

        for p, ref in enumerate(grad_refs):
            for j in range(3):
                at = (j * parts + p) * small
                g_ref[:, at : at + small] = ref[:, j * small : (j + 1) * small]
        value = nt(g_ref[...], w_ref[...])
        write(part_refs, value.astype(jnp.bfloat16))
        bias_ref[0:1, :] += jnp.sum(g_ref[...].astype(jnp.float32), axis=0, keepdims=True)
        normed = (x_ref[...].astype(jnp.float32) - stat_ref[:, 0:1]) * stat_ref[:, 1:2]
        sum_ref[0:1, :] += jnp.sum(value * normed, axis=0, keepdims=True)
        sum_ref[1:2, :] += jnp.sum(value, axis=0, keepdims=True)

    bias_sums, sums, *parts_out = launch(
        body,
        (rows // BLK,),
        [fixed(weight), (x, tile(BLK, wide)), (row_stats, tile(BLK, 128))]
        + [(g, tile(BLK, cols // parts)) for g in grads],
        [
            ((8, cols), jnp.float32, pl.BlockSpec((8, cols), lambda i, *_: (0, 0))),
            ((8, wide), jnp.float32, pl.BlockSpec((8, wide), lambda i, *_: (0, 0))),
        ]
        + outs,
        scratch=[pltpu.VMEM((BLK, cols), jnp.bfloat16)],
        after=after,
        name="input_back",
    )
    return bias_sums, sums, parts_out


def key_limits(bounds, spans, kind, total):
    places = jnp.arange(total, dtype=jnp.int32)
    below = bounds[:, None] <= places[None, :]
    doc_first = jnp.max(jnp.where(below, bounds[:, None], 0), axis=0)
    doc_last = jnp.min(jnp.where(below, total, bounds[:, None]), axis=0) - 1
    doc_last = jnp.minimum(doc_last, total - 1)
    inside = (spans[:, None] <= places[None, :]) & (places[None, :] < spans[:, None] + SPAN) & (kind > 0)
    span_last = jnp.max(jnp.where(inside, spans[:, None] + SPAN - 1, 0), axis=0)
    span_first = jnp.min(jnp.where(inside, spans[:, None], total), axis=0)
    hi = jnp.minimum(jnp.maximum(places, span_last), doc_last)
    q_first = jnp.maximum(jnp.minimum(places, span_first), doc_first)
    return doc_first, hi, q_first, doc_last


def block_limits(lo, hi, qf, ql):
    low = lo.reshape(-1, BLK)[:, 0] // BLK
    high = hi.reshape(-1, BLK)[:, -1] // BLK + 1
    qlow = qf.reshape(-1, BLK)[:, 0] // BLK
    qhigh = ql.reshape(-1, BLK)[:, -1] // BLK + 1
    return low, high, qlow, qhigh


class Exchange:
    def __init__(self, ranks, batches, rows, me):
        self.ranks, self.batches, self.rows, self.me = ranks, batches, rows, me
        self.square = ranks == 4 and rows == 2 * BLK
        self.half = rows // 2
        self.groups = 4 if self.square else 1
        self.forwarded = ()
        self.order = ((0, 1, 2, 3), (0, 2, 1, 3))
        total = ranks * rows
        block = jnp.arange(total // BLK, dtype=jnp.int32)
        if self.square:
            owner, part = block // 2, block % 2
            near = owner ^ me
            swapped = (near >> 1) | ((near & 1) << 1)
            self.slots = (part * 4 + jnp.where(part == 0, near, swapped)).astype(jnp.int32)
            owners = jnp.stack([me ^ r for half in self.order for r in half])
            firsts = owners * rows + jnp.repeat(jnp.arange(2), 4) * self.half
            self.places = (firsts[:, None] + jnp.arange(self.half)[None, :]).reshape(total).astype(jnp.int32)
        else:
            self.slots = block
            self.places = jnp.arange(total, dtype=jnp.int32)

    def swap(self, value, bit):
        return lax.ppermute(value, "seq", [(r, r ^ bit) for r in range(self.ranks)])

    def gather(self, upper, lower, late=None):
        if not self.square:
            return [lax.all_gather(jnp.concatenate([upper, lower], axis=0), "seq", axis=0, tiled=True)]
        near_upper, near_lower = self.swap(upper, 1), self.swap(lower, 2)
        again = (upper, lower, near_upper, near_lower)
        if late is not None:
            again, _ = lax.optimization_barrier((again, late))
        return [upper, near_upper, self.swap(again[0], 2), self.swap(again[2], 2)] + [
            lower,
            near_lower,
            self.swap(again[1], 1),
            self.swap(again[3], 1),
        ]

    def scatter(self, parts, after=()):
        if not self.square:
            own = lax.psum_scatter(parts[0], "seq", scatter_dimension=0, tiled=True)
            return [[(own, 0)], [(own, self.half)]]
        keep_upper, send_upper, keep_lower, send_lower = parts
        near_upper, near_lower = self.swap(send_upper, 2), self.swap(send_lower, 1)
        far_upper, far_lower = add_rows([(keep_upper, near_upper), (keep_lower, near_lower)], after)
        sums = (far_upper, far_lower)
        far_upper, far_lower = self.swap(far_upper, 1), self.swap(far_lower, 2)
        self.forwarded = sums
        return [[(keep_upper, 0), (near_upper, 0), (far_upper, 0)], [(keep_lower, 0), (near_lower, 0), (far_lower, 0)]]

    def picked(self, value, axis):
        if not self.square:
            return [jnp.moveaxis(value, axis, 0)]
        return [lax.dynamic_index_in_dim(value, self.me ^ r, axis, False) for r in range(self.ranks)]

    def sent(self, pieces):
        if not self.square:
            return [lax.all_to_all(pieces[0], "seq", 0, 0)]
        return [pieces[0]] + [self.swap(pieces[r], r) for r in range(1, self.ranks)]

    def ordered(self, pieces):
        return flipped(jnp.stack(pieces), self.me, 2) if self.square else pieces[0]

    def spread(self, value):
        lines = value.shape[0]
        if not self.square:
            every = lax.all_gather(value, "seq", axis=0)
            return [(every[r], pl.BlockSpec((lines, BLK), lambda i, *_: (0, i))) for r in range(self.ranks)]
        out = [(value, pl.BlockSpec((lines, BLK), lambda i, *_: (0, i)))]
        for bit, other in ((1, 2), (2, 1), (3, 3)):
            spec = pl.BlockSpec(
                (lines, BLK), lambda i, *_, a=bit, b=other: (0, (i // 4) * 4 + ((i % 4) ^ (a + (i // 4) * (b - a))))
            )
            out.append((self.swap(value, bit), spec))
        return out


def flipped(value, device, bits):
    shape = value.shape
    for bit in range(bits):
        two = value.reshape((-1, 2, 1 << bit) + shape[1:])
        value = jnp.where((device >> bit) & 1, two[:, ::-1], two).reshape(shape)
    return value


def share_small(value, batches, ranks):
    if (batches, ranks) != (8, 4):
        return lax.all_gather(value, EVERY, axis=0)
    batch, me = lax.axis_index("batch"), lax.axis_index("seq")
    parts = value[None]
    for axis, count, steps in (("seq", ranks, (1, 2, 3)), ("batch", batches, (1,)), ("batch", batches, (2, 4, 6))):
        parts = jnp.concatenate(
            [parts] + [lax.ppermute(parts, axis, [(r, r ^ s) for r in range(count)]) for s in steps], axis=0
        )
    return flipped(parts, batch * ranks + me, 5)


def sum_small(value, batches, ranks, late):
    if (batches, ranks) != (8, 4):
        return lax.psum_scatter(value, EVERY, scatter_dimension=0, tiled=True)[0]
    batch, me = lax.axis_index("batch"), lax.axis_index("seq")
    value = flipped(value, batch * ranks + me, 5)
    for axis, count, steps, left in (("batch", batches, (2, 4, 6), 8), ("batch", batches, (1,), 4), ("seq", ranks, (1, 2, 3), 1)):
        if axis == "seq":
            value, _ = lax.optimization_barrier((value, late))
        total = value[:left]
        for i, s in enumerate(steps):
            at = (i + 1) * left
            total = total + lax.ppermute(value[at : at + left], axis, [(r, r ^ s) for r in range(count)])
        value = total
    return value[0]


def rot_tables(places):
    column = jnp.arange(128) % HEAD_DIM
    pair_idx = (column // 2).astype(jnp.float32)
    frequency = jnp.power(10000.0, -2.0 * pair_idx / HEAD_DIM)
    place_float = places.astype(jnp.float32)
    angles = place_float[:, None] * frequency[None, :]
    zeta_base = (2.0 * pair_idx + 0.4 * HEAD_DIM) / (1.4 * HEAD_DIM)
    exponent = (place_float - SEQ_LEN // 2) / 512.0
    scales = jnp.power(zeta_base[None, :], exponent[:, None])
    cosine, sine = jnp.cos(angles), jnp.sin(angles)
    even = (column % 2 == 0)[None, :]
    right, left = jnp.where(even, -sine, 0.0), jnp.where(even, 0.0, sine)
    return tuple(t * s for s in (scales, 1.0 / scales) for t in (cosine, right, left))


def local(
    layer_input,
    cotangent,
    w_qkv,
    bias_qkv,
    w_out,
    w_up,
    w_down,
    gains_d,
    biases_d,
    gain_ff,
    biases_ff,
    data_type,
    doc_bounds,
    span_starts,
    *,
    batches,
    ranks,
):
    me = lax.axis_index("seq")
    rows = layer_input.shape[1]
    half = rows // 2
    move = Exchange(ranks, batches, rows, me)
    tokens = rows * ranks
    cols = D // ranks
    strip, d_rows = w_down.shape[0], w_up.shape[0]
    units = strip * batches
    f32, bf16 = jnp.float32, jnp.bfloat16
    x_own = [layer_input.reshape(2, half, D)[i] for i in range(2)]
    cot_own = [cotangent.reshape(2, half, D)[i] for i in range(2)]

    x_pieces = move.gather(*x_own, late=())
    small = jnp.concatenate(
        [bias_qkv.reshape(-1), gains_d.reshape(-1), biases_d.reshape(-1), gain_ff, biases_ff.reshape(-1)]
    )

    small = share_small(small, batches, ranks)

    w_qkv, _ = lax.optimization_barrier((w_qkv, x_own))
    part_qkv = move.ordered(move.sent(move.picked(w_qkv.reshape(d_rows, 3, ranks, cols), 2)))
    up_pieces = move.picked(w_up.reshape(d_rows, batches, ranks, strip), 2)
    order = [(i, (i % batches) * ranks + i // batches) for i in range(batches * ranks)]
    part_out = lax.ppermute(w_out, EVERY, order)
    tables = rot_tables(move.places)
    early = (small, part_out, up_pieces, tables, x_pieces[1:2] + x_pieces[5:6])
    part_qkv, (small, part_out, up_pieces, tables, _) = lax.optimization_barrier((part_qkv, early))
    full_qkv = lax.all_gather(part_qkv.reshape(d_rows * ranks, 3 * cols), "batch", axis=0, tiled=True)
    cut = 11 * d_rows
    rows_d = small[:, :cut].reshape(-1, 11, d_rows).swapaxes(0, 1).reshape(11, D).astype(f32)
    rows_f = small[:, cut:].reshape(batches, ranks, 3, strip)
    rows_f = lax.dynamic_index_in_dim(rows_f, me, 1, False).swapaxes(0, 1).reshape(3, units).astype(f32)
    qkv_shift = lax.dynamic_slice_in_dim(rows_d[:3], me * cols, cols, 1).reshape(1, 3 * cols)
    branch = lax.dynamic_slice_in_dim(rows_d[3:], me * cols, cols, 1)
    gain_in, gain_mid = rows_d[3:4], rows_d[5:6]
    shift_in, shift_mid, shift_out, shift_down = rows_d[6:7], rows_d[8:9], rows_d[9:10], rows_d[10:11]
    gain_branch, shift_branch = branch[1:2], branch[4:5]
    gain_ffn, shift_ffn, shift_up = rows_f[0:1], rows_f[1:2], rows_f[2:3]

    (up_pieces, *cot_send), _ = lax.optimization_barrier(((up_pieces, *cot_own), x_pieces))
    full_out = lax.all_gather(part_out, "batch", axis=0, tiled=True)
    full_down = lax.all_gather(w_down, "batch", axis=0, tiled=True)
    up_pieces = move.sent(up_pieces)

    x_full, input_low, row_stats = enter_attention(x_pieces, gain_in, shift_in)
    query_rot, key_rot, value_low = qkv_project(input_low, full_qkv, qkv_shift, tables)
    cot_pieces = move.gather(*cot_send, late=(query_rot,))
    up_pieces, _ = lax.optimization_barrier((up_pieces, query_rot))
    full_up = lax.all_gather(move.ordered(up_pieces).reshape(d_rows * ranks, units), "batch", axis=0, tiled=True)
    lo, hi, q_lo, q_hi = key_limits(doc_bounds[0], span_starts[0], data_type[0], tokens)
    k_first, k_last, q_first, q_last = block_limits(lo, hi, q_lo, q_hi)
    lo, hi = lo[None], hi[None]
    attn, lse, stat = attention_fwd(
        query_rot, key_rot, value_low, lo, hi, move.slots, k_first, k_last, after=cot_pieces[1:2] + cot_pieces[5:6]
    )
    stat, _ = lax.optimization_barrier((stat, cot_pieces))
    stats2 = move.spread(stat)
    branch_low, parts = out_project(attn, stats2, gain_branch, shift_branch, full_out, move.groups, after=cot_pieces)

    def enter(vectors, values, arrived):
        resid = values[0].astype(f32) + (arrived + vectors[0])
        normed, _ = norm_parts(resid)
        return resid, normed * vectors[1] + vectors[2]

    cot_full = jnp.concatenate(cot_pieces, axis=0)
    *resid, mid_upper, mid_lower = own_rows(
        enter,
        [shift_out, gain_mid, shift_mid],
        [x_own],
        move.scatter(parts),
        [(f32, False), (bf16, False)],
        after=(cot_full,),
        name="enter_ffn",
    )
    mid_pieces = move.gather(mid_upper, mid_lower)
    (cot_here, *_) = lax.optimization_barrier((cot_full, mid_upper))
    scaled_grad, grad_sums, shift_sums = ffn_grad(cot_here, full_down, gain_ffn)
    mid_low, up_proj, stat = ffn_up(mid_pieces, scaled_grad, grad_sums, full_up, shift_up)
    stats4 = move.spread(stat)
    ffn_low, grad_up, sums_ff, parts = ffn_mid(up_proj, scaled_grad, stats4, gain_ffn, shift_ffn, full_up, move.groups)
    g_down = tn(ffn_low, cot_full).astype(bf16)
    sum_down = lax.psum_scatter(g_down, "batch", scatter_dimension=0, tiled=True)
    arriving = move.scatter(parts, (g_down,))
    grad_up, _ = lax.optimization_barrier((grad_up, move.forwarded))
    g_up = tn(mid_low, grad_up).astype(bf16)
    sum_up = lax.psum_scatter(g_up, "batch", scatter_dimension=0, tiled=True)

    def leave(vectors, values, arrived):
        normed, inverse = norm_parts(values[0])
        cot = values[1].astype(f32)
        grad = cot + norm_lower(normed, inverse, vectors[0], arrived)
        low = grad.astype(bf16)
        return grad, low, arrived * normed, arrived, low.astype(f32), cot

    *grad_resid, resid_upper, resid_lower, sums_mid = own_rows(
        leave,
        [gain_mid],
        [resid, cot_own],
        arriving,
        [(f32, False), (bf16, False)],
        sums=4,
        after=(g_up,),
        name="leave_ffn",
    )
    resid_pieces = move.gather(resid_upper, resid_lower)
    down_parts = down_project(ffn_low, full_down, move.groups, after=(resid_upper,))

    resid_low, grad_branch, stat, sums_branch = branch_back(
        resid_pieces, full_out, attn, stats2, gain_branch, after=down_parts
    )
    down_parts, _ = lax.optimization_barrier((down_parts, resid_pieces))
    stats3 = move.spread(stat)
    g_out = tn(branch_low, resid_low).astype(bf16)
    attn_low, dots = attn_grad(grad_branch, attn, stats2, stats3, gain_branch, after=(g_out,))

    def back(part, after):
        return attention_bwd(
            part, 2, query_rot, key_rot, value_low, attn_low, lse, dots, lo, hi, tables, move.slots, q_first, q_last, after
        )

    grad_first = back(0, (sum_down,))
    arriving = move.scatter(down_parts, (grad_first,))
    forwarded = move.forwarded
    g_first = tn(input_low, grad_first).astype(bf16)
    sum_first = lax.psum_scatter(g_first, "batch", scatter_dimension=0, tiled=True)
    g_out, _ = lax.optimization_barrier((g_out, sum_down))
    sum_out = lax.psum_scatter(g_out, "batch", scatter_dimension=0, tiled=True)
    grad_second = back(1, (g_first, sum_up, *forwarded))
    bias_sums, sums_in, parts = input_back(
        (grad_first, grad_second),
        full_qkv,
        x_full,
        row_stats,
        move.groups,
        after=[terms[-1][0] for terms in arriving],
    )

    def finish(vectors, values, arrived):
        return (values[0] + (arrived + vectors[0]),)

    result = own_rows(
        finish, [shift_down], [resid], arriving, [(bf16, True)], after=(parts[0],), name="finish"
    )[0]
    sum_up, _ = lax.optimization_barrier((sum_up, parts))
    up_rows = move.sent(move.picked(sum_up.reshape(ranks, d_rows, batches, strip), 0))
    arriving = move.scatter(parts, (sum_first, sum_out, result, *up_rows))
    out_up = jnp.moveaxis(move.ordered(up_rows), 0, 2).reshape(d_rows, batches * ranks * strip).astype(f32)
    grad_second, _ = lax.optimization_barrier((grad_second, parts))
    g_second = tn(input_low, grad_second).astype(bf16)
    sum_second = lax.psum_scatter(g_second, "batch", scatter_dimension=0, tiled=True)
    sums_qkv = jnp.stack([s.reshape(ranks, d_rows, 3, cols // 2) for s in (sum_first, sum_second)], axis=3)
    qkv_rows = move.sent(move.picked(sums_qkv.reshape(ranks, d_rows, 3, cols), 0))
    sum_out, _ = lax.optimization_barrier((sum_out, sums_qkv))
    out_rows = lax.ppermute(sum_out, EVERY, [(b, a) for a, b in order])

    def end(vectors, values, arrived):
        normed, inverse = norm_parts(values[0].astype(f32))
        return (values[1] + norm_lower(normed, inverse, vectors[0], arrived),)

    def placed(value):
        return lax.dynamic_update_slice(jnp.zeros((value.shape[0], D), f32), value, (0, me * cols))

    branch_rows = placed(sums_branch[:2])
    vector_d = jnp.concatenate(
        [
            placed(bias_sums[0].reshape(3, cols)),
            sums_in[:1],
            branch_rows[:1],
            sums_mid[:1],
            sums_in[1:2],
            branch_rows[1:],
            sums_mid[1:4],
        ]
    )
    vector_f = jnp.concatenate([sums_ff[:1] / gain_ffn, shift_sums[:1], sums_ff[1:2]]).reshape(3, batches, 1, strip)
    vector_f = lax.dynamic_update_slice(jnp.zeros((3, batches, ranks, strip), f32), vector_f, (0, 0, me, 0))
    vector = jnp.concatenate(
        [
            vector_d.reshape(11, batches * ranks, d_rows).swapaxes(0, 1).reshape(batches * ranks, -1),
            vector_f.reshape(3, batches * ranks, strip).swapaxes(0, 1).reshape(batches * ranks, -1),
        ],
        axis=1,
    )
    vector = sum_small(vector, batches, ranks, [terms[-1][0] for terms in arriving] + qkv_rows)
    out_qkv = jnp.moveaxis(move.ordered(qkv_rows), 0, 2).reshape(d_rows, 3 * D).astype(f32)
    out_out = out_rows.astype(f32)
    out_down = sum_down.astype(f32)
    grad_total = own_rows(
        end, [gain_in], [x_own, grad_resid], arriving, [(f32, True)], after=(out_qkv, out_up), name="end"
    )[0]
    own_d = vector[:cut].reshape(11, d_rows)
    own_f = vector[cut:].reshape(3, strip)
    return (
        result.reshape(1, rows, D),
        grad_total.reshape(1, rows, D),
        out_qkv,
        own_d[:3],
        out_out,
        out_up,
        out_down,
        own_d[3:6],
        own_d[6:],
        own_f[0],
        own_f[1:],
    )


def solution(mesh):
    sizes = dict(mesh.shape)

    def run(*args):
        return local(*args, batches=sizes["batch"], ranks=sizes["seq"])

    return jax.shard_map(
        run,
        mesh=mesh,
        in_specs=(
            P("batch", "seq", None),
            P("batch", "seq", None),
            P(("batch", "seq"), None),
            P(None, ("batch", "seq")),
            P(("batch", "seq"), None),
            P(("batch", "seq"), None),
            P(("batch", "seq"), None),
            P(None, ("batch", "seq")),
            P(None, ("batch", "seq")),
            P(("batch", "seq")),
            P(None, ("batch", "seq")),
            P("batch"),
            P("batch", None),
            P("batch", None),
        ),
        out_specs=(
            P("batch", "seq", None),
            P("batch", "seq", None),
            P(("batch", "seq"), None),
            P(None, ("batch", "seq")),
            P(("batch", "seq"), None),
            P(("batch", "seq"), None),
            P(("batch", "seq"), None),
            P(None, ("batch", "seq")),
            P(None, ("batch", "seq")),
            P(("batch", "seq")),
            P(None, ("batch", "seq")),
        ),
        check_vma=False,
    )
```
